128 devices in a mesh: ctx: 32 (over y, z, core), wsh: 4 (over x).
Axes of the slice: x: 4, y: 4, z: 4, core: 2. Of those that a mesh axis runs over, the one named last changes fastest.
Arguments:
- tokens: bfloat16 [24576, 512], P(('wsh', 'ctx')), may hold values from -6 to 6
- cotangent: bfloat16 [24576, 512], P(('wsh', 'ctx')), may hold values from -6 to 6
- ln_gain: float32 [512], replicated, may hold values from 0.5 to 1.5
- ln_bias: float32 [512], replicated, may hold values from -1.75 to 1.75
- biases: float32 [4608], replicated, may hold values from -1.75 to 1.75
- w_qkv: float32 [512, 1536], P('wsh'), may hold values from -0.25 to 0.25
- w_out: float32 [512, 512], P('wsh'), may hold values from -1.5 to 1.5
- w_in: float32 [512, 2048], P('wsh'), may hold values from -0.25 to 0.25
- w_fin: float32 [2048, 512], P('wsh'), may hold values from -0.125 to 0.125
- mom_qkv: float32 [512, 1536], P('wsh'), may hold values from -1792 to 1792
- mom_out: float32 [512, 512], P('wsh'), may hold values from -48 to 48
- mom_in: float32 [512, 2048], P('wsh'), may hold values from -224 to 224
- mom_fin: float32 [2048, 512], P('wsh'), may hold values from -384 to 384
- vec_mom: float32 [5632], replicated, may hold values from -1792 to 1792
- starts: int32 [4], replicated, may hold values from 1 to 18623, as said below
Outputs:
- block_out: bfloat16 [24576, 512], P(('wsh', 'ctx'))
- grad_tokens: float32 [24576, 512], P(('wsh', 'ctx'))
- new_mom_qkv: float32 [512, 1536], P('wsh')
- new_w_qkv: float32 [512, 1536], P('wsh')
- new_mom_out: float32 [512, 512], P('wsh')
- new_w_out: float32 [512, 512], P('wsh')
- new_mom_in: float32 [512, 2048], P('wsh')
- new_w_in: float32 [512, 2048], P('wsh')
- new_mom_fin: float32 [2048, 512], P('wsh')
- new_w_fin: float32 [2048, 512], P('wsh')
- new_vec_mom: float32 [5632], replicated
- new_vectors: float32 [5632], replicated
The draws below stay inside these ranges and needn't reach their ends.
Inputs may be any that keep to these rules, and one draw needn't show every extreme that they name: Packed row g holds tokens g * 6144 to (g + 1) * 6144 - 1; a sequence starts at its first token and another at starts[g], which lies among the row's first 192 tokens and is not its first token.
All inputs are finite; a program needn't handle non-finite values.
Results may differ from the reference program's by a relative error of at most 0.007.
The reference program's roundings to bfloat16 on the way count: a program that leaves them out, or rounds other values in their place, can miss the bound.
Values may be sent and summed in bfloat16 or wider, within the bound.
A program may use at most 320 MiB of HBM per device.

```python
import math
import jax
import jax.numpy as jnp
from jax import lax

D = 512
HEADS = 8
HD = 64
ROT = 16
FF = 2048
TOK_DEV = 192
NS_ITERS = 5
GROUP = 6144
TOKENS = 24576
VECS = 5632


def draw_starts(key, part):
    key = jax.random.fold_in(key, 11)
    row_groups = TOKENS // GROUP
    offsets = jax.random.randint(key, (row_groups,), 1, TOK_DEV, dtype=jnp.int32)
    return jnp.arange(row_groups, dtype=jnp.int32) * GROUP + offsets


def block_levels(key, extent, shards, least, high):
    def one(dim, parts):
        steps = jax.random.uniform(jax.random.fold_in(jax.random.fold_in(key, 6), dim), (parts,), jnp.float32, least / len(shards), high / len(shards))
        return jnp.repeat(jnp.exp(steps), extent[dim] // parts).reshape((-1,) + (1,) * (len(extent) - dim - 1))

    gain = one(*shards[0])
    for cut in shards[1:]:
        gain = gain * one(*cut)
    return gain


def noise(rng, dims, width, reach, pieces=(), kind=jnp.bfloat16):
    entries = jax.random.normal(rng, dims, jnp.float32) * width
    if len(pieces) > 0:
        entries = block_levels(rng, dims, pieces, -0.22, 0.18) * entries
    return jnp.clip(entries, min=-reach, max=reach).astype(kind)


def setup_inputs(seed: int = 0) -> dict:
    streams_of = jax.random.split(jax.random.key(seed), 16)
    tokens = noise(streams_of[0], (TOKENS, D), 1.0, 6.0, ((0, 128),))
    cotangent = noise(streams_of[1], (TOKENS, D), 1.0, 6.0, ((0, 128),))
    ln_gain = jnp.clip(1.0 + 0.1 * jax.random.normal(streams_of[2], (D,), jnp.float32), 0.5, 1.5)
    ln_bias = noise(streams_of[3], (D,), 0.3, 1.75, (), jnp.float32)
    biases = noise(streams_of[4], (5 * D + FF,), 0.3, 1.75, (), jnp.float32)
    w_qkv = noise(streams_of[5], (D, 3 * D), D ** -0.5, 0.25, ((0, 4),), jnp.float32)
    w_out = noise(streams_of[6], (D, D), 16 ** -0.5, 1.5, ((0, 4),), jnp.float32)
    w_in = noise(streams_of[7], (D, FF), D ** -0.5, 0.25, ((0, 4),), jnp.float32)
    w_fin = noise(streams_of[8], (FF, D), FF ** -0.5, 0.125, ((0, 4),), jnp.float32)
    mom_qkv = noise(streams_of[9], (D, 3 * D), (2.0 * TOKENS ** 0.5), 1792.0, ((0, 4),), jnp.float32)
    mom_out = noise(streams_of[10], (D, D), (0.05 * TOKENS ** 0.5), 48.0, ((0, 4),), jnp.float32)
    mom_in = noise(streams_of[11], (D, FF), (0.25 * TOKENS ** 0.5), 224.0, ((0, 4),), jnp.float32)
    mom_fin = noise(streams_of[12], (FF, D), (0.4 * TOKENS ** 0.5), 384.0, ((0, 4),), jnp.float32)
    vec_mom = noise(streams_of[13], (VECS,), (2.0 * TOKENS ** 0.5), 1792.0, (), jnp.float32)
    starts = draw_starts(jax.random.fold_in(streams_of[15], 71), 0)
    return {"tokens": tokens, "cotangent": cotangent, "ln_gain": ln_gain, "ln_bias": ln_bias, "biases": biases, "w_qkv": w_qkv, "w_out": w_out, "w_in": w_in, "w_fin": w_fin, "mom_qkv": mom_qkv, "mom_out": mom_out, "mom_in": mom_in, "mom_fin": mom_fin, "vec_mom": vec_mom, "starts": starts}


@jax.custom_vjp
def low(v):
    return lax.optimization_barrier(v.astype(jnp.bfloat16)).astype(jnp.float32)

@jax.custom_vjp
def low_back(v):
    return v

def low_keep(v):
    return (low(v), None)

def low_pass(kept, grad):
    return (grad,)

def back_keep(v):
    return (v, None)

def back_low(kept, grad):
    return (low(grad),)
low.defvjp(low_keep, low_pass)
low_back.defvjp(back_keep, back_low)
highest = lax.Precision.HIGHEST
first_coef = 3.4445
second_coef = -4.775
third_coef = 2.0315
muon_momentum = 0.95
muon_rate = 0.6
weight_decay = 0.01
vector_momentum = 0.9
vector_rate = 0.0005

def matmul(left, right):
    return jnp.dot(left, right, precision=highest, preferred_element_type=jnp.float32)

def rotary_tables(positions):
    half_dim = ROT // 2
    frequency = 10000.0 ** (-2.0 * jnp.arange(half_dim, dtype=jnp.float32) / ROT)
    angles = positions.astype(jnp.float32)[:, None] * frequency[None, :]
    return (jnp.cos(angles), jnp.sin(angles))

def rotate(matrix, cosine_table, sine_table):
    row_count = matrix.shape[0]
    shaped = matrix.reshape(row_count, HEADS, HD)
    half_dim = ROT // 2
    lower_half = shaped[:, :, :half_dim]
    upper_half = shaped[:, :, half_dim:ROT]
    cosine_part = cosine_table[:, None, :]
    sine_part = sine_table[:, None, :]
    turned = jnp.concatenate([lower_half * cosine_part - upper_half * sine_part, upper_half * cosine_part + lower_half * sine_part, shaped[:, :, ROT:]], axis=2)
    return turned.reshape(row_count, HEADS * HD)

def orthogonalize(update):
    row_count, col_count = update.shape
    matrix = update.T if row_count > col_count else update
    matrix = matrix / (jnp.sqrt(jnp.sum(matrix * matrix)) + 1e-07)
    for sweep_index in range(NS_ITERS):
        gram_matrix = jnp.dot(matrix, matrix.T, precision=highest, preferred_element_type=jnp.float32)
        poly_term = second_coef * gram_matrix + third_coef * jnp.dot(gram_matrix, gram_matrix, precision=highest, preferred_element_type=jnp.float32)
        matrix = first_coef * matrix + jnp.dot(poly_term, matrix, precision=highest, preferred_element_type=jnp.float32)
    if row_count > col_count:
        matrix = matrix.T
    return matrix * (0.2 * math.sqrt(max(row_count, col_count)))

def group_forward(x_rows, gain_vec, shift_vec, bias_vec, mat_qkv, mat_out, mat_in, mat_fin, boundary):
    centered = x_rows - lax.optimization_barrier(jnp.mean(x_rows, axis=1, keepdims=True))
    normed = centered * lax.rsqrt(lax.optimization_barrier(jnp.mean(centered * centered, axis=1, keepdims=True)) + 1e-05)
    hidden = low(normed * gain_vec + shift_vec)
    qkv_pre = low_back(matmul(hidden, low(mat_qkv)) + bias_vec[:3 * D])
    places = jnp.arange(GROUP, dtype=jnp.int32)
    second_doc = places >= boundary
    seq_pos = places - jnp.where(second_doc, boundary, 0)
    cosine_table, sine_table = rotary_tables(seq_pos)
    queries = low(rotate(qkv_pre[:, :D], cosine_table, sine_table))
    key_heads = low(rotate(qkv_pre[:, D:2 * D], cosine_table, sine_table)).reshape(GROUP, HEADS, HD)
    value_heads = low(qkv_pre[:, 2 * D:]).reshape(GROUP, HEADS, HD)
    block_rows = min(512, GROUP)

    def attend_block(first_row):
        block_queries = lax.dynamic_slice_in_dim(queries, first_row, block_rows, 0).reshape(block_rows, HEADS, HD)
        block_places = first_row + jnp.arange(block_rows, dtype=jnp.int32)
        block_second = block_places >= boundary
        raw_scores = jnp.einsum('qhd,khd->hqk', block_queries, key_heads, precision=highest, preferred_element_type=jnp.float32)
        scores = low_back(raw_scores * HD ** (-0.5))
        allowed = (places[None, :] <= block_places[:, None]) & (second_doc[None, :] == block_second[:, None])
        scores = jnp.where(allowed[None], scores, -1e+30)
        row_max = lax.optimization_barrier(jnp.max(scores, axis=2, keepdims=True))
        exponent_terms = jnp.exp(scores - row_max)
        attn_probs = low(exponent_terms / lax.optimization_barrier(jnp.sum(exponent_terms, axis=2, keepdims=True)))
        block_context = jnp.einsum('hqk,khd->qhd', attn_probs, value_heads, precision=highest, preferred_element_type=jnp.float32)
        return block_context.reshape(block_rows, D)
    block_firsts = jnp.arange(GROUP // block_rows, dtype=jnp.int32) * block_rows
    context = lax.map(jax.checkpoint(attend_block), block_firsts).reshape(GROUP, D)
    context = low_back(low(context))
    attn_out = matmul(context, low(mat_out)) + bias_vec[3 * D:4 * D]
    pre_act = low_back(matmul(hidden, low(mat_in)) + bias_vec[4 * D:4 * D + FF])
    activation = low(jax.nn.gelu(pre_act, approximate=True))
    mlp_out = matmul(activation, low(mat_fin)) + bias_vec[4 * D + FF:]
    return x_rows + attn_out + mlp_out

def reference(tokens, cotangent, ln_gain, ln_bias, biases, w_qkv, w_out, w_in, w_fin, mom_qkv, mom_out, mom_in, mom_fin, vec_mom, starts):
    row_groups = TOKENS // GROUP
    params = (ln_gain, ln_bias, biases, w_qkv, w_out, w_in, w_fin)
    token_groups = tokens.astype(jnp.float32).reshape(row_groups, GROUP, D)
    cot_groups = cotangent.astype(jnp.float32).reshape(row_groups, GROUP, D)
    boundaries = starts - jnp.arange(row_groups, dtype=jnp.int32) * GROUP

    def one_group(totals, inputs):
        x_rows, cot_rows, boundary = inputs

        def forward(x_in, params_in):
            gain_vec, shift_vec, bias_vec, mat_qkv, mat_out, mat_in, mat_fin = params_in
            return group_forward(x_in, gain_vec, shift_vec, bias_vec, mat_qkv, mat_out, mat_in, mat_fin, boundary)
        group_out, pullback = jax.vjp(forward, x_rows, params)
        grad_x, grad_params = pullback(cot_rows)
        totals = jax.tree.map(lambda former, latter: former + latter, totals, grad_params)
        return (totals, (group_out.astype(jnp.bfloat16), grad_x))
    zero_params = jax.tree.map(jnp.zeros_like, params)
    totals, (outs_low, grads_x) = lax.scan(one_group, zero_params, (token_groups, cot_groups, boundaries))
    grad_gain, grad_shift, grad_bias, grad_qkv, grad_out, grad_in, grad_fin = totals
    results = []
    for weight, moment, gradient in ((w_qkv, mom_qkv, grad_qkv), (w_out, mom_out, grad_out), (w_in, mom_in, grad_in), (w_fin, mom_fin, grad_fin)):
        new_moment = muon_momentum * moment + gradient
        advance = gradient + muon_momentum * new_moment
        new_weight = weight * (1.0 - muon_rate * weight_decay) - muon_rate * orthogonalize(advance)
        results.append(new_moment)
        results.append(new_weight)
    vec_grad = jnp.concatenate([grad_gain, grad_shift, grad_bias])
    vec_moment = vector_momentum * vec_mom + vec_grad
    vec_new = jnp.concatenate([ln_gain, ln_bias, biases]) - vector_rate * vec_moment
    return (outs_low.reshape(TOKENS, D), grads_x.reshape(TOKENS, D), results[0], results[1], results[2], results[3], results[4], results[5], results[6], results[7], vec_moment, vec_new)
```

```python
import functools
import math

import jax
import jax.numpy as jnp
from jax import lax
from jax.experimental import pallas as pl
from jax.experimental.pallas import tpu as pltpu
from jax.sharding import PartitionSpec as P

f32 = jnp.float32
bf16 = jnp.bfloat16
MESH = pl.DeviceIdType.MESH
HEADS = 8
HD = 64
ROT = 16
D = 512
TOK = 192
GROUP = 6144
QB = 256
NQB = 6
UU = 8
NS_ITERS = 5
C1, C2, C3 = 3.4445, -4.775, 2.0315
MU, LR, WD = 0.95, 0.6, 0.01
VMU, VLR = 0.9, 0.0005
R_QKV, R_OUT, R_IN, R_FIN = 48, 16, 64, 64

VM = pl.BlockSpec(memory_space=pltpu.VMEM)
SM = pl.BlockSpec(memory_space=pltpu.SMEM)
ANY = pl.BlockSpec(memory_space=pl.ANY)
DMA = pltpu.SemaphoreType.DMA


def dot(a, b):
    return jnp.dot(a, b, preferred_element_type=f32)


def dot_nt(a, b):
    return lax.dot_general(a, b, (((1,), (1,)), ((), ())), preferred_element_type=f32)


def dot_tn(a, b):
    return lax.dot_general(a, b, (((0,), (0,)), ((), ())), preferred_element_type=f32)


def coords():
    c = lax.axis_index("ctx")
    return c // 8, (c // 2) % 4, c % 2, lax.axis_index("wsh")


def at(y, z, s, x):
    return {"ctx": (y * 4 + z) * 2 + s, "wsh": x}


def call(kernel, name, args, in_specs, outs, out_specs, scratch=(), cid=None):
    params = dict(vmem_limit_bytes=58 * 2**20)
    if cid is not None:
        params.update(collective_id=cid, has_side_effects=True)
    return pl.pallas_call(
        kernel,
        out_shape=tuple(jax.ShapeDtypeStruct(s, t) for s, t in outs),
        in_specs=list(in_specs),
        out_specs=tuple(out_specs),
        scratch_shapes=list(scratch),
        compiler_params=pltpu.CompilerParams(**params),
        name=name,
    )(*args)


def meet(partners):
    sem = pltpu.get_barrier_semaphore()
    for p in partners:
        pl.semaphore_signal(sem, inc=1, device_id=p, device_id_type=MESH)
    pl.semaphore_wait(sem, len(partners))


def meet_slab():
    c = lax.axis_index("ctx")
    sem = pltpu.get_barrier_semaphore()

    def tell(d, _):
        pl.semaphore_signal(
            sem, inc=1, device_id={"ctx": lax.rem(c + d, 32)}, device_id_type=MESH
        )
        return 0

    lax.fori_loop(1, 32, tell, 0)
    pl.semaphore_wait(sem, 31)


def lines(y, z, s, x, with_x=True):
    out = [at((y + d) % 4, z, s, x) for d in (1, 2, 3)]
    out += [at(y, (z + d) % 4, s, x) for d in (1, 2, 3)]
    out += [at(y, z, 1 - s, x)]
    if with_x:
        out += [at(y, z, s, (x + d) % 4) for d in (1, 2, 3)]
    return out


def send(src, dst, ss, rs, dev):
    cp = pltpu.make_async_remote_copy(
        src_ref=src, dst_ref=dst, send_sem=ss, recv_sem=rs, device_id=dev, device_id_type=MESH
    )
    cp.start()
    return cp


ALL = slice(None)


def slab_gather(items, ss, rs):
    y, z, s, x = coords()
    first = []
    for i, (get, y_first) in enumerate(items):
        for d in (1, 2, 3):
            to = at((y + d) % 4, z, s, x) if y_first else at(y, (z + d) % 4, s, x)
            piece = get(y, z, s)
            first.append(send(piece, piece, ss.at[i, d - 1], rs.at[i, d - 1], to))
    for cp in first:
        cp.wait()
    second, across = {}, []
    for i, (get, y_first) in enumerate(items):
        piece = get(ALL, z, s) if y_first else get(y, ALL, s)
        for d in (1, 2, 3):
            to = at(y, (z + d) % 4, s, x) if y_first else at((y + d) % 4, z, s, x)
            second[i, d] = send(piece, piece, ss.at[i, d + 2], rs.at[i, d + 2], to)
        across.append(send(piece, piece, ss.at[i, 6], rs.at[i, 6], at(y, z, 1 - s, x)))
    for d in (1, 2, 3):
        for i, (get, y_first) in enumerate(items):
            second[i, d].wait_recv()
            piece = get(ALL, (z - d) % 4, s) if y_first else get((y - d) % 4, ALL, s)
            across.append(
                send(piece, piece, ss.at[i, 6 + d], rs.at[i, 6 + d], at(y, z, 1 - s, x))
            )
    for cp in second.values():
        cp.wait_send()
    for cp in across:
        cp.wait()


def weights_kernel(wc_ref, wf_ref, wc, wf, lsem, xs, xr, ss, rs):
    y, z, s, x = coords()
    mine_c = wc.at[y, z, s, pl.ds(x * 128, 128)]
    mine_f = wf.at[x, y, z, s]
    l0 = pltpu.make_async_copy(wc_ref, mine_c, lsem.at[0])
    l1 = pltpu.make_async_copy(wf_ref, mine_f, lsem.at[1])
    l0.start()
    l1.start()
    meet(lines(y, z, s, x))
    cps = []
    for d in (1, 2, 3):
        to = at(y, z, s, (x + d) % 4)
        cps.append(send(wc_ref, mine_c, xs.at[0, d - 1], xr.at[0, d - 1], to))
        cps.append(send(wf_ref, mine_f, xs.at[1, d - 1], xr.at[1, d - 1], to))
    l0.wait()
    l1.wait()
    for cp in cps:
        cp.wait()
    slab_gather(
        [
            (lambda a, b, e: wc.at[a, b, e, pl.ds(0, 384)], True),
            (lambda a, b, e: wc.at[a, b, e, pl.ds(384, 128)], False),
            (lambda a, b, e: wf.at[:, a, b, e], False),
        ],
        ss,
        rs,
    )


def gather_weights(wc_own, wf_own):
    return call(
        weights_kernel,
        "gather_weights",
        (wc_own, wf_own),
        [ANY, ANY],
        [((4, 4, 2, 512, 128), bf16), ((4, 4, 4, 2, 16, 512), bf16)],
        [ANY, ANY],
        [DMA((2,)), DMA((2, 3)), DMA((2, 3)), DMA((3, 10)), DMA((3, 10))],
        cid=1,
    )


def norm_parts(x_ref, gain, shift):
    xf = x_ref[...].astype(f32)
    centered = xf - jnp.mean(xf, axis=1, keepdims=True)
    inv = lax.rsqrt(jnp.mean(centered * centered, axis=1, keepdims=True) + 1e-05)
    normed = centered * inv
    hidden = (normed * gain + shift).astype(bf16)
    return xf, inv, normed, hidden


def turn(v, co, s1, s2):
    return v * co + pltpu.roll(v, 120, 1) * s1 + pltpu.roll(v, 8, 1) * s2


def wide(wc_ref, first, count):
    return jnp.concatenate([wc_ref[first + i] for i in range(count)], axis=1)


def front_kernel(
    x_ref, dy_ref, gain_ref, shift_ref, bias_ref, co_ref, s1_ref, s2_ref, wc_ref, wf_ref,
    kv_ref, qd_ref, gm_ref, res_ref, dh_ref, bin_ref,
):
    xf, inv, normed, hidden = norm_parts(x_ref, gain_ref[...], shift_ref[...])
    dy = dy_ref[...]
    co, s1, s2 = co_ref[...], s1_ref[...], s2_ref[...]
    left = lax.broadcasted_iota(jnp.int32, (TOK, 128), 1) < 64
    dctx = dot_nt(dy, wide(wc_ref, 12, 4))
    for pair in range(4):
        blocks = []
        for third in range(3):
            b = third * 4 + pair
            blocks.append(dot(hidden, wc_ref[b]) + bias_ref[:, b * 128 : b * 128 + 128])
        q = turn(blocks[0], co, s1, s2).astype(bf16).astype(f32) * 0.125
        k = turn(blocks[1], co, s1, s2)
        v = blocks[2]
        g = dctx[:, pair * 128 : pair * 128 + 128]
        h = 2 * pair
        kv_ref[h] = jnp.where(left, k, pltpu.roll(v, 64, 1)).astype(bf16)
        kv_ref[h + 1] = jnp.where(left, pltpu.roll(k, 64, 1), v).astype(bf16)
        qd_ref[h] = jnp.where(left, q, pltpu.roll(g, 64, 1)).astype(bf16)
        qd_ref[h + 1] = jnp.where(left, pltpu.roll(q, 64, 1), g).astype(bf16)
    root = math.sqrt(2.0 / math.pi)
    mlp = jnp.zeros((TOK, D), f32)
    dh = jnp.zeros((TOK, D), f32)
    for i in range(4):
        w_in = wide(wc_ref, 16 + 4 * i, 4)
        w_fin = wf_ref[pl.ds(512 * i, 512), :]
        pre = dot(hidden, w_in) + bias_ref[:, 2048 + 512 * i : 2560 + 512 * i]
        sq = pre * pre
        th = jnp.tanh(root * (pre + 0.044715 * (pre * sq)))
        act = (0.5 * pre * (1.0 + th)).astype(bf16)
        slope = 0.5 * (1.0 + th) + (0.5 * root) * pre * (1.0 - th * th) * (
            1.0 + (3.0 * 0.044715) * sq
        )
        dpre = (dot_nt(dy, w_fin) * slope).astype(bf16)
        mlp = mlp + dot(act, w_fin)
        dh = dh + dot_nt(dpre, w_in)
        bin_ref[:, 512 * i : 512 * i + 512] = jnp.sum(dpre.astype(f32), axis=0, keepdims=True)
        gm_ref[8 * i : 8 * i + 8, 0:64, :] = dot_tn(dpre, hidden).astype(bf16).reshape(8, 64, 512)
        gm_ref[:, 64 + 16 * i : 80 + 16 * i, :] = (
            dot_tn(act, dy).astype(bf16).reshape(32, 16, 512)
        )
    res_ref[...] = xf + mlp + bias_ref[:, 4096:4608] + bias_ref[:, 1536:2048]
    dh_ref[...] = dh


def front(x, dy, gain, shift, biases, co, s1, s2, wc, wf):
    return call(
        front_kernel,
        "front",
        (x, dy, gain, shift, biases, co, s1, s2, wc, wf),
        [VM] * 10,
        [
            ((HEADS, TOK, 128), bf16),
            ((HEADS, TOK, 128), bf16),
            ((32, 128, 512), bf16),
            ((TOK, D), f32),
            ((TOK, D), f32),
            ((1, 2048), f32),
        ],
        [VM] * 6,
    )


def query_home(piece):
    block = piece // 4
    part = block % 8
    low = part < 4
    return jnp.where(low, part, 7 - part), 2 * (block // 8) + jnp.where(low, 0, 1), piece % 4


def query_block(t, j):
    return 8 * (t // 2) + jnp.where(t % 2 == 0, j, 7 - j)


def scatter_kernel(kvs, qds, kv, qd, lsem, ks, kr, qs, qr, cs, cr):
    y, z, s, x = coords()
    c = lax.axis_index("ctx")
    p = c // 2
    own = pltpu.make_async_copy(kvs.at[p // 2], kv.at[p, s], lsem)
    own.start()
    meet_slab()

    def kv_copy(d):
        to = lax.rem(p + d, 16)
        return pltpu.make_async_remote_copy(
            src_ref=kvs.at[to // 2], dst_ref=kv.at[p, s], send_sem=ks.at[d], recv_sem=kr.at[d],
            device_id={"ctx": to * 2 + s}, device_id_type=MESH,
        )

    def across(d):
        block = kv.at[lax.rem(p + 16 - d, 16), s]
        return pltpu.make_async_remote_copy(
            src_ref=block, dst_ref=block, send_sem=cs.at[d], recv_sem=cr.at[d],
            device_id={"ctx": p * 2 + 1 - s}, device_id_type=MESH,
        )

    def each_query(k, what):
        h, i = k // 3, k % 3
        j, t, quarter = query_home(3 * c + i)
        to = 4 * h + j
        src = qds.at[h, pl.ds(64 * i, 64)]
        dst = qd.at[t, pl.ds(64 * quarter, 64)]

        @pl.when(to == c)
        def _():
            if what == "start":
                pltpu.make_async_copy(src, dst, qr).start()

        @pl.when(to != c)
        def _():
            cp = pltpu.make_async_remote_copy(
                src_ref=src, dst_ref=dst, send_sem=qs.at[k], recv_sem=qr,
                device_id={"ctx": to}, device_id_type=MESH,
            )
            if what == "start":
                cp.start()
            else:
                cp.wait_send()

    def loop(lo, hi, f):
        def step(i, _):
            f(i)
            return 0

        lax.fori_loop(lo, hi, step, 0)

    loop(1, 16, lambda d: kv_copy(d).start())
    loop(0, 24, lambda k: each_query(k, "start"))
    own.wait()
    across(0).start()

    def arrived(d):
        kv_copy(d).wait_recv()
        across(d).start()

    loop(1, 16, arrived)
    loop(1, 16, lambda d: kv_copy(d).wait_send())
    loop(0, 24, lambda k: each_query(k, "wait"))
    pltpu.make_async_copy(qd, qd, qr).wait()
    loop(0, 16, lambda d: across(d).wait())


def scatter(kvs, qds):
    return call(
        scatter_kernel,
        "to_heads",
        (kvs, qds),
        [ANY, ANY],
        [((16, 2, TOK, 128), bf16), ((NQB, QB, 128), bf16)],
        [ANY, ANY],
        [DMA, DMA((16,)), DMA((16,)), DMA((24,)), DMA, DMA((16,)), DMA((16,))],
        cid=2,
    )


def attention_kernel(bnd_ref, kv_ref, qd_ref, out_ref, dkv_ref, kvt, acc, s_sc, p_sc):
    n = kv_ref.shape[0]
    j = lax.axis_index("ctx") % 4
    bnd = bnd_ref[0]

    def prepare(i, _):
        r = pl.multiple_of(i * QB, QB)
        kvt[:, pl.ds(r, QB)] = kv_ref[pl.ds(r, QB), :].T
        acc[pl.ds(r, QB), :] = jnp.zeros((QB, 128), f32)
        return 0

    lax.fori_loop(0, n // QB, prepare, 0)
    lane = lax.broadcasted_iota(jnp.int32, (QB, 128), 1)

    def block(t, _):
        qb = query_block(t, j)
        qd = qd_ref[t]
        w1 = jnp.where(lane < 64, qd, jnp.zeros_like(qd))
        w2 = jnp.where(lane < 64, jnp.zeros_like(qd), qd)
        q_t = w1.T
        d_t = w2.T

        def scores(kt, masked, carry, tiles, first=False):
            m8, l8, r8 = carry
            ss, ds = [], []
            for u in range(tiles):
                r = pl.multiple_of((kt + u) * QB, QB)
                rows = kv_ref[pl.ds(r, QB), :]
                s = dot(rows, q_t)
                if masked and not (first and u > 0):
                    kp = r + lax.broadcasted_iota(jnp.int32, (QB, QB), 0)
                    qp = qb * QB + lax.broadcasted_iota(jnp.int32, (QB, QB), 1)
                    s = jnp.where((kp <= qp) & ((kp >= bnd) == (qp >= bnd)), s, -1e30)
                dp = dot(rows, d_t)
                s_sc[pl.ds(r, QB), :] = s
                p_sc[pl.ds(r, QB), :] = dp
                ss.append(s.reshape(QB // 8, 8, QB))
                ds.append(dp.reshape(QB // 8, 8, QB))
            mn = m8
            for s3 in ss:
                mn = jnp.maximum(mn, jnp.max(s3, axis=0))
            al = jnp.exp(m8 - mn)
            l8 = l8 * al
            r8 = r8 * al
            for s3, d3 in zip(ss, ds):
                e = jnp.exp(s3 - mn[None])
                l8 = l8 + jnp.sum(e, axis=0)
                r8 = r8 + jnp.sum(e * d3, axis=0)
            return mn, l8, r8

        zero = jnp.zeros((8, QB), f32)
        base = t // 2 * 8
        pairs = (qb - base) // 2 + 1
        carry = lax.fori_loop(
            0, pairs, lambda g, c: scores(base + 2 * g, True, c, 2),
            (jnp.full((8, QB), -1e30, f32), zero, zero),
        )
        carry = lax.cond(
            base > 0, lambda c: scores(0, True, c, UU, True), lambda c: c, carry
        )
        carry = lax.fori_loop(
            1, base // UU, lambda g, c: scores(g * UU, False, c, UU), carry
        )
        m8, l8, r8 = carry
        m = jnp.max(m8, axis=0, keepdims=True)
        w = jnp.exp(m8 - m)
        l = jnp.sum(l8 * w, axis=0, keepdims=True)
        lse = m + jnp.log(l)
        rd = jnp.sum(r8 * w, axis=0, keepdims=True) / l

        def grads(kt, carry, tiles):
            c_t, g_t = carry
            for u in range(tiles):
                r = pl.multiple_of((kt + u) * QB, QB)
                p = jnp.exp(s_sc[pl.ds(r, QB), :] - lse)
                pb = p.astype(bf16)
                ds = (p * (p_sc[pl.ds(r, QB), :] - rd)).astype(bf16)
                c_t = c_t + dot(kvt[64:128, pl.ds(r, QB)], pb)
                g_t = g_t + dot(kvt[0:64, pl.ds(r, QB)], ds)
                acc[pl.ds(r, QB), :] += dot(ds, w1) + dot(pb, w2)
            return c_t, g_t

        z = jnp.zeros((64, QB), f32)
        c = lax.fori_loop(0, base // UU, lambda g, c: grads(g * UU, c, UU), (z, z))
        c_t, g_t = lax.fori_loop(0, pairs, lambda g, c: grads(base + 2 * g, c, 2), c)
        out_ref[t] = jnp.concatenate([g_t * 0.125, c_t], axis=0).T.astype(bf16)
        return 0

    lax.fori_loop(0, NQB, block, 0)

    def finish(i, _):
        r = pl.multiple_of(i * QB, QB)
        dkv_ref[pl.ds(r, QB), :] = acc[pl.ds(r, QB), :].astype(bf16)
        return 0

    lax.fori_loop(0, n // QB, finish, 0)


def attention(bnd, kv, qd):
    return call(
        attention_kernel,
        "attention",
        (bnd, kv, qd),
        [SM, VM, VM],
        [((NQB, QB, 128), bf16), ((GROUP, 128), bf16)],
        [VM, VM],
        [
            pltpu.VMEM((128, GROUP), bf16),
            pltpu.VMEM((GROUP, 128), f32),
            pltpu.VMEM((GROUP, QB), f32),
            pltpu.VMEM((GROUP, QB), f32),
        ],
    )


def return_kernel(dkv, cq_in, cq, kr, other, both, ws, wr, ss, sr, qs, qr):
    y, z, s, x = coords()
    c = lax.axis_index("ctx")
    p = c // 2
    h = c // 4
    meet_slab()

    def loop(lo, hi, f):
        def step(i, _):
            f(i)
            return 0

        lax.fori_loop(lo, hi, step, 0)

    swap = send(dkv.at[:, 1 - s], other, ws, wr, {"ctx": p * 2 + 1 - s})

    def each_query(k, what):
        t, quarter = k // 4, k % 4
        piece = 4 * query_block(t, c % 4) + quarter
        to, i = piece // 3, piece % 3
        src = cq_in.at[t, pl.ds(64 * quarter, 64)]
        dst = cq.at[h, pl.ds(64 * i, 64)]

        @pl.when(to == c)
        def _():
            if what == "start":
                pltpu.make_async_copy(src, dst, qr).start()

        @pl.when(to != c)
        def _():
            cp = pltpu.make_async_remote_copy(
                src_ref=src, dst_ref=dst, send_sem=qs.at[k], recv_sem=qr,
                device_id={"ctx": to}, device_id_type=MESH,
            )
            if what == "start":
                cp.start()
            else:
                cp.wait_send()

    loop(0, 24, lambda k: each_query(k, "start"))
    swap.wait()

    def add(d):
        to = lax.rem(p + d, 16)
        both[d] = (dkv[to, s].astype(f32) + other[to].astype(f32)).astype(bf16)

    def block_copy(d):
        return pltpu.make_async_remote_copy(
            src_ref=both.at[d], dst_ref=kr.at[h, p % 2], send_sem=ss.at[d], recv_sem=sr,
            device_id={"ctx": lax.rem(p + d, 16) * 2 + s}, device_id_type=MESH,
        )

    def push(d):
        add(d)
        block_copy(d).start()

    loop(1, 16, push)
    add(0)
    pltpu.make_async_copy(both.at[0], kr.at[h, p % 2], sr).start()
    loop(1, 16, lambda d: block_copy(d).wait_send())
    loop(0, 24, lambda k: each_query(k, "wait"))
    pltpu.make_async_copy(cq, cq, qr).wait()
    pltpu.make_async_copy(kr, kr, sr).wait()


def give_back(dkv, cq_in):
    return call(
        return_kernel,
        "to_tokens",
        (dkv, cq_in),
        [VM, VM],
        [((HEADS, TOK, 128), bf16), ((HEADS, 2, TOK, 128), bf16)],
        [VM, VM],
        [
            pltpu.VMEM((16, TOK, 128), bf16),
            pltpu.VMEM((16, TOK, 128), bf16),
            DMA, DMA, DMA((16,)), DMA, DMA((24,)), DMA,
        ],
        cid=3,
    )


def split(v):
    hi = v.astype(bf16)
    return hi, (v - hi.astype(f32)).astype(bf16)


def back_kernel(
    cq_ref, kr_ref, x_ref, dy_ref, gain_ref, shift_ref, co_ref, s1_ref, s2_ref, wc_ref,
    res_ref, dh_ref, bin_ref, out_ref, gt_ref, ga_ref, vec_ref, dqkv,
):
    xf, inv, normed, hidden = norm_parts(x_ref, gain_ref[...], shift_ref[...])
    dy = dy_ref[...]
    co, s1, s2 = co_ref[...], -s1_ref[...], -s2_ref[...]
    left = lax.broadcasted_iota(jnp.int32, (TOK, 128), 1) < 64
    ctx = []
    for pair in range(4):
        a = cq_ref[2 * pair].astype(f32)
        b = cq_ref[2 * pair + 1].astype(f32)
        e = kr_ref[2 * pair, 0].astype(f32) + kr_ref[2 * pair, 1].astype(f32)
        f = kr_ref[2 * pair + 1, 0].astype(f32) + kr_ref[2 * pair + 1, 1].astype(f32)
        dq = jnp.where(left, a, pltpu.roll(b, 64, 1))
        dk = jnp.where(left, e, pltpu.roll(f, 64, 1))
        lanes = slice(128 * pair, 128 * pair + 128)
        dqkv[:, 128 * pair : 128 * pair + 128] = turn(dq, co, s1, s2).astype(bf16)
        dqkv[:, 512 + 128 * pair : 640 + 128 * pair] = turn(dk, co, s1, s2).astype(bf16)
        dqkv[:, 1024 + 128 * pair : 1152 + 128 * pair] = jnp.where(
            left, pltpu.roll(e, 64, 1), f
        ).astype(bf16)
        ctx.append(jnp.where(left, pltpu.roll(a, 64, 1), b).astype(bf16))
    ctx = jnp.concatenate(ctx, axis=1)
    out_ref[...] = (res_ref[...] + dot(ctx, wide(wc_ref, 12, 4))).astype(bf16)
    hi, lo = split(dot_tn(dy, ctx))
    ga_ref[:, 48:64, :] = hi.reshape(32, 16, 512)
    ga_ref[:, 64:80, :] = lo.reshape(32, 16, 512)
    dh = dh_ref[...]
    for third in range(3):
        part = dqkv[:, 512 * third : 512 * third + 512]
        dh = dh + dot_nt(part, wide(wc_ref, 4 * third, 4))
        vec_ref[2 + third : 3 + third, :] = jnp.sum(part.astype(f32), axis=0, keepdims=True)
    for i in range(4):
        part = dqkv[:, 384 * i : 384 * i + 384]
        ga_ref[8 * i : 8 * i + 8, 0:48, :] = dot_tn(part, hidden).astype(bf16).reshape(8, 48, 512)
    scaled = dh * gain_ref[...]
    dyf = dy.astype(f32)
    gt_ref[...] = dyf + inv * (
        scaled
        - jnp.mean(scaled, axis=1, keepdims=True)
        - normed * jnp.mean(scaled * normed, axis=1, keepdims=True)
    )
    dsum = jnp.sum(dyf, axis=0, keepdims=True)
    vec_ref[0:1, :] = jnp.sum(dh * normed, axis=0, keepdims=True)
    vec_ref[1:2, :] = jnp.sum(dh, axis=0, keepdims=True)
    vec_ref[5:6, :] = dsum
    for i in range(4):
        vec_ref[6 + i : 7 + i, :] = bin_ref[:, 512 * i : 512 * i + 512]
    vec_ref[10:11, :] = dsum
    vec_ref[11:16, :] = jnp.zeros((5, 512), f32)


def back(cq, kr, x, dy, gain, shift, co, s1, s2, wc, res, dh, bin_sum):
    return call(
        back_kernel,
        "back",
        (cq, kr, x, dy, gain, shift, co, s1, s2, wc, res, dh, bin_sum),
        [VM] * 13,
        [
            ((TOK, D), bf16),
            ((TOK, D), f32),
            ((32, 80, 512), bf16),
            ((16, 512), f32),
        ],
        [VM] * 4,
        [pltpu.VMEM((TOK, 1536), bf16)],
    )


def total(parts):
    v = [p.astype(f32) for p in parts]
    v = functools.reduce(lambda a, b: a + b, v)
    return v[0:48], v[48:64] + v[64:80], v[80:208]


def put(ref, index, v):
    a, o, b = v
    hi, lo = split(o)
    ref[index + (slice(0, 48),)] = a.astype(bf16)
    ref[index + (slice(48, 64),)] = hi
    ref[index + (slice(64, 80),)] = lo
    ref[index + (slice(80, 208),)] = b.astype(bf16)


def reduce_kernel(
    ga_ref, gm_ref, vec_ref, mt_ref, mf_ref,
    ua, gx, vec_out,
    rca, rcm, hbuf, ra, rb, ha, hb, ra2, rb2, gsum, rv0, rvy, rvz, rvx, ts, tr, gs, gr,
    cs, cr, s1, r1, s2, r2, xs, xr, ss, rs,
):
    y, z, s, x = coords()
    me = at(y, z, s, x)
    del me
    meet(lines(y, z, s, x))
    core = at(y, z, 1 - s, x)
    cps = [
        send(ga_ref.at[:, :, 1 - s], rca, cs.at[0], cr.at[0], core),
        send(gm_ref.at[:, :, 1 - s], rcm, cs.at[1], cr.at[1], core),
        send(vec_ref, rv0, cs.at[2], cr.at[2], core),
    ]
    for cp in cps:
        cp.wait()

    def add(i, _):
        a, b = i // 4, i % 4
        both = ga_ref[a, b, s].astype(f32) + rca[a, b].astype(f32)
        hi, lo = split(both[48:64] + both[64:80])
        hbuf[a, b, 0:48] = both[0:48].astype(bf16)
        hbuf[a, b, 48:64] = hi
        hbuf[a, b, 64:80] = lo
        hbuf[a, b, 80:208] = (gm_ref[a, b, s].astype(f32) + rcm[a, b].astype(f32)).astype(bf16)
        return 0

    lax.fori_loop(0, 16, add, 0)
    rvy[y] = vec_ref[...] + rv0[...]
    cps = []
    for d in (1, 2, 3):
        to_y, to_z = at((y + d) % 4, z, s, x), at(y, (z + d) % 4, s, x)
        cps.append(
            send(hbuf.at[(y + d) % 4, :, :, pl.ds(0, 256)], ra.at[d - 1], s1.at[0, d - 1], r1.at[0, d - 1], to_y)
        )
        cps.append(
            send(hbuf.at[:, (z + d) % 4, :, pl.ds(256, 256)], rb.at[d - 1], s1.at[1, d - 1], r1.at[1, d - 1], to_z)
        )
        cps.append(send(rvy.at[y], rvy.at[y], s1.at[2, d - 1], r1.at[2, d - 1], to_y))
    for cp in cps:
        cp.wait()

    def add_lines(i, _):
        put(ha, (i,), total([hbuf[y, i, :, 0:256], ra[0, i], ra[1, i], ra[2, i]]))
        put(hb, (i,), total([hbuf[i, z, :, 256:512], rb[0, i], rb[1, i], rb[2, i]]))
        return 0

    lax.fori_loop(0, 4, add_lines, 0)
    rvz[z] = (rvy[0] + rvy[1]) + (rvy[2] + rvy[3])
    cps = []
    for d in (1, 2, 3):
        to_y, to_z = at((y + d) % 4, z, s, x), at(y, (z + d) % 4, s, x)
        cps.append(send(ha.at[(z + d) % 4], ra2.at[d - 1], s2.at[0, d - 1], r2.at[0, d - 1], to_z))
        cps.append(send(hb.at[(y + d) % 4], rb2.at[d - 1], s2.at[1, d - 1], r2.at[1, d - 1], to_y))
        cps.append(send(rvz.at[z], rvz.at[z], s2.at[2, d - 1], r2.at[2, d - 1], to_z))
    for cp in cps:
        cp.wait()
    for lanes, v in (
        (slice(0, 256), total([ha[z], ra2[0], ra2[1], ra2[2]])),
        (slice(256, 512), total([hb[y], rb2[0], rb2[1], rb2[2]])),
    ):
        gsum[0:48, lanes] = v[0]
        gsum[48:64, lanes] = v[1]
        gsum[64:192, lanes] = v[2]
    rvx[x] = (rvz[0] + rvz[1]) + (rvz[2] + rvz[3])
    both_c = 1.0 + MU
    ts[...] = jnp.zeros_like(ts)
    for k in range(4):
        lanes = slice(128 * k, 128 * k + 128)
        own = gsum[0:128, lanes]
        t = both_c * own + jnp.where(x == k, MU * MU * mt_ref[...], 0.0)
        ts[0, 0:48, lanes] = t[0:48].astype(bf16)
        hi, lo = split(t[48:64])
        ts[1, 0:16, lanes] = hi
        ts[1, 16:32, lanes] = lo
        ts[2, :, lanes] = t[64:128].astype(bf16)
        rows = slice(16 * k, 16 * k + 16)
        fin = gsum[128 + 16 * k : 144 + 16 * k, :]
        ts[3, rows, :] = (both_c * fin + jnp.where(x == k, MU * MU * mf_ref[...], 0.0)).astype(bf16)
        gs[k, 0:128] = own.astype(bf16)
        for b in range(4):
            gs[k, 128 + 16 * b : 144 + 16 * b] = fin[:, 128 * b : 128 * b + 128].astype(bf16)
    cps = []
    for d in (1, 2, 3):
        xt = (x + d) % 4
        to = at(y, z, s, xt)
        cps.append(send(ts.at[xt], tr.at[d - 1], xs.at[0, d - 1], xr.at[0, d - 1], to))
        cps.append(send(gs.at[xt], gr.at[d - 1], xs.at[1, d - 1], xr.at[1, d - 1], to))
        cps.append(send(rvx.at[x], rvx.at[x], xs.at[2, d - 1], xr.at[2, d - 1], to))
    for cp in cps:
        cp.wait()
    vec_out[...] = (rvx[0] + rvx[1]) + (rvx[2] + rvx[3])
    u = ts[x].astype(f32) + tr[0].astype(f32) + tr[1].astype(f32) + tr[2].astype(f32)
    hi, lo = split(u[0:16] + u[16:32])
    ub = u.astype(bf16)
    is_out = x == 1
    ua[y, z, s, 0:16] = jnp.where(is_out, hi, ub[0:16])
    ua[y, z, s, 16:32] = jnp.where(is_out, lo, ub[16:32])
    ua[y, z, s, 32:64] = ub[32:64]
    gx[y, z, s] = (
        gs[x].astype(f32) + gr[0].astype(f32) + gr[1].astype(f32) + gr[2].astype(f32)
    ).astype(bf16)
    slab_gather(
        [
            (lambda a, b, e: ua.at[a, b, e], True),
            (lambda a, b, e: gx.at[a, b, e], False),
        ],
        ss,
        rs,
    )


def reduce_gradients(ga, gm, vec, mt, mf):
    V = pltpu.VMEM
    return call(
        reduce_kernel,
        "reduce_gradients",
        (ga.reshape(4, 4, 2, 80, 512), gm.reshape(4, 4, 2, 128, 512), vec, mt, mf),
        [VM] * 5,
        [((4, 4, 2, 64, 512), bf16), ((4, 4, 2, 192, 128), bf16), ((16, 512), f32)],
        [VM] * 3,
        [
            V((4, 4, 80, 512), bf16),
            V((4, 4, 128, 512), bf16),
            V((4, 4, 208, 512), bf16),
            V((3, 4, 208, 256), bf16),
            V((3, 4, 208, 256), bf16),
            V((4, 208, 256), bf16),
            V((4, 208, 256), bf16),
            V((3, 208, 256), bf16),
            V((3, 208, 256), bf16),
            V((192, 512), f32),
            V((16, 512), f32),
            V((4, 16, 512), f32),
            V((4, 16, 512), f32),
            V((4, 16, 512), f32),
            V((4, 64, 512), bf16),
            V((3, 64, 512), bf16),
            V((4, 192, 128), bf16),
            V((3, 192, 128), bf16),
            DMA((3,)), DMA((3,)),
            DMA((3, 3)), DMA((3, 3)),
            DMA((3, 3)), DMA((3, 3)),
            DMA((3, 3)), DMA((3, 3)),
            DMA((2, 10)), DMA((2, 10)),
        ],
        cid=4,
    )


def dot3(a, b):
    (ah, al), (bh, bl) = a, b
    return dot(ah, bh) + (dot(ah, bl) + dot(al, bh))


def newton_kernel(ua_ref, o_ref, a_ref, ah, al, ph, pl_, th, tl, uh, ul):
    y, z, s, x = coords()
    c = lax.axis_index("ctx")

    def load(hi, lo):
        return hi[...], lo[...]

    def store(hi, lo, v):
        h, l = split(v)
        hi[...] = h
        lo[...] = l

    @pl.when(x == 1)
    def _():
        uh[...] = ua_ref[:, 0:16, :].reshape(512, 512)
        ul[...] = ua_ref[:, 16:32, :].reshape(512, 512)
        h, l = uh[...], ul[...]
        a_ref[...] = dot_tn(h, h) + (dot_tn(h, l) + dot_tn(l, h))

    @pl.when(x != 1)
    def _():
        u = ua_ref[...].reshape(2048, 512)
        a_ref[...] = dot_tn(u, u)

    row = lax.broadcasted_iota(jnp.int32, (512, 512), 0)
    col = lax.broadcasted_iota(jnp.int32, (512, 512), 1)
    eye = row == col
    a = a_ref[...]
    square = jnp.sum(jnp.sum(jnp.where(eye, a, 0.0), axis=0, keepdims=True), axis=1, keepdims=True)
    scale = 1.0 / (jnp.sqrt(square) + 1e-07)
    a_ref[...] = a * (scale * scale)
    mine = ua_ref[c].astype(f32) * scale

    def poly():
        store(ah, al, a_ref[...])
        sq = dot3(load(ah, al), load(ah, al))
        return C2 * a_ref[...] + C3 * sq + jnp.where(eye, C1, 0.0)

    def step(_, mine):
        store(ph, pl_, poly())
        pair = load(ph, pl_)
        store(th, tl, dot3(pair, load(ah, al)))
        a_ref[...] = dot3(pair, load(th, tl))
        return dot3(split(mine), pair)

    mine = lax.fori_loop(0, NS_ITERS - 1, step, mine)
    store(ph, pl_, poly())
    mine = dot3(split(mine), load(ph, pl_))
    side = jnp.where(x == 0, math.sqrt(1536.0), jnp.where(x == 1, math.sqrt(512.0), math.sqrt(2048.0)))
    mine = mine * (0.2 * side)
    o_ref[0:16] = jnp.where(x == 1, mine[0:16] + mine[16:32], mine[0:16]).astype(bf16)
    o_ref[16:64] = mine[16:64].astype(bf16)


def newton(ua):
    V = pltpu.VMEM
    square = [V((512, 512), f32)] + [V((512, 512), bf16)] * 8
    return call(
        newton_kernel, "newton_schulz", (ua,), [VM], [((64, 512), bf16)], [VM], square
    )[0]


def spread_kernel(o_ref, oa, os, rows, xs, xr, ss, rs):
    y, z, s, x = coords()
    meet(lines(y, z, s, x))
    for k in range(4):
        by_lanes = o_ref[:, 128 * k : 128 * k + 128]
        by_rows = jnp.concatenate(
            [o_ref[16 * k : 16 * k + 16, 128 * b : 128 * b + 128] for b in range(4)], axis=0
        )
        os[k] = jnp.where(x == 3, by_rows, by_lanes)
    cps = []
    for d in (1, 2, 3):
        xt = (x + d) % 4
        cps.append(send(os.at[xt], rows.at[x], xs.at[d - 1], xr.at[d - 1], at(y, z, s, xt)))
    rows[x] = os[x]
    for cp in cps:
        cp.wait()
    oa[y, z, s, 0:48] = rows[0, 0:48]
    oa[y, z, s, 48:64] = rows[1, 0:16]
    oa[y, z, s, 64:128] = rows[2]
    oa[y, z, s, 128:192] = rows[3]
    slab_gather(
        [
            (lambda a, b, e: oa.at[a, b, e, pl.ds(0, 96)], True),
            (lambda a, b, e: oa.at[a, b, e, pl.ds(96, 96)], False),
        ],
        ss,
        rs,
    )


def spread(o):
    return call(
        spread_kernel,
        "spread_update",
        (o,),
        [VM],
        [((4, 4, 2, 192, 128), bf16)],
        [VM],
        [
            pltpu.VMEM((4, 64, 128), bf16),
            pltpu.VMEM((4, 64, 128), bf16),
            DMA((3,)), DMA((3,)),
            DMA((2, 10)), DMA((2, 10)),
        ],
        cid=5,
    )[0]


def update_kernel(
    gx, oa, wq, wo, wi, wf, mq, mo, mi, mf, nmq, nwq, nmo, nwo, nmi, nwi, nmf, nwf
):
    for lo, n, w, m, nm, nw in (
        (0, 48, wq, mq, nmq, nwq),
        (48, 16, wo, mo, nmo, nwo),
        (64, 64, wi, mi, nmi, nwi),
    ):
        step = 384 // n
        if n != 48:
            step = 256 // n
        width = step * n
        for g in range(32 // step):
            cols = slice(g * width, g * width + width)
            grad = gx[g * step : g * step + step, lo : lo + n, :].astype(f32).reshape(width, 128).T
            turn_ = oa[g * step : g * step + step, lo : lo + n, :].astype(f32).reshape(width, 128).T
            nm[:, cols] = MU * m[:, cols] + grad
            nw[:, cols] = (1.0 - LR * WD) * w[:, cols] - LR * turn_
    for b in range(4):
        cols = slice(128 * b, 128 * b + 128)
        rows = slice(128 + 16 * b, 144 + 16 * b)
        grad = gx[:, rows, :].astype(f32).reshape(512, 128)
        turn_ = oa[:, rows, :].astype(f32).reshape(512, 128)
        nmf[:, cols] = MU * mf[:, cols] + grad
        nwf[:, cols] = (1.0 - LR * WD) * wf[:, cols] - LR * turn_


def update(gx, oa, weights, moments):
    outs = []
    for w in weights:
        outs += [(w.shape, f32)] * 2
    return call(
        update_kernel,
        "update_weights",
        (gx, oa, *weights, *moments),
        [VM] * 10,
        outs,
        [VM] * 8,
    )


def body(
    tokens, cotangent, ln_gain, ln_bias, biases, w_qkv, w_out, w_in, w_fin,
    mom_qkv, mom_out, mom_in, mom_fin, vec_mom, starts,
):
    x = lax.axis_index("wsh")
    c = lax.axis_index("ctx")
    bnd = lax.dynamic_slice(starts, (x,), (1,)) - x * GROUP
    w_cols = jnp.concatenate([w_qkv, w_out, w_in], axis=1)
    wc_own = lax.dynamic_slice(w_cols, (0, c * 128), (128, 128)).astype(bf16)
    wf_own = lax.dynamic_slice(w_fin, (c * 16, 0), (16, 512)).astype(bf16)
    wc, wf = gather_weights(wc_own, wf_own)
    wc = wc.reshape(32, 512, 128)
    wf = wf.reshape(2048, 512)
    places = c * TOK + jnp.arange(TOK, dtype=jnp.int32)
    pos = (places - jnp.where(places >= bnd[0], bnd[0], 0)).astype(f32)
    lane = jnp.arange(128) % HD
    freq = 10000.0 ** (-2.0 * jnp.arange(ROT // 2, dtype=f32) / ROT)
    freq = jnp.where(lane < ROT, jnp.tile(freq, 16), 0.0)
    angles = pos[:, None] * freq[None, :]
    co = jnp.cos(angles)
    si = jnp.sin(angles)
    s1 = jnp.where(lane < 8, -si, 0.0)
    s2 = jnp.where((lane >= 8) & (lane < 16), si, 0.0)
    gain, shift = ln_gain[None, :], ln_bias[None, :]
    kvs, qds, gm, res, dh, bin_sum = front(
        tokens, cotangent, gain, shift, biases[None, :], co, s1, s2, wc, wf
    )
    kv, qd = scatter(kvs, qds)
    cq_in, dkv = attention(bnd, kv.reshape(GROUP, 128), qd)
    cq, kr = give_back(dkv.reshape(16, 2, TOK, 128), cq_in)
    block_out, grad_tokens, ga, vec = back(
        cq, kr, tokens, cotangent, gain, shift, co, s1, s2, wc, res, dh, bin_sum
    )
    mt = jnp.concatenate(
        [
            lax.dynamic_slice(m, (0, c * n), (128, n)).T
            for m, n in ((mom_qkv, R_QKV), (mom_out, R_OUT), (mom_in, R_IN))
        ],
        axis=0,
    )
    mf = lax.dynamic_slice(mom_fin, (c * 16, 0), (16, 512))
    ua, gx, vec_sum = reduce_gradients(ga, gm, vec, mt, mf)
    oa = spread(newton(ua.reshape(32, 64, 512)))
    new = update(
        gx.reshape(32, 192, 128),
        oa.reshape(32, 192, 128),
        (w_qkv, w_out, w_in, w_fin),
        (mom_qkv, mom_out, mom_in, mom_fin),
    )
    vec_moment = VMU * vec_mom + vec_sum.reshape(-1)[:5632]
    vec_new = jnp.concatenate([ln_gain, ln_bias, biases]) - VLR * vec_moment
    return (block_out, grad_tokens, *new, vec_moment, vec_new)


def solution(mesh):
    tok = P(("wsh", "ctx"), None)
    row = P("wsh", None)
    return jax.shard_map(
        body,
        mesh=mesh,
        in_specs=(tok, tok, P(), P(), P()) + (row,) * 8 + (P(), P()),
        out_specs=(tok, tok) + (row,) * 8 + (P(), P()),
        check_vma=False,
    )
```

```python
import functools
import math

import jax
import jax.numpy as jnp
from jax import lax
from jax.experimental import pallas as pl
from jax.experimental.pallas import tpu as pltpu
from jax.sharding import PartitionSpec as P

f32 = jnp.float32
bf16 = jnp.bfloat16
MESH = pl.DeviceIdType.MESH
HEADS = 8
HD = 64
ROT = 16
D = 512
TOK = 192
GROUP = 6144
QB = 256
NQB = 6
UU = 8
NS_ITERS = 5
C1, C2, C3 = 3.4445, -4.775, 2.0315
MU, LR, WD = 0.95, 0.6, 0.01
VMU, VLR = 0.9, 0.0005
R_QKV, R_OUT, R_IN, R_FIN = 48, 16, 64, 64

VM = pl.BlockSpec(memory_space=pltpu.VMEM)
SM = pl.BlockSpec(memory_space=pltpu.SMEM)
ANY = pl.BlockSpec(memory_space=pl.ANY)
DMA = pltpu.SemaphoreType.DMA


def dot(a, b):
    return jnp.dot(a, b, preferred_element_type=f32)


def dot_nt(a, b):
    return lax.dot_general(a, b, (((1,), (1,)), ((), ())), preferred_element_type=f32)


def dot_tn(a, b):
    return lax.dot_general(a, b, (((0,), (0,)), ((), ())), preferred_element_type=f32)


def coords():
    c = lax.axis_index("ctx")
    return c // 8, (c // 2) % 4, c % 2, lax.axis_index("wsh")


def at(y, z, s, x):
    return {"ctx": (y * 4 + z) * 2 + s, "wsh": x}


def call(kernel, name, args, in_specs, outs, out_specs, scratch=(), cid=None):
    params = dict(vmem_limit_bytes=58 * 2**20)
    if cid is not None:
        params.update(collective_id=cid, has_side_effects=True)
    return pl.pallas_call(
        kernel,
        out_shape=tuple(jax.ShapeDtypeStruct(s, t) for s, t in outs),
        in_specs=list(in_specs),
        out_specs=tuple(out_specs),
        scratch_shapes=list(scratch),
        compiler_params=pltpu.CompilerParams(**params),
        name=name,
    )(*args)


def tell(partners):
    sem = pltpu.get_barrier_semaphore()
    for p in partners:
        pl.semaphore_signal(sem, inc=1, device_id=p, device_id_type=MESH)


def tell_slab():
    c = lax.axis_index("ctx")
    sem = pltpu.get_barrier_semaphore()

    def one(d, _):
        pl.semaphore_signal(
            sem, inc=1, device_id={"ctx": lax.rem(c + d, 32)}, device_id_type=MESH
        )
        return 0

    lax.fori_loop(1, 32, one, 0)


def met(count):
    pl.semaphore_wait(pltpu.get_barrier_semaphore(), count)


def loop(lo, hi, f):
    def step(i, _):
        f(i)
        return 0

    lax.fori_loop(lo, hi, step, 0)


AXES = ("y", "z", "x")


def moved(axis, d):
    y, z, s, x = coords()
    if axis == "y":
        return at((y + d) % 4, z, s, x)
    if axis == "z":
        return at(y, (z + d) % 4, s, x)
    return at(y, z, s, (x + d) % 4)


def other_core():
    y, z, s, x = coords()
    return at(y, z, 1 - s, x)


def lines(axes=AXES):
    return [moved(a, d) for a in axes for d in (1, 2, 3)]


def send(src, dst, ss, rs, dev):
    cp = pltpu.make_async_remote_copy(
        src_ref=src, dst_ref=dst, send_sem=ss, recv_sem=rs, device_id=dev, device_id_type=MESH
    )
    cp.start()
    return cp


ALL = slice(None)


class Gather:
    def __init__(self, items, ss, rs):
        self.items, self.ss, self.rs = items, ss, rs

    def begin(self):
        y, z, s, x = coords()
        self.first = []
        for i, (get, y_first) in enumerate(self.items):
            piece = get(y, z, s)
            for d in (1, 2, 3):
                to = moved("y" if y_first else "z", d)
                self.first.append(
                    send(piece, piece, self.ss.at[i, d - 1], self.rs.at[i, d - 1], to)
                )

    def turn(self):
        y, z, s, x = coords()
        for cp in self.first:
            cp.wait()
        self.second, self.across = {}, []
        for i, (get, y_first) in enumerate(self.items):
            piece = get(ALL, z, s) if y_first else get(y, ALL, s)
            for d in (1, 2, 3):
                to = moved("z" if y_first else "y", d)
                self.second[i, d] = send(
                    piece, piece, self.ss.at[i, d + 2], self.rs.at[i, d + 2], to
                )
        for i, (get, y_first) in enumerate(self.items):
            piece = get(ALL, z, s) if y_first else get(y, ALL, s)
            self.across.append(
                send(piece, piece, self.ss.at[i, 6], self.rs.at[i, 6], other_core())
            )

    def pass_on(self):
        y, z, s, x = coords()
        for d in (1, 3, 2):
            for i, (get, y_first) in enumerate(self.items):
                self.second[i, d].wait_recv()
                piece = get(ALL, (z - d) % 4, s) if y_first else get((y - d) % 4, ALL, s)
                self.across.append(
                    send(piece, piece, self.ss.at[i, 6 + d], self.rs.at[i, 6 + d], other_core())
                )

    def end(self):
        for cp in self.second.values():
            cp.wait_send()
        for cp in self.across:
            cp.wait()

    @staticmethod
    def sems(n):
        return [DMA((n, 10)), DMA((n, 10))]


def split(v):
    hi = v.astype(bf16)
    return hi, (v - hi.astype(f32)).astype(bf16)


class Reduce:
    def __init__(self, src, parts, bufs, ss, rs):
        self.src, self.parts, self.ss, self.rs = src, parts, ss, rs
        y, z, s, x = coords()
        self.me = {"y": y, "z": z, "x": x}
        self.bufs = [bufs[5 * i : 5 * i + 5] for i in range(len(parts))]

    @staticmethod
    def scratch(parts):
        out = []
        for lo, n, order, paired in parts:
            out += [
                pltpu.VMEM((3, 4, 4, n, 128), bf16),
                pltpu.VMEM((4, 4, n, 128), bf16),
                pltpu.VMEM((3, 4, n, 128), bf16),
                pltpu.VMEM((4, n, 128), bf16),
                pltpu.VMEM((3, n, 128), bf16),
            ]
        return out

    @staticmethod
    def sems(parts):
        return [DMA((3, len(parts), 3)), DMA((3, len(parts), 3))]

    @staticmethod
    def summed(pieces, paired):
        v = functools.reduce(lambda a, b: a + b, [p.astype(f32) for p in pieces])
        if not paired:
            return v.astype(bf16)
        half = v.shape[0] // 2
        return jnp.concatenate(split(v[:half] + v[half:]), axis=0)

    def begin(self, stage):
        self.cps = []
        for d in (2, 1, 3):
            for i, (lo, n, order, paired) in enumerate(self.parts):
                r1, h1, r2, h2, r3 = self.bufs[i]
                axis = order[stage]
                place = (self.me[axis] + d) % 4
                left = [a for a in AXES if a not in order[:stage]]
                index = tuple(place if a == axis else ALL for a in left)
                if stage == 0:
                    src = self.src.at[index + (pl.ds(lo, n),)]
                else:
                    src = (h1, h2)[stage - 1].at[index]
                self.cps.append(
                    send(
                        src, (r1, r2, r3)[stage].at[d - 1],
                        self.ss.at[stage, i, d - 1], self.rs.at[stage, i, d - 1], moved(axis, d),
                    )
                )

    def end(self, stage):
        for cp in self.cps:
            cp.wait()
        out = []
        for i, (lo, n, order, paired) in enumerate(self.parts):
            r1, h1, r2, h2, r3 = self.bufs[i]
            mine = self.me[order[stage]]
            if stage == 0:
                axis = AXES.index(order[0])

                def add(k, _, axis=axis, mine=mine, lo=lo, n=n, paired=paired, r1=r1, h1=h1):
                    a, b = k // 4, k % 4
                    index = [a, b]
                    index.insert(axis, mine)
                    own = self.src[tuple(index) + (slice(lo, lo + n),)]
                    h1[a, b] = self.summed([own, r1[0, a, b], r1[1, a, b], r1[2, a, b]], paired)
                    return 0

                lax.fori_loop(0, 16, add, 0)
            elif stage == 1:
                left = [a for a in AXES if a != order[0]]
                first = left.index(order[1]) == 0
                for a in range(4):
                    own = h1[mine, a] if first else h1[a, mine]
                    h2[a] = self.summed([own, r2[0, a], r2[1, a], r2[2, a]], paired)
            else:
                v = h2[mine].astype(f32) + r3[0].astype(f32) + r3[1].astype(f32) + r3[2].astype(f32)
                if paired:
                    v = v[: n // 2] + v[n // 2 :]
                out.append(v)
        return out


MLP_PARTS = ((0, 48, ("y", "z", "x"), False), (48, 48, ("z", "x", "y"), False), (96, 32, ("x", "y", "z"), False))
ATT_PARTS = ((0, 32, ("y", "z", "x"), False), (32, 16, ("z", "x", "y"), False), (48, 32, ("x", "y", "z"), True))


def norm_parts(x_ref, gain, shift):
    xf = x_ref[...].astype(f32)
    centered = xf - jnp.mean(xf, axis=1, keepdims=True)
    inv = lax.rsqrt(jnp.mean(centered * centered, axis=1, keepdims=True) + 1e-05)
    normed = centered * inv
    hidden = (normed * gain + shift).astype(bf16)
    return xf, inv, normed, hidden


def turn(v, co, s1, s2):
    return v * co + pltpu.roll(v, 120, 1) * s1 + pltpu.roll(v, 8, 1) * s2


def wide(w, first, count):
    blocks = [w[(first + i) // 4, (first + i) % 4].reshape(512, 128) for i in range(count)]
    return jnp.concatenate(blocks, axis=1) if count > 1 else blocks[0]


def query_home(piece):
    block = piece // 4
    part = block % 8
    low = part < 4
    return jnp.where(low, part, 7 - part), 2 * (block // 8) + jnp.where(low, 0, 1), piece % 4


def query_block(t, j):
    if isinstance(t, int):
        return 8 * (t // 2) + (j if t % 2 == 0 else 7 - j)
    return 8 * (t // 2) + jnp.where(t % 2 == 0, j, 7 - j)


def front_kernel(
    x_ref, dy_ref, gain_ref, shift_ref, bias_ref, co_ref, s1_ref, s2_ref, wq, wo, wi, wf,
    kv, qd, w1, gm_ref, res_ref, dh_ref, bin_ref,
    t1, t2, t3, w2, w3, kvs, qds, lsem, xs, xr, sa, ra, sb, rb, own_sem, ks, kr, qs, qr, cs, cr,
):
    y, z, s, x = coords()
    c = lax.axis_index("ctx")
    p = c // 2
    tell_slab()
    tell(lines(("x",)))
    rows = pl.ds(64 * s, 64)

    def load(src, dst, k):
        return pltpu.make_async_copy(src, dst, lsem.at[k])

    @pl.when(p < 12)
    def _():
        load(wq.at[rows, pl.ds(pl.multiple_of(jnp.minimum(p, 11) * 128, 128), 128)], t1, 0).start()

    @pl.when(p >= 12)
    def _():
        load(wo.at[rows, pl.ds(pl.multiple_of(jnp.maximum(p - 12, 0) * 128, 128), 128)], t1, 0).start()

    cp2 = load(wi.at[rows, pl.ds(pl.multiple_of(p * 128, 128), 128)], t2, 1)
    cp2.start()
    cp3 = load(wf.at[pl.ds(16 * c, 16)], t3, 2)
    cp3.start()
    load(wo.at[rows, pl.ds(0, 128)], t1, 0).wait()
    cp2.wait()
    cp3.wait()
    w1[y, z, x, s] = t1[...].astype(bf16)
    w2[y, z, x, s] = t2[...].astype(bf16)
    w3[x, y, z, s] = t3[...].astype(bf16)
    met(34)
    cps = []
    for i, own in enumerate((w1.at[y, z, x, s], w2.at[y, z, x, s], w3.at[x, y, z, s])):
        cps.append([
            send(own, own, xs.at[i, d - 1], xr.at[i, d - 1], moved("x", d)) for d in (1, 2, 3)
        ])
    xf, inv, normed, hidden = norm_parts(x_ref, gain_ref[...], shift_ref[...])
    dy = dy_ref[...]
    for cp in cps[0]:
        cp.wait()
    early = Gather(
        [
            (lambda a, b, e: w1.at[a, b, :, e, pl.ds(0, 32)], True),
            (lambda a, b, e: w1.at[a, b, :, e, pl.ds(32, 32)], False),
        ],
        sa, ra,
    )
    late = Gather(
        [
            (lambda a, b, e: w2.at[a, b, :, e], True),
            (lambda a, b, e: w3.at[:, a, b, e], False),
        ],
        sb, rb,
    )
    early.begin()
    early.turn()
    early.pass_on()
    for cp in cps[1] + cps[2]:
        cp.wait()
    late.begin()
    early.end()
    co, s1, s2 = co_ref[...], s1_ref[...], s2_ref[...]
    left = lax.broadcasted_iota(jnp.int32, (TOK, 128), 1) < 64
    dctx = dot_nt(dy, wide(w1, 12, 4))
    for half in range(2):
        thirds = []
        for third in range(3):
            b = third * 4 + 2 * half
            thirds.append(dot(hidden, wide(w1, b, 2)) + bias_ref[:, b * 128 : b * 128 + 256])
        for e in range(2):
            lanes = slice(128 * e, 128 * e + 128)
            q = turn(thirds[0][:, lanes], co, s1, s2).astype(bf16).astype(f32) * 0.125
            k = turn(thirds[1][:, lanes], co, s1, s2)
            v = thirds[2][:, lanes]
            pair = 2 * half + e
            g = dctx[:, pair * 128 : pair * 128 + 128]
            h = 2 * pair
            kvs[h] = jnp.where(left, k, pltpu.roll(v, 64, 1)).astype(bf16)
            kvs[h + 1] = jnp.where(left, pltpu.roll(k, 64, 1), v).astype(bf16)
            qds[h] = jnp.where(left, q, pltpu.roll(g, 64, 1)).astype(bf16)
            qds[h + 1] = jnp.where(left, pltpu.roll(q, 64, 1), g).astype(bf16)

    def kv_copy(d):
        to = lax.rem(p + d, 16)
        return pltpu.make_async_remote_copy(
            src_ref=kvs.at[to // 2], dst_ref=kv.at[p, s], send_sem=ks.at[d], recv_sem=kr.at[d],
            device_id={"ctx": to * 2 + s}, device_id_type=MESH,
        )

    def across(d):
        block = kv.at[lax.rem(p + 16 - d, 16), s]
        return pltpu.make_async_remote_copy(
            src_ref=block, dst_ref=block, send_sem=cs.at[d], recv_sem=cr.at[d],
            device_id={"ctx": p * 2 + 1 - s}, device_id_type=MESH,
        )

    def each_query(k, what):
        h, i = k // 3, k % 3
        j, t, quarter = query_home(3 * c + i)
        to = 4 * h + j
        src = qds.at[h, pl.ds(64 * i, 64)]
        dst = qd.at[t, pl.ds(64 * quarter, 64)]

        @pl.when(to == c)
        def _():
            if what == "start":
                pltpu.make_async_copy(src, dst, qr).start()

        @pl.when(to != c)
        def _():
            cp = pltpu.make_async_remote_copy(
                src_ref=src, dst_ref=dst, send_sem=qs.at[k], recv_sem=qr,
                device_id={"ctx": to}, device_id_type=MESH,
            )
            if what == "start":
                cp.start()
            else:
                cp.wait_send()

    own = pltpu.make_async_copy(kvs.at[p // 2], kv.at[p, s], own_sem)
    own.start()
    loop(1, 16, lambda d: kv_copy(d).start())
    late.turn()
    loop(0, 24, lambda k: each_query(k, "start"))
    own.wait()
    across(0).start()

    def arrived(d):
        kv_copy(d).wait_recv()
        across(d).start()

    late.pass_on()
    loop(1, 16, arrived)
    late.end()
    root = math.sqrt(2.0 / math.pi)
    mlp = jnp.zeros((TOK, D), f32)
    dh = jnp.zeros((TOK, D), f32)
    for i in range(4):
        w_in = wide(w2, 4 * i, 4)
        w_fin = w3[i].reshape(512, 512)
        pre = dot(hidden, w_in) + bias_ref[:, 2048 + 512 * i : 2560 + 512 * i]
        sq = pre * pre
        th = jnp.tanh(root * (pre + 0.044715 * (pre * sq)))
        act = (0.5 * pre * (1.0 + th)).astype(bf16)
        slope = 0.5 * (1.0 + th) + (0.5 * root) * pre * (1.0 - th * th) * (
            1.0 + (3.0 * 0.044715) * sq
        )
        dpre = (dot_nt(dy, w_fin) * slope).astype(bf16)
        mlp = mlp + dot(act, w_fin)
        dh = dh + dot_nt(dpre, w_in)
        bin_ref[:, 512 * i : 512 * i + 512] = jnp.sum(dpre.astype(f32), axis=0, keepdims=True)
        g_in = dot_tn(dpre, hidden).astype(bf16).reshape(8, 64, 512)
        g_fin = dot_tn(act, dy).astype(bf16).reshape(32, 16, 512)
        for b in range(4):
            lanes = slice(128 * b, 128 * b + 128)
            gm_ref[8 * i : 8 * i + 8, b, 0:64] = g_in[:, :, lanes]
            gm_ref[:, i, 64 + 16 * b : 80 + 16 * b] = g_fin[:, :, lanes]
    res_ref[...] = xf + mlp + bias_ref[:, 4096:4608] + bias_ref[:, 1536:2048]
    dh_ref[...] = dh
    loop(1, 16, lambda d: kv_copy(d).wait_send())
    loop(0, 24, lambda k: each_query(k, "wait"))
    pltpu.make_async_copy(qd, qd, qr).wait()
    loop(0, 16, lambda d: across(d).wait())


def front(x, dy, gain, shift, biases, co, s1, s2, weights):
    V = pltpu.VMEM
    return call(
        front_kernel,
        "front",
        (x, dy, gain, shift, biases, co, s1, s2, *weights),
        [VM] * 8 + [ANY] * 4,
        [
            ((16, 2, TOK, 128), bf16),
            ((NQB, QB, 128), bf16),
            ((4, 4, 4, 2, 64, 128), bf16),
            ((32, 4, 128, 128), bf16),
            ((TOK, D), f32),
            ((TOK, D), f32),
            ((1, 2048), f32),
        ],
        [ANY, ANY] + [VM] * 5,
        [
            V((64, 128), f32), V((64, 128), f32), V((16, 512), f32),
            V((4, 4, 4, 2, 64, 128), bf16), V((4, 4, 4, 2, 16, 512), bf16),
            V((HEADS, TOK, 128), bf16), V((HEADS, TOK, 128), bf16),
            DMA((3,)), DMA((3, 3)), DMA((3, 3)),
            *Gather.sems(2), *Gather.sems(2),
            DMA, DMA((16,)), DMA((16,)), DMA((24,)), DMA, DMA((16,)), DMA((16,)),
        ],
        cid=1,
    )


RETURNS = ((11, 16), (6, 11), (0, 6))


def attention_kernel(
    starts_ref, kv_ref, qd_ref, gm_ref,
    cq, kr, gx_ref,
    kvt, acc, s_sc, p_sc, cqs, half, other, both, rcm, hbuf, *rest,
):
    bufs, (m_s, m_r, ms, mr, ws, wr, ss, sr, qs, qr) = rest[:15], rest[15:]
    y, z, s, x = coords()
    c = lax.axis_index("ctx")
    p = c // 2
    h = c // 4
    j = c % 4
    n = kv_ref.shape[0]
    tell_slab()
    tell(lines(("x",)))
    bnd = starts_ref[x] - x * GROUP

    def prepare(i, _):
        r = pl.multiple_of(i * QB, QB)
        kvt[:, pl.ds(r, QB)] = kv_ref[pl.ds(r, QB), :].T
        acc[pl.ds(r, QB), :] = jnp.zeros((QB, 128), f32)
        return 0

    lax.fori_loop(0, n // QB, prepare, 0)
    lane = lax.broadcasted_iota(jnp.int32, (QB, 128), 1)

    def block(t):
        qb = query_block(t, j)
        qd = qd_ref[t]
        w1 = jnp.where(lane < 64, qd, jnp.zeros_like(qd))
        w2 = jnp.where(lane < 64, jnp.zeros_like(qd), qd)
        q_t = w1.T
        d_t = w2.T

        def scores(kt, masked, carry, tiles, first=False):
            m8, l8, r8 = carry
            ss, ds = [], []
            for u in range(tiles):
                r = pl.multiple_of((kt + u) * QB, QB)
                rows = kv_ref[pl.ds(r, QB), :]
                s = dot(rows, q_t)
                if masked and not (first and u > 0):
                    kp = r + lax.broadcasted_iota(jnp.int32, (QB, QB), 0)
                    qp = qb * QB + lax.broadcasted_iota(jnp.int32, (QB, QB), 1)
                    s = jnp.where((kp <= qp) & ((kp >= bnd) == (qp >= bnd)), s, -1e30)
                dp = dot(rows, d_t)
                s_sc[pl.ds(r, QB), :] = s
                p_sc[pl.ds(r, QB), :] = dp
                ss.append(s.reshape(QB // 8, 8, QB))
                ds.append(dp.reshape(QB // 8, 8, QB))
            mn = m8
            for s3 in ss:
                mn = jnp.maximum(mn, jnp.max(s3, axis=0))
            al = jnp.exp(m8 - mn)
            l8 = l8 * al
            r8 = r8 * al
            for s3, d3 in zip(ss, ds):
                e = jnp.exp(s3 - mn[None])
                l8 = l8 + jnp.sum(e, axis=0)
                r8 = r8 + jnp.sum(e * d3, axis=0)
            return mn, l8, r8

        zero = jnp.zeros((8, QB), f32)
        base = t // 2 * 8
        pairs = (qb - base) // 2 + 1
        carry = lax.fori_loop(
            0, pairs, lambda g, c: scores(base + 2 * g, True, c, 2),
            (jnp.full((8, QB), -1e30, f32), zero, zero),
        )
        if base > 0:
            carry = scores(0, True, carry, UU, True)
        carry = lax.fori_loop(
            1, base // UU, lambda g, c: scores(g * UU, False, c, UU), carry
        )
        m8, l8, r8 = carry
        m = jnp.max(m8, axis=0, keepdims=True)
        w = jnp.exp(m8 - m)
        l = jnp.sum(l8 * w, axis=0, keepdims=True)
        lse = m + jnp.log(l)
        rd = jnp.sum(r8 * w, axis=0, keepdims=True) / l

        def grads(kt, carry, tiles):
            c_t, g_t = carry
            for u in range(tiles):
                r = pl.multiple_of((kt + u) * QB, QB)
                p = jnp.exp(s_sc[pl.ds(r, QB), :] - lse)
                pb = p.astype(bf16)
                ds = (p * (p_sc[pl.ds(r, QB), :] - rd)).astype(bf16)
                c_t = c_t + dot(kvt[64:128, pl.ds(r, QB)], pb)
                g_t = g_t + dot(kvt[0:64, pl.ds(r, QB)], ds)
                acc[pl.ds(r, QB), :] += dot(ds, w1) + dot(pb, w2)
            return c_t, g_t

        z = jnp.zeros((64, QB), f32)
        c = lax.fori_loop(0, base // UU, lambda g, c: grads(g * UU, c, UU), (z, z))
        c_t, g_t = lax.fori_loop(0, pairs, lambda g, c: grads(base + 2 * g, c, 2), c)
        cqs[t] = jnp.concatenate([g_t * 0.125, c_t], axis=0).T.astype(bf16)

    def each_query(t, quarter, what):
        piece = 4 * query_block(t, j) + quarter
        to, i = piece // 3, piece % 3
        src = cqs.at[t, pl.ds(64 * quarter, 64)]
        dst = cq.at[h, pl.ds(64 * i, 64)]

        @pl.when(to == c)
        def _():
            if what == "start":
                pltpu.make_async_copy(src, dst, qr).start()

        @pl.when(to != c)
        def _():
            cp = pltpu.make_async_remote_copy(
                src_ref=src, dst_ref=dst, send_sem=qs.at[t, quarter], recv_sem=qr,
                device_id={"ctx": to}, device_id_type=MESH,
            )
            if what == "start":
                cp.start()
            else:
                cp.wait_send()

    def return_queries(t):
        loop(0, 4, lambda quarter: each_query(t, quarter, "start"))

    swaps = {}

    def exchange(g):
        lo, hi = RETURNS[g]

        def low(i):
            r = pl.multiple_of((2 * i + 1 - s) * TOK, TOK)
            half[i] = acc[pl.ds(r, TOK), :].astype(bf16)

        loop(lo, hi, low)
        part = pl.ds(lo, hi - lo)
        swaps[g] = send(half.at[part], other.at[part], ws.at[g], wr.at[g], other_core())

    def block_copy(i):
        return pltpu.make_async_remote_copy(
            src_ref=both.at[i], dst_ref=kr.at[h, p % 2], send_sem=ss.at[i], recv_sem=sr,
            device_id={"ctx": i * 2 + s}, device_id_type=MESH,
        )

    def push(g):
        lo, hi = RETURNS[g]
        swaps[g].wait()

        def one(i):
            r = pl.multiple_of((2 * i + s) * TOK, TOK)
            both[i] = (acc[pl.ds(r, TOK), :] + other[i].astype(f32)).astype(bf16)

            @pl.when(i == p)
            def _():
                pltpu.make_async_copy(both.at[i], kr.at[h, p % 2], sr).start()

            @pl.when(i != p)
            def _():
                block_copy(i).start()

        loop(lo, hi, one)

    met(34)
    chip = send(gm_ref.at[:, :, 1 - s], rcm, m_s, m_r, other_core())
    sums = Reduce(hbuf, MLP_PARTS, bufs, ms, mr)
    block(5)
    return_queries(5)
    chip.wait()

    def add(i):
        a, b, e = i // 16, (i // 4) % 4, i % 4
        hbuf[a, b, e] = (gm_ref[a, b, s, e].astype(f32) + rcm[a, b, e].astype(f32)).astype(bf16)

    loop(0, 64, add)
    sums.begin(0)
    block(4)
    return_queries(4)
    exchange(0)
    sums.end(0)
    sums.begin(1)
    block(3)
    return_queries(3)
    push(0)
    sums.end(1)
    sums.begin(2)
    block(2)
    return_queries(2)
    exchange(1)
    block(1)
    return_queries(1)
    push(1)
    block(0)
    return_queries(0)
    exchange(2)
    lo = 0
    for v in sums.end(2):
        gx_ref[lo : lo + v.shape[0], :] = v
        lo += v.shape[0]
    push(2)

    def sent(i):
        @pl.when(i != p)
        def _():
            block_copy(i).wait_send()

    loop(0, 16, sent)
    for t in range(NQB):
        loop(0, 4, lambda quarter, t=t: each_query(t, quarter, "wait"))
    pltpu.make_async_copy(cq, cq, qr).wait()
    pltpu.make_async_copy(kr, kr, sr).wait()


def attention(starts, kv, qd, gm):
    V = pltpu.VMEM
    return call(
        attention_kernel,
        "attention",
        (starts, kv, qd, gm),
        [SM, VM, VM, VM],
        [((HEADS, TOK, 128), bf16), ((HEADS, 2, TOK, 128), bf16), ((128, 128), f32)],
        [ANY, ANY, VM],
        [
            V((128, GROUP), bf16),
            V((GROUP, 128), f32),
            V((GROUP, QB), f32),
            V((GROUP, QB), f32),
            V((NQB, QB, 128), bf16),
            V((16, TOK, 128), bf16),
            V((16, TOK, 128), bf16),
            V((16, TOK, 128), bf16),
            V((4, 4, 4, 128, 128), bf16),
            V((4, 4, 4, 128, 128), bf16),
            *Reduce.scratch(MLP_PARTS),
            DMA, DMA, *Reduce.sems(MLP_PARTS),
            DMA((3,)), DMA((3,)), DMA((16,)), DMA, DMA((NQB, 4)), DMA,
        ],
        cid=2,
    )


def back_kernel(
    cq_ref, kr_ref, x_ref, dy_ref, gain_ref, shift_ref, co_ref, s1_ref, s2_ref, w1,
    res_ref, dh_ref, bin_ref, gxm_ref, mq, mo, mi, mf,
    out_ref, gt_ref, ua, gxb_ref, vec_ref,
    dqkv, ga, rcm, hbuf, mwin, mtr, mfin, gx, us, ur, v0, v1, vy, vz, vx, *rest,
):
    bufs, (lsem, m_s, m_r, vs, vr, ms, mr, xs, xr, ss, rs) = rest[:15], rest[15:]
    y, z, s, x = coords()
    c = lax.axis_index("ctx")
    tell(lines())
    tell([other_core()])
    starts = (jnp.minimum(48 * c // 128, 10), 16 * c // 128, 64 * c // 128)
    loads = []
    for k, (m, width) in enumerate(((mq, 256), (mo, 128), (mi, 128))):
        first = pl.multiple_of(starts[k] * 128, 128)
        loads.append(
            pltpu.make_async_copy(
                m.at[:, pl.ds(first, width)], mwin.at[:, pl.ds((0, 256, 384)[k], width)], lsem.at[k]
            )
        )
    loads.append(pltpu.make_async_copy(mf.at[pl.ds(16 * c, 16)], mfin, lsem.at[3]))
    for cp in loads:
        cp.start()
    xf, inv, normed, hidden = norm_parts(x_ref, gain_ref[...], shift_ref[...])
    dy = dy_ref[...]
    co, s1, s2 = co_ref[...], -s1_ref[...], -s2_ref[...]
    left = lax.broadcasted_iota(jnp.int32, (TOK, 128), 1) < 64
    ctx = []
    for pair in range(4):
        a = cq_ref[2 * pair].astype(f32)
        b = cq_ref[2 * pair + 1].astype(f32)
        e = kr_ref[2 * pair, 0].astype(f32) + kr_ref[2 * pair, 1].astype(f32)
        f = kr_ref[2 * pair + 1, 0].astype(f32) + kr_ref[2 * pair + 1, 1].astype(f32)
        dq = jnp.where(left, a, pltpu.roll(b, 64, 1))
        dk = jnp.where(left, e, pltpu.roll(f, 64, 1))
        dqkv[:, 128 * pair : 128 * pair + 128] = turn(dq, co, s1, s2).astype(bf16)
        dqkv[:, 512 + 128 * pair : 640 + 128 * pair] = turn(dk, co, s1, s2).astype(bf16)
        dqkv[:, 1024 + 128 * pair : 1152 + 128 * pair] = jnp.where(
            left, pltpu.roll(e, 64, 1), f
        ).astype(bf16)
        ctx.append(jnp.where(left, pltpu.roll(a, 64, 1), b).astype(bf16))
    ctx = jnp.concatenate(ctx, axis=1)
    hi, lo = split(dot_tn(dy, ctx))
    hi, lo = hi.reshape(4, 4, 2, 16, 512), lo.reshape(4, 4, 2, 16, 512)
    for b in range(4):
        lanes = slice(128 * b, 128 * b + 128)
        ga[:, :, :, b, 48:64] = hi[..., lanes]
        ga[:, :, :, b, 64:80] = lo[..., lanes]
    for i in range(4):
        part = dqkv[:, 384 * i : 384 * i + 384]
        g = dot_tn(part, hidden).astype(bf16).reshape(4, 2, 48, 512)
        for b in range(4):
            ga[i, :, :, b, 0:48] = g[..., 128 * b : 128 * b + 128]
    met(10)
    chip = send(ga.at[:, :, 1 - s], rcm, m_s, m_r, other_core())
    out_ref[...] = (res_ref[...] + dot(ctx, wide(w1, 12, 4))).astype(bf16)
    dh = dh_ref[...]
    for third in range(3):
        part = dqkv[:, 512 * third : 512 * third + 512]
        dh = dh + dot_nt(part, wide(w1, 4 * third, 4))
        v0[2 + third : 3 + third, :] = jnp.sum(part.astype(f32), axis=0, keepdims=True)
    scaled = dh * gain_ref[...]
    dyf = dy.astype(f32)
    gt_ref[...] = dyf + inv * (
        scaled
        - jnp.mean(scaled, axis=1, keepdims=True)
        - normed * jnp.mean(scaled * normed, axis=1, keepdims=True)
    )
    dsum = jnp.sum(dyf, axis=0, keepdims=True)
    v0[0:1, :] = jnp.sum(dh * normed, axis=0, keepdims=True)
    v0[1:2, :] = jnp.sum(dh, axis=0, keepdims=True)
    v0[5:6, :] = dsum
    for i in range(4):
        v0[6 + i : 7 + i, :] = bin_ref[:, 512 * i : 512 * i + 512]
    v0[10:11, :] = dsum
    v0[11:16, :] = jnp.zeros((5, 512), f32)
    chip.wait()
    vcp = [send(v0, v1, vs.at[0], vr.at[0], other_core())]

    def add(i):
        a, b, e = i // 16, (i // 4) % 4, i % 4
        both = ga[a, b, s, e].astype(f32) + rcm[a, b, e].astype(f32)
        hi, lo = split(both[48:64] + both[64:80])
        hbuf[a, b, e, 0:48] = both[0:48].astype(bf16)
        hbuf[a, b, e, 48:64] = hi
        hbuf[a, b, e, 64:80] = lo

    loop(0, 64, add)
    sums = Reduce(hbuf, ATT_PARTS, bufs, ms, mr)
    sums.begin(0)
    for cp in loads:
        cp.wait()
    mtr[...] = mwin[...].T
    offset = 48 * c - starts[0] * 128
    mt = jnp.concatenate(
        [
            mtr[pl.ds(pl.multiple_of(offset, 16), 48), :],
            mtr[pl.ds(pl.multiple_of(256 + 16 * c % 128, 16), 16), :],
            mtr[pl.ds(pl.multiple_of(384 + 64 * c % 128, 64), 64), :],
        ]
        + [mfin[:, 128 * b : 128 * b + 128] for b in range(4)],
        axis=0,
    )

    def vec_stage(k, buf, axis):
        for cp in vcp:
            cp.wait()
        vcp.clear()
        if k == 0:
            v = v0[...] + v1[...]
        else:
            last = (vy, vz)[k - 1]
            v = (last[0] + last[1]) + (last[2] + last[3])
        place = {"y": y, "z": z, "x": x}[axis]
        buf[place] = v
        for d in (1, 2, 3):
            vcp.append(
                send(buf.at[place], buf.at[place], vs.at[3 * k + d], vr.at[3 * k + d], moved(axis, d))
            )

    sums.end(0)
    sums.begin(1)
    vec_stage(0, vy, "y")
    sums.end(1)
    sums.begin(2)
    vec_stage(1, vz, "z")
    g = sums.end(2)
    gx[0:32, :] = g[0]
    gx[32:48, :] = g[1]
    gx[48:64, :] = g[2]
    gx[64:192, :] = gxm_ref[...]
    grad = gx[...]
    u = (1.0 + MU) * grad + (MU * MU) * mt
    ub = u.astype(bf16)
    hi, lo = split(u[48:64])
    us[0, 0:48] = ub[0:48]
    us[0, 48:64] = jnp.zeros((16, 128), bf16)
    us[1, 0:16] = hi
    us[1, 16:32] = lo
    us[1, 32:64] = jnp.zeros((32, 128), bf16)
    us[2] = ub[64:128]
    us[3] = ub[128:192]
    cps = []
    for d in (1, 2, 3):
        cps.append(send(us.at[(x + d) % 4], ur.at[x], xs.at[d - 1], xr.at[d - 1], moved("x", d)))
    vec_stage(2, vx, "x")
    ur[x] = us[x]
    gxb_ref[...] = grad.astype(bf16)
    for cp in cps:
        cp.wait()
    for k in range(4):
        lanes = slice(128 * k, 128 * k + 128)
        piece = ur[k]

        @pl.when(x != 3)
        def _(lanes=lanes, piece=piece):
            ua[y, z, s, :, lanes] = piece

        @pl.when(x == 3)
        def _(k=k, piece=piece):
            for b in range(4):
                ua[y, z, s, 16 * k : 16 * k + 16, 128 * b : 128 * b + 128] = piece[16 * b : 16 * b + 16]

    gather = Gather(
        [
            (lambda a, b, e: ua.at[a, b, e, pl.ds(0, 32)], True),
            (lambda a, b, e: ua.at[a, b, e, pl.ds(32, 32)], False),
        ],
        ss, rs,
    )
    gather.begin()
    for cp in vcp:
        cp.wait()
    vec_ref[...] = (vx[0] + vx[1]) + (vx[2] + vx[3])
    gather.turn()
    gather.pass_on()
    gather.end()


def back(*args):
    V = pltpu.VMEM
    return call(
        back_kernel,
        "back",
        args,
        [VM] * 14 + [ANY] * 4,
        [
            ((TOK, D), bf16),
            ((TOK, D), f32),
            ((4, 4, 2, 64, 512), bf16),
            ((192, 128), bf16),
            ((16, 512), f32),
        ],
        [VM] * 5,
        [
            V((TOK, 1536), bf16),
            V((4, 4, 2, 4, 80, 128), bf16),
            V((4, 4, 4, 80, 128), bf16),
            V((4, 4, 4, 80, 128), bf16),
            V((128, 512), f32),
            V((512, 128), f32),
            V((16, 512), f32),
            V((192, 128), f32),
            V((4, 64, 128), bf16),
            V((4, 64, 128), bf16),
            V((16, 512), f32), V((16, 512), f32),
            V((4, 16, 512), f32), V((4, 16, 512), f32), V((4, 16, 512), f32),
            *Reduce.scratch(ATT_PARTS),
            DMA((4,)), DMA, DMA, DMA((10,)), DMA((10,)),
            *Reduce.sems(ATT_PARTS),
            DMA((3,)), DMA((3,)),
            *Gather.sems(2),
        ],
        cid=3,
    )


def dot3(a, b):
    (ah, al), (bh, bl) = a, b
    return dot(ah, bh) + (dot(ah, bl) + dot(al, bh))


def newton_kernel(
    ua_ref, gxb_ref, ga, oa,
    a_ref, ah, al, ph, pl_, th, tl, uh, ul, os, rows, xs, xr, sg, rg, so, ro,
):
    y, z, s, x = coords()
    tell(lines())
    tell([other_core()])
    ga[y, z, s] = gxb_ref[...]

    def load(hi, lo):
        return hi[...], lo[...]

    def store(hi, lo, v):
        h, l = split(v)
        hi[...] = h
        lo[...] = l

    @pl.when(x == 1)
    def _():
        uh[...] = ua_ref[:, :, :, 0:16, :].reshape(512, 512)
        ul[...] = ua_ref[:, :, :, 16:32, :].reshape(512, 512)
        h, l = uh[...], ul[...]
        a_ref[...] = dot_tn(h, h) + (dot_tn(h, l) + dot_tn(l, h))

    @pl.when(x != 1)
    def _():
        u = ua_ref[...].reshape(2048, 512)
        a_ref[...] = dot_tn(u, u)

    met(10)
    grads = Gather(
        [
            (lambda a, b, e: ga.at[a, b, e, pl.ds(0, 96)], True),
            (lambda a, b, e: ga.at[a, b, e, pl.ds(96, 96)], False),
        ],
        sg, rg,
    )
    grads.begin()
    row = lax.broadcasted_iota(jnp.int32, (512, 512), 0)
    col = lax.broadcasted_iota(jnp.int32, (512, 512), 1)
    eye = row == col
    a = a_ref[...]
    square = jnp.sum(jnp.sum(jnp.where(eye, a, 0.0), axis=0, keepdims=True), axis=1, keepdims=True)
    scale = 1.0 / (jnp.sqrt(square) + 1e-07)
    a_ref[...] = a * (scale * scale)
    mine = ua_ref[y, z, s].astype(f32) * scale

    def poly():
        store(ah, al, a_ref[...])
        sq = dot3(load(ah, al), load(ah, al))
        return C2 * a_ref[...] + C3 * sq + jnp.where(eye, C1, 0.0)

    def step(_, mine):
        store(ph, pl_, poly())
        pair = load(ph, pl_)
        store(th, tl, dot3(pair, load(ah, al)))
        a_ref[...] = dot3(pair, load(th, tl))
        return dot3(split(mine), pair)

    mine = lax.fori_loop(0, 2, step, mine)
    grads.turn()
    mine = lax.fori_loop(2, NS_ITERS - 1, step, mine)
    grads.pass_on()
    store(ph, pl_, poly())
    mine = dot3(split(mine), load(ph, pl_))
    side = jnp.where(x == 0, math.sqrt(1536.0), jnp.where(x == 1, math.sqrt(512.0), math.sqrt(2048.0)))
    mine = mine * (0.2 * side)
    mine = jnp.concatenate(
        [jnp.where(x == 1, mine[0:16] + mine[16:32], mine[0:16]), mine[16:64]], axis=0
    ).astype(bf16)
    for k in range(4):
        by_lanes = mine[:, 128 * k : 128 * k + 128]
        by_rows = jnp.concatenate(
            [mine[16 * k : 16 * k + 16, 128 * b : 128 * b + 128] for b in range(4)], axis=0
        )
        os[k] = jnp.where(x == 3, by_rows, by_lanes)
    cps = []
    for d in (1, 2, 3):
        cps.append(send(os.at[(x + d) % 4], rows.at[x], xs.at[d - 1], xr.at[d - 1], moved("x", d)))
    rows[x] = os[x]
    grads.end()
    for cp in cps:
        cp.wait()
    oa[y, z, s, 0:48] = rows[0, 0:48]
    oa[y, z, s, 48:64] = rows[1, 0:16]
    oa[y, z, s, 64:128] = rows[2]
    oa[y, z, s, 128:192] = rows[3]
    update = Gather(
        [
            (lambda a, b, e: oa.at[a, b, e, pl.ds(0, 96)], True),
            (lambda a, b, e: oa.at[a, b, e, pl.ds(96, 96)], False),
        ],
        so, ro,
    )
    update.begin()
    update.turn()
    update.pass_on()
    update.end()


def newton(ua, gxb):
    V = pltpu.VMEM
    return call(
        newton_kernel,
        "newton_schulz",
        (ua, gxb),
        [VM, VM],
        [((4, 4, 2, 192, 128), bf16), ((4, 4, 2, 192, 128), bf16)],
        [VM, VM],
        [V((512, 512), f32)] + [V((512, 512), bf16)] * 8
        + [V((4, 64, 128), bf16), V((4, 64, 128), bf16), DMA((3,)), DMA((3,))]
        + Gather.sems(2) + Gather.sems(2),
        cid=4,
    )


def update_kernel(
    gx, oa, wq, wo, wi, wf, mq, mo, mi, mf, nmq, nwq, nmo, nwo, nmi, nwi, nmf, nwf
):
    for lo, n, w, m, nm, nw in (
        (0, 48, wq, mq, nmq, nwq),
        (48, 16, wo, mo, nmo, nwo),
        (64, 64, wi, mi, nmi, nwi),
    ):
        step = 384 // n
        if n != 48:
            step = 256 // n
        width = step * n
        for g in range(32 // step):
            cols = slice(g * width, g * width + width)
            grad = gx[g * step : g * step + step, lo : lo + n, :].astype(f32).reshape(width, 128).T
            turn_ = oa[g * step : g * step + step, lo : lo + n, :].astype(f32).reshape(width, 128).T
            nm[:, cols] = MU * m[:, cols] + grad
            nw[:, cols] = (1.0 - LR * WD) * w[:, cols] - LR * turn_
    for b in range(4):
        cols = slice(128 * b, 128 * b + 128)
        rows = slice(128 + 16 * b, 144 + 16 * b)
        grad = gx[:, rows, :].astype(f32).reshape(512, 128)
        turn_ = oa[:, rows, :].astype(f32).reshape(512, 128)
        nmf[:, cols] = MU * mf[:, cols] + grad
        nwf[:, cols] = (1.0 - LR * WD) * wf[:, cols] - LR * turn_


def update(gx, oa, weights, moments):
    outs = []
    for w in weights:
        outs += [(w.shape, f32)] * 2
    return call(
        update_kernel,
        "update_weights",
        (gx, oa, *weights, *moments),
        [VM] * 10,
        outs,
        [VM] * 8,
    )


def body(
    tokens, cotangent, ln_gain, ln_bias, biases, w_qkv, w_out, w_in, w_fin,
    mom_qkv, mom_out, mom_in, mom_fin, vec_mom, starts,
):
    x = lax.axis_index("wsh")
    c = lax.axis_index("ctx")
    weights = (w_qkv, w_out, w_in, w_fin)
    moments = (mom_qkv, mom_out, mom_in, mom_fin)
    bnd = lax.dynamic_slice(starts, (x,), (1,)) - x * GROUP
    places = c * TOK + jnp.arange(TOK, dtype=jnp.int32)
    pos = (places - jnp.where(places >= bnd[0], bnd[0], 0)).astype(f32)
    lane = jnp.arange(128) % HD
    freq = 10000.0 ** (-2.0 * jnp.arange(ROT // 2, dtype=f32) / ROT)
    freq = jnp.where(lane < ROT, jnp.tile(freq, 16), 0.0)
    angles = pos[:, None] * freq[None, :]
    co = jnp.cos(angles)
    si = jnp.sin(angles)
    s1 = jnp.where(lane < 8, -si, 0.0)
    s2 = jnp.where((lane >= 8) & (lane < 16), si, 0.0)
    gain, shift = ln_gain[None, :], ln_bias[None, :]
    kv, qd, w1, gm, res, dh, bin_sum = front(
        tokens, cotangent, gain, shift, biases[None, :], co, s1, s2, weights
    )
    cq, kr, gxm = attention(
        starts, kv.reshape(GROUP, 128), qd, gm.reshape(4, 4, 2, 4, 128, 128)
    )
    block_out, grad_tokens, ua, gxb, vec_sum = back(
        cq, kr, tokens, cotangent, gain, shift, co, s1, s2, w1, res, dh, bin_sum, gxm, *moments
    )
    gx, oa = newton(ua, gxb)
    new = update(gx.reshape(32, 192, 128), oa.reshape(32, 192, 128), weights, moments)
    vec_moment = VMU * vec_mom + vec_sum.reshape(-1)[:5632]
    vec_new = jnp.concatenate([ln_gain, ln_bias, biases]) - VLR * vec_moment
    return (block_out, grad_tokens, *new, vec_moment, vec_new)


def solution(mesh):
    tok = P(("wsh", "ctx"), None)
    row = P("wsh", None)
    return jax.shard_map(
        body,
        mesh=mesh,
        in_specs=(tok, tok, P(), P(), P()) + (row,) * 8 + (P(), P()),
        out_specs=(tok, tok) + (row,) * 8 + (P(), P()),
        check_vma=False,
    )
```

```python
import functools
import math
import types

import jax
import jax.numpy as jnp
from jax import lax
from jax.experimental import pallas as pl
from jax.experimental.pallas import tpu as pltpu
from jax.sharding import PartitionSpec as P

f32 = jnp.float32
bf16 = jnp.bfloat16
MESH = pl.DeviceIdType.MESH
HEADS = 8
HD = 64
ROT = 16
D = 512
TOK = 192
GROUP = 6144
QB = 256
NQB = 6
HB = 128
UU = 8
TT = 4
NS_ITERS = 5
C1, C2, C3 = 3.4445, -4.775, 2.0315
MU, LR, WD = 0.95, 0.6, 0.01
VMU, VLR = 0.9, 0.0005
R_QKV, R_OUT, R_IN, R_FIN = 48, 16, 64, 64

VM = pl.BlockSpec(memory_space=pltpu.VMEM)
SM = pl.BlockSpec(memory_space=pltpu.SMEM)
ANY = pl.BlockSpec(memory_space=pl.ANY)
DMA = pltpu.SemaphoreType.DMA


def dot(a, b):
    return jnp.dot(a, b, preferred_element_type=f32)


def dot_nt(a, b):
    return lax.dot_general(a, b, (((1,), (1,)), ((), ())), preferred_element_type=f32)


def dot_tn(a, b):
    return lax.dot_general(a, b, (((0,), (0,)), ((), ())), preferred_element_type=f32)


def coords():
    c = lax.axis_index("ctx")
    return c // 8, (c // 2) % 4, c % 2, lax.axis_index("wsh")


def at(y, z, s, x):
    return {"ctx": (y * 4 + z) * 2 + s, "wsh": x}


def tell(partners):
    sem = pltpu.get_barrier_semaphore()
    for p in partners:
        pl.semaphore_signal(sem, inc=1, device_id=p, device_id_type=MESH)


def tell_slab():
    c = lax.axis_index("ctx")
    sem = pltpu.get_barrier_semaphore()

    def one(d, _):
        pl.semaphore_signal(
            sem, inc=1, device_id={"ctx": lax.rem(c + d, 32)}, device_id_type=MESH
        )
        return 0

    lax.fori_loop(1, 32, one, 0)


def met(count):
    pl.semaphore_wait(pltpu.get_barrier_semaphore(), count)


def loop(lo, hi, f):
    def step(i, _):
        f(i)
        return 0

    lax.fori_loop(lo, hi, step, 0)


AXES = ("y", "z", "x")


def moved(axis, d):
    y, z, s, x = coords()
    if axis == "y":
        return at((y + d) % 4, z, s, x)
    if axis == "z":
        return at(y, (z + d) % 4, s, x)
    return at(y, z, s, (x + d) % 4)


def other_core():
    y, z, s, x = coords()
    return at(y, z, 1 - s, x)


def lines(axes=AXES):
    return [moved(a, d) for a in axes for d in (1, 2, 3)]


def send(src, dst, ss, rs, dev):
    cp = pltpu.make_async_remote_copy(
        src_ref=src, dst_ref=dst, send_sem=ss, recv_sem=rs, device_id=dev, device_id_type=MESH
    )
    cp.start()
    return cp


ALL = slice(None)


class Gather:
    def __init__(self, items, ss, rs):
        self.items, self.ss, self.rs = items, ss, rs

    def begin(self):
        y, z, s, x = coords()
        self.first = []
        for i, (get, y_first) in enumerate(self.items):
            piece = get(y, z, s)
            for d in (1, 2, 3):
                to = moved("y" if y_first else "z", d)
                self.first.append(
                    send(piece, piece, self.ss.at[i, d - 1], self.rs.at[i, d - 1], to)
                )

    def turn(self):
        y, z, s, x = coords()
        for cp in self.first:
            cp.wait()
        self.second, self.across = {}, []
        for i, (get, y_first) in enumerate(self.items):
            piece = get(ALL, z, s) if y_first else get(y, ALL, s)
            for d in (1, 2, 3):
                to = moved("z" if y_first else "y", d)
                self.second[i, d] = send(
                    piece, piece, self.ss.at[i, d + 2], self.rs.at[i, d + 2], to
                )
        for i, (get, y_first) in enumerate(self.items):
            piece = get(ALL, z, s) if y_first else get(y, ALL, s)
            self.across.append(
                send(piece, piece, self.ss.at[i, 6], self.rs.at[i, 6], other_core())
            )

    def pass_on(self):
        y, z, s, x = coords()
        for d in (1, 3, 2):
            for i, (get, y_first) in enumerate(self.items):
                self.second[i, d].wait_recv()
                piece = get(ALL, (z - d) % 4, s) if y_first else get((y - d) % 4, ALL, s)
                self.across.append(
                    send(piece, piece, self.ss.at[i, 6 + d], self.rs.at[i, 6 + d], other_core())
                )

    def end(self):
        for cp in self.second.values():
            cp.wait_send()
        for cp in self.across:
            cp.wait()

    @staticmethod
    def sems(n):
        return [DMA((n, 10)), DMA((n, 10))]


def split(v):
    hi = v.astype(bf16)
    return hi, (v - hi.astype(f32)).astype(bf16)


class Reduce:
    def __init__(self, src, parts, bufs, ss, rs):
        self.src, self.parts, self.ss, self.rs = src, parts, ss, rs
        y, z, s, x = coords()
        self.me = {"y": y, "z": z, "x": x}
        self.bufs = [bufs[5 * i : 5 * i + 5] for i in range(len(parts))]

    @staticmethod
    def scratch(parts):
        out = []
        for lo, n, order, paired in parts:
            out += [
                pltpu.VMEM((3, 4, 4, n, 128), bf16),
                pltpu.VMEM((4, 4, n, 128), bf16),
                pltpu.VMEM((3, 4, n, 128), bf16),
                pltpu.VMEM((4, n, 128), bf16),
                pltpu.VMEM((3, n, 128), bf16),
            ]
        return out

    @staticmethod
    def sems(parts):
        return [DMA((3, len(parts), 3)), DMA((3, len(parts), 3))]

    @staticmethod
    def summed(pieces, paired):
        v = functools.reduce(lambda a, b: a + b, [p.astype(f32) for p in pieces])
        if not paired:
            return v.astype(bf16)
        half = v.shape[-2] // 2
        return jnp.concatenate(split(v[..., :half, :] + v[..., half:, :]), axis=-2)

    def begin(self, stage):
        self.cps = []
        for d in (2, 1, 3):
            for i, (lo, n, order, paired) in enumerate(self.parts):
                r1, h1, r2, h2, r3 = self.bufs[i]
                axis = order[stage]
                place = (self.me[axis] + d) % 4
                left = [a for a in AXES if a not in order[:stage]]
                index = tuple(place if a == axis else ALL for a in left)
                if stage == 0:
                    src = self.src.at[index + (pl.ds(lo, n),)]
                else:
                    src = (h1, h2)[stage - 1].at[index]
                self.cps.append(
                    send(
                        src, (r1, r2, r3)[stage].at[d - 1],
                        self.ss.at[stage, i, d - 1], self.rs.at[stage, i, d - 1], moved(axis, d),
                    )
                )

    def end(self, stage):
        for cp in self.cps:
            cp.wait()
        out = []
        for i, (lo, n, order, paired) in enumerate(self.parts):
            r1, h1, r2, h2, r3 = self.bufs[i]
            mine = self.me[order[stage]]
            if stage == 0:
                axis = AXES.index(order[0])

                def add(a, _, axis=axis, mine=mine, lo=lo, n=n, paired=paired, r1=r1, h1=h1):
                    index = [a, ALL]
                    index.insert(axis, mine)
                    own = self.src[tuple(index) + (slice(lo, lo + n),)]
                    h1[a] = self.summed([own, r1[0, a], r1[1, a], r1[2, a]], paired)
                    return 0

                lax.fori_loop(0, 4, add, 0)
            elif stage == 1:
                left = [a for a in AXES if a != order[0]]
                first = left.index(order[1]) == 0
                own = h1[mine] if first else h1[:, mine]
                h2[...] = self.summed([own, r2[0], r2[1], r2[2]], paired)
            else:
                v = h2[mine].astype(f32) + r3[0].astype(f32) + r3[1].astype(f32) + r3[2].astype(f32)
                if paired:
                    v = v[: n // 2] + v[n // 2 :]
                out.append(v)
        return out


MLP_PARTS = ((0, 48, ("y", "z", "x"), False), (48, 48, ("z", "x", "y"), False), (96, 32, ("x", "y", "z"), False))
ATT_PARTS = ((0, 32, ("y", "z", "x"), False), (32, 16, ("z", "x", "y"), False), (48, 32, ("x", "y", "z"), True))


def norm_parts(x_ref, gain, shift):
    xf = x_ref[...].astype(f32)
    centered = xf - jnp.mean(xf, axis=1, keepdims=True)
    inv = lax.rsqrt(jnp.mean(centered * centered, axis=1, keepdims=True) + 1e-05)
    normed = centered * inv
    hidden = (normed * gain + shift).astype(bf16)
    return xf, inv, normed, hidden


def turn(v, co, s1, s2):
    return v * co + pltpu.roll(v, 120, 1) * s1 + pltpu.roll(v, 8, 1) * s2


def rolled(ref, x):
    parts = [ref[:, pl.ds(pl.multiple_of((x + d) % 4 * 128, 128), 128)] for d in range(4)]
    return jnp.concatenate(parts, axis=1)


def unroll(v, ref, x):
    for d in range(4):
        ref[:, pl.ds(pl.multiple_of((x + d) % 4 * 128, 128), 128)] = v[:, 128 * d : 128 * d + 128]
    return ref[...]


def rotary(starts_ref, x, c):
    bnd = starts_ref[x] - x * GROUP
    place = c * TOK + lax.broadcasted_iota(jnp.int32, (TOK, 128), 0)
    pos = (place - jnp.where(place >= bnd, bnd, 0)).astype(f32)
    lane = lax.broadcasted_iota(jnp.int32, (TOK, 128), 1) % HD
    freq = jnp.zeros((TOK, 128), f32)
    for i in range(ROT // 2):
        freq = jnp.where(lane % 8 == i, 10000.0 ** (-2.0 * i / ROT), freq)
    angle = pos * jnp.where(lane < ROT, freq, 0.0)
    co, si = jnp.cos(angle), jnp.sin(angle)
    return co, jnp.where(lane < 8, -si, 0.0), jnp.where(lane < 8, 0.0, si)


def wide(w, first, count):
    blocks = [w[(first + i) // 4, (first + i) % 4].reshape(512, 128) for i in range(count)]
    return jnp.concatenate(blocks, axis=1) if count > 1 else blocks[0]


def query_home(piece):
    block = piece // 4
    part = block % 8
    low = part < 4
    return jnp.where(low, part, 7 - part), 2 * (block // 8) + jnp.where(low, 0, 1), piece % 4


def query_block(t, j):
    if isinstance(t, int):
        return 8 * (t // 2) + (j if t % 2 == 0 else 7 - j)
    return 8 * (t // 2) + jnp.where(t % 2 == 0, j, 7 - j)


def front_phase(r):
    y, z, s, x = coords()
    c = lax.axis_index("ctx")
    p = c // 2
    w1, w2, w3, kvs, qds, kv, qd = r.w1, r.w2, r.w3, r.kvs, r.qds, r.kv, r.qd
    ks, kr, qs, qr, cs, cr = r.ks, r.kvr, r.qs, r.qr, r.cs, r.cr
    bias_ref = r.bias
    tell_slab()
    tell(lines(("x",)))
    loads = [
        pltpu.make_async_copy(src, dst, r.lsem.at[k])
        for k, (src, dst) in enumerate(
            ((r.wq, r.fq), (r.wo, r.fo), (r.wi, r.fi), (r.wf, r.ff), (r.x_in, r.x), (r.dy_in, r.dy))
        )
    ]
    for cp in loads:
        cp.start()
    momenta_begin(r)
    for cp in loads:
        cp.wait()
    for b in range(16):
        w = r.fq[:, 128 * b : 128 * b + 128] if b < 12 else r.fo[:, 128 * b - 1536 : 128 * b - 1408]
        w1[b // 4, b % 4, 0] = w.astype(bf16).reshape(2, 64, 128)
        w2[b // 4, b % 4, 0] = r.fi[:, 128 * b : 128 * b + 128].astype(bf16).reshape(2, 64, 128)
    w3[0] = r.ff[...].astype(bf16).reshape(4, 4, 2, 16, 512)
    met(34)
    cps = []
    for i, piece in enumerate(
        (lambda d: w1.at[y, z, d, s], lambda d: w2.at[y, z, d, s], lambda d: w3.at[d, y, z, s])
    ):
        cps.append([
            send(piece(0), piece(4 - d), r.xs.at[i, d - 1], r.xr.at[i, d - 1], moved("x", d))
            for d in (1, 2, 3)
        ])
    co, s1, s2 = rotary(r.starts, x, c)
    r.co[...], r.s1[...], r.s2[...] = co, s1, s2
    xf, inv, normed, hidden = norm_parts(r.x, r.gain[...], r.shift[...])
    r.hid[...] = hidden
    hidden_r = rolled(r.hid, x)
    dy = r.dy[...]
    for cp in cps[0]:
        cp.wait()
    others = pl.ds(1, 3)
    early = Gather(
        [
            (lambda a, b, e: w1.at[a, b, others, e, pl.ds(0, 32)], True),
            (lambda a, b, e: w1.at[a, b, others, e, pl.ds(32, 32)], False),
        ],
        r.sa, r.ra,
    )
    late = Gather(
        [
            (lambda a, b, e: w2.at[a, b, others, e], True),
            (lambda a, b, e: w3.at[others, a, b, e], False),
        ],
        r.sb, r.rb,
    )
    early.begin()
    early.turn()
    early.pass_on()
    for cp in cps[1] + cps[2]:
        cp.wait()
    late.begin()
    early.end()
    left = lax.broadcasted_iota(jnp.int32, (TOK, 128), 1) < 64
    dctx = unroll(dot_nt(dy, wide(w1, 12, 4)), r.wide_f, x)
    for half in range(2):
        if half == 1:
            late.turn()
        thirds = []
        for third in range(3):
            b = third * 4 + 2 * half
            thirds.append(dot(hidden_r, wide(w1, b, 2)) + bias_ref[:, b * 128 : b * 128 + 256])
        for e in range(2):
            lanes = slice(128 * e, 128 * e + 128)
            q = turn(thirds[0][:, lanes], co, s1, s2).astype(bf16).astype(f32) * 0.125
            k = turn(thirds[1][:, lanes], co, s1, s2)
            v = thirds[2][:, lanes]
            pair = 2 * half + e
            g = dctx[:, pair * 128 : pair * 128 + 128]
            h = 2 * pair
            kvs[h] = jnp.where(left, k, pltpu.roll(v, 64, 1)).astype(bf16)
            kvs[h + 1] = jnp.where(left, pltpu.roll(k, 64, 1), v).astype(bf16)
            qds[h] = jnp.where(left, q, pltpu.roll(g, 64, 1)).astype(bf16)
            qds[h + 1] = jnp.where(left, pltpu.roll(q, 64, 1), g).astype(bf16)

    def kv_copy(d):
        to = lax.rem(p + d, 16)
        return pltpu.make_async_remote_copy(
            src_ref=kvs.at[to // 2], dst_ref=kv.at[pl.ds(c * TOK, TOK)], send_sem=ks.at[d], recv_sem=kr.at[d],
            device_id={"ctx": to * 2 + s}, device_id_type=MESH,
        )

    def across(d):
        block = kv.at[pl.ds((lax.rem(p + 16 - d, 16) * 2 + s) * TOK, TOK)]
        return pltpu.make_async_remote_copy(
            src_ref=block, dst_ref=block, send_sem=cs.at[d], recv_sem=cr.at[d],
            device_id={"ctx": p * 2 + 1 - s}, device_id_type=MESH,
        )

    def each_query(k, what):
        h, i = k // 3, k % 3
        j, t, quarter = query_home(3 * c + i)
        to = 4 * h + j
        src = qds.at[h, pl.ds(64 * i, 64)]
        dst = qd.at[t, pl.ds(64 * quarter, 64)]

        @pl.when(to == c)
        def _():
            if what == "start":
                pltpu.make_async_copy(src, dst, qr).start()

        @pl.when(to != c)
        def _():
            cp = pltpu.make_async_remote_copy(
                src_ref=src, dst_ref=dst, send_sem=qs.at[k], recv_sem=qr,
                device_id={"ctx": to}, device_id_type=MESH,
            )
            if what == "start":
                cp.start()
            else:
                cp.wait_send()

    own = pltpu.make_async_copy(kvs.at[p // 2], kv.at[pl.ds(c * TOK, TOK)], r.own_sem)
    own.start()
    loop(1, 16, lambda d: kv_copy(d).start())
    loop(0, 24, lambda k: each_query(k, "start"))
    own.wait()
    across(0).start()

    def arrived(d):
        kv_copy(d).wait_recv()
        across(d).start()

    late.pass_on()
    late.end()
    root = math.sqrt(2.0 / math.pi)
    mlp = jnp.zeros((TOK, D), f32)
    dh = jnp.zeros((TOK, D), f32)
    for i in range(4):
        if i == 2:
            loop(1, 16, arrived)
        w_in = wide(w2, 4 * i, 4)
        w_fin = w3[(i + 4 - x) % 4].reshape(512, 512)
        pre = dot(hidden_r, w_in) + bias_ref[:, 2048 + 512 * i : 2560 + 512 * i]
        sq = pre * pre
        th = jnp.tanh(root * (pre + 0.044715 * (pre * sq)))
        act = (0.5 * pre * (1.0 + th)).astype(bf16)
        slope = 0.5 * (1.0 + th) + (0.5 * root) * pre * (1.0 - th * th) * (
            1.0 + (3.0 * 0.044715) * sq
        )
        dpre = (dot_nt(dy, w_fin) * slope).astype(bf16)
        mlp = mlp + dot(act, w_fin)
        dh = dh + dot_nt(dpre, w_in)
        r.v0[6 + i : 7 + i, :] = jnp.sum(dpre.astype(f32), axis=0, keepdims=True)
        g_in = dot_tn(dpre, hidden).astype(bf16).reshape(4, 2, 64, 512)
        g_fin = dot_tn(act, dy).astype(bf16).reshape(4, 4, 2, 16, 512)
        for b in range(4):
            lanes = slice(128 * b, 128 * b + 128)
            r.gm[i, :, :, b, 0:64] = g_in[..., lanes]
            r.gm[:, :, :, i, 64 + 16 * b : 80 + 16 * b] = g_fin[..., lanes]
    r.res[...] = xf + mlp + bias_ref[:, 4096:4608] + bias_ref[:, 1536:2048]
    r.dh[...] = dh
    chip = send(r.gm.at[:, :, 1 - s], r.rcm, r.m_s.at[0], r.m_r.at[0], other_core())
    loop(1, 16, lambda d: kv_copy(d).wait_send())
    loop(0, 24, lambda k: each_query(k, "wait"))
    pltpu.make_async_copy(qd, qd, qr).wait()
    loop(0, 16, lambda d: across(d).wait())
    return chip


RETURNS = ((11, 16), (6, 11), (0, 6))


def attention_phase(r, chip):
    kvt, acc, s_sc, p_sc, m_sc, cqs = r.kvt, r.acc, r.s_sc, r.p_sc, r.m_sc, r.cqs
    half, other, both, rcm, hbuf = r.half, r.other, r.both, r.rcm, r.hbuf
    cq, kr, kv_ref, qd_ref, gm_ref = r.cq, r.kr, r.kv, r.qd, r.gm
    ws, wr, ss, sr, qs, qr = r.ws, r.wr, r.bs, r.br, r.rqs, r.rqr
    y, z, s, x = coords()
    c = lax.axis_index("ctx")
    p = c // 2
    h = c // 4
    j = c % 4
    n = kv_ref.shape[0]
    bnd = r.starts[x] - x * GROUP

    def prepare(i, _):
        o = pl.multiple_of(i * QB, QB)
        kvt[:, pl.ds(o, QB)] = kv_ref[pl.ds(o, QB), :].T
        acc[pl.ds(o, QB), :] = jnp.zeros((QB, 128), f32)
        return 0

    lax.fori_loop(0, n // QB, prepare, 0)
    lane = lax.broadcasted_iota(jnp.int32, (QB, 128), 1)

    def block(t):
        qb = query_block(t, j)
        qd = qd_ref[t]
        w1 = jnp.where(lane < 64, qd, jnp.zeros_like(qd))
        w2 = jnp.where(lane < 64, jnp.zeros_like(qd), qd)
        q_t = w1.T
        d_t = w2.T

        def scores(kt, masked, carry, tiles, first=False):
            m8, l8, r8 = carry
            for u in range(2 * tiles):
                o = pl.multiple_of(kt * QB + u * HB, HB)
                rows = kv_ref[pl.ds(o, HB), :]
                s = dot(rows, q_t)
                if masked and not (first and u > 1):
                    kp = o + lax.broadcasted_iota(jnp.int32, (HB, QB), 0)
                    qp = qb * QB + lax.broadcasted_iota(jnp.int32, (HB, QB), 1)
                    s = jnp.where((kp <= qp) & ((kp >= bnd) == (qp >= bnd)), s, -1e30)
                s = s.reshape(HB // 8, 8, QB)
                dp = dot(rows, d_t)
                p_sc[pl.ds(o, HB), :] = dp
                mn = jnp.maximum(m8, jnp.max(s, axis=0))
                e = jnp.exp(s - mn[None])
                s_sc[pl.ds(o, HB), :] = e.reshape(HB, QB)
                m_sc[2 * kt + u] = mn
                al = jnp.exp(m8 - mn)
                l8 = l8 * al + jnp.sum(e, axis=0)
                r8 = r8 * al + jnp.sum(e * dp.reshape(HB // 8, 8, QB), axis=0)
                m8 = mn
            return m8, l8, r8

        zero = jnp.zeros((8, QB), f32)
        base = t // 2 * 8
        tail = (qb - base) // TT + 1
        carry = lax.fori_loop(
            0, tail, lambda g, c: scores(base + TT * g, True, c, TT),
            (jnp.full((8, QB), -1e30, f32), zero, zero),
        )
        if base > 0:
            carry = scores(0, True, carry, UU, True)
        carry = lax.fori_loop(
            1, base // UU, lambda g, c: scores(g * UU, False, c, UU), carry
        )
        m8, l8, r8 = carry
        m = jnp.max(m8, axis=0, keepdims=True)
        w = jnp.exp(m8 - m)
        l = jnp.sum(l8 * w, axis=0, keepdims=True)
        lse = m + jnp.log(l)
        rd = jnp.sum(r8 * w, axis=0, keepdims=True) / l

        def grads(kt, carry, tiles):
            c_t, g_t = carry
            for u in range(tiles):
                o = pl.multiple_of((kt + u) * QB, QB)
                e = s_sc[pl.ds(o, QB), :].reshape(2, HB // 8, 8, QB)
                w0 = jnp.exp(m_sc[2 * (kt + u)] - lse)
                w1_ = jnp.exp(m_sc[2 * (kt + u) + 1] - lse)
                p = jnp.concatenate([e[0] * w0[None], e[1] * w1_[None]], axis=0).reshape(QB, QB)
                pb = p.astype(bf16)
                ds = (p * (p_sc[pl.ds(o, QB), :] - rd)).astype(bf16)
                c_t = c_t + dot(kvt[64:128, pl.ds(o, QB)], pb)
                g_t = g_t + dot(kvt[0:64, pl.ds(o, QB)], ds)
                acc[pl.ds(o, QB), :] += dot(ds, w1) + dot(pb, w2)
            return c_t, g_t

        z = jnp.zeros((64, QB), f32)
        c = lax.fori_loop(0, base // UU, lambda g, c: grads(g * UU, c, UU), (z, z))
        c_t, g_t = lax.fori_loop(0, tail, lambda g, c: grads(base + TT * g, c, TT), c)
        cqs[t] = jnp.concatenate([g_t * 0.125, c_t], axis=0).T.astype(bf16)

    def each_query(t, quarter, what):
        piece = 4 * query_block(t, j) + quarter
        to, i = piece // 3, piece % 3
        src = cqs.at[t, pl.ds(64 * quarter, 64)]
        dst = cq.at[h, pl.ds(64 * i, 64)]

        @pl.when(to == c)
        def _():
            if what == "start":
                pltpu.make_async_copy(src, dst, qr).start()

        @pl.when(to != c)
        def _():
            cp = pltpu.make_async_remote_copy(
                src_ref=src, dst_ref=dst, send_sem=qs.at[t, quarter], recv_sem=qr,
                device_id={"ctx": to}, device_id_type=MESH,
            )
            if what == "start":
                cp.start()
            else:
                cp.wait_send()

    def return_queries(t):
        loop(0, 4, lambda quarter: each_query(t, quarter, "start"))

    swaps = {}

    def exchange(g):
        lo, hi = RETURNS[g]

        def low(i):
            o = pl.multiple_of((2 * i + 1 - s) * TOK, TOK)
            half[i] = acc[pl.ds(o, TOK), :].astype(bf16)

        loop(lo, hi, low)
        part = pl.ds(lo, hi - lo)
        swaps[g] = send(half.at[part], other.at[part], ws.at[g], wr.at[g], other_core())

    def block_copy(i):
        return pltpu.make_async_remote_copy(
            src_ref=both.at[i], dst_ref=kr.at[h, p % 2], send_sem=ss.at[i], recv_sem=sr,
            device_id={"ctx": i * 2 + s}, device_id_type=MESH,
        )

    def push(g):
        lo, hi = RETURNS[g]
        swaps[g].wait()

        def one(i):
            o = pl.multiple_of((2 * i + s) * TOK, TOK)
            both[i] = (acc[pl.ds(o, TOK), :] + other[i].astype(f32)).astype(bf16)

            @pl.when(i == p)
            def _():
                pltpu.make_async_copy(both.at[i], kr.at[h, p % 2], sr).start()

            @pl.when(i != p)
            def _():
                block_copy(i).start()

        loop(lo, hi, one)

    def add(i):
        a, b = i // 4, i % 4
        hbuf[a, b] = (gm_ref[a, b, s].astype(f32) + rcm[a, b].astype(f32)).astype(bf16)

    chip.wait()
    loop(0, 16, add)
    sums = Reduce(hbuf, MLP_PARTS, r.mlp_bufs, r.ms, r.mr)
    sums.begin(0)
    block(5)
    return_queries(5)
    block(4)
    return_queries(4)
    exchange(0)
    sums.end(0)
    sums.begin(1)
    block(3)
    return_queries(3)
    push(0)
    sums.end(1)
    sums.begin(2)
    block(2)
    return_queries(2)
    exchange(1)
    block(1)
    return_queries(1)
    push(1)
    block(0)
    return_queries(0)
    exchange(2)
    lo = 64
    for v in sums.end(2):
        r.gx[lo : lo + v.shape[0], :] = v
        lo += v.shape[0]
    push(2)

    def sent(i):
        @pl.when(i != p)
        def _():
            block_copy(i).wait_send()

    loop(0, 16, sent)
    for t in range(NQB):
        loop(0, 4, lambda quarter, t=t: each_query(t, quarter, "wait"))
    pltpu.make_async_copy(cq, cq, qr).wait()
    pltpu.make_async_copy(kr, kr, sr).wait()


def momenta_starts():
    c = lax.axis_index("ctx")
    return jnp.minimum(48 * c // 128, 10), 16 * c // 128, 64 * c // 128


def momenta_loads(r):
    c = lax.axis_index("ctx")
    starts = momenta_starts()
    loads = []
    for k, (m, width) in enumerate(((r.mq, 256), (r.mo, 128), (r.mi, 128))):
        first = pl.multiple_of(starts[k] * 128, 128)
        loads.append(
            pltpu.make_async_copy(
                m.at[:, pl.ds(first, width)],
                r.mwin.at[:, pl.ds((0, 256, 384)[k], width)],
                r.msem.at[k],
            )
        )
    loads.append(pltpu.make_async_copy(r.mf.at[pl.ds(16 * c, 16)], r.mfin, r.msem.at[3]))
    return loads


def momenta_begin(r):
    for cp in momenta_loads(r):
        cp.start()


def momenta(r):
    c = lax.axis_index("ctx")
    for cp in momenta_loads(r):
        cp.wait()
    r.mtr[...] = r.mwin[...].T
    offset = 48 * c - momenta_starts()[0] * 128
    return jnp.concatenate(
        [
            r.mtr[pl.ds(pl.multiple_of(offset, 16), 48), :],
            r.mtr[pl.ds(pl.multiple_of(256 + 16 * c % 128, 16), 16), :],
            r.mtr[pl.ds(pl.multiple_of(384 + 64 * c % 128, 64), 64), :],
        ]
        + [r.mfin[:, 128 * b : 128 * b + 128] for b in range(4)],
        axis=0,
    )


def back_phase(r):
    dqkv, gx, us, ur, v0, v1, vy, vz, vx = r.dqkv, r.gx, r.us, r.ur, r.v0, r.v1, r.vy, r.vz, r.vx
    cq_ref, kr_ref, w1, ga, rcm, hbuf = r.cq, r.kr, r.w1, r.gm, r.rcm, r.hbuf
    vs, vr, xs, xr, ua = r.vs, r.vr, r.us_s, r.us_r, r.w3
    att = pl.ds(0, 80)
    y, z, s, x = coords()
    c = lax.axis_index("ctx")
    xf, inv, normed, hidden = norm_parts(r.x, r.gain[...], r.shift[...])
    dy = r.dy[...]
    co, s1, s2 = r.co[...], -r.s1[...], -r.s2[...]
    left = lax.broadcasted_iota(jnp.int32, (TOK, 128), 1) < 64
    ctx = []
    for pair in range(4):
        a = cq_ref[2 * pair].astype(f32)
        b = cq_ref[2 * pair + 1].astype(f32)
        e = kr_ref[2 * pair, 0].astype(f32) + kr_ref[2 * pair, 1].astype(f32)
        f = kr_ref[2 * pair + 1, 0].astype(f32) + kr_ref[2 * pair + 1, 1].astype(f32)
        dq = jnp.where(left, a, pltpu.roll(b, 64, 1))
        dk = jnp.where(left, e, pltpu.roll(f, 64, 1))
        dqkv[:, 128 * pair : 128 * pair + 128] = turn(dq, co, s1, s2).astype(bf16)
        dqkv[:, 512 + 128 * pair : 640 + 128 * pair] = turn(dk, co, s1, s2).astype(bf16)
        dqkv[:, 1024 + 128 * pair : 1152 + 128 * pair] = jnp.where(
            left, pltpu.roll(e, 64, 1), f
        ).astype(bf16)
        ctx.append(jnp.where(left, pltpu.roll(a, 64, 1), b).astype(bf16))
    ctx = jnp.concatenate(ctx, axis=1)
    r.hid[...] = ctx
    hi, lo = split(dot_tn(dy, ctx))
    hi, lo = hi.reshape(4, 4, 2, 16, 512), lo.reshape(4, 4, 2, 16, 512)
    for b in range(4):
        lanes = slice(128 * b, 128 * b + 128)
        ga[:, :, :, b, 48:64] = hi[..., lanes]
        ga[:, :, :, b, 64:80] = lo[..., lanes]
    for i in range(4):
        part = dqkv[:, 384 * i : 384 * i + 384]
        g = dot_tn(part, hidden).astype(bf16).reshape(4, 2, 48, 512)
        for b in range(4):
            ga[i, :, :, b, 0:48] = g[..., 128 * b : 128 * b + 128]
    chip = send(ga.at[:, :, 1 - s, :, att], rcm.at[:, :, :, att], r.m_s.at[1], r.m_r.at[1], other_core())
    r.out[...] = (r.res[...] + dot(rolled(r.hid, x), wide(w1, 12, 4))).astype(bf16)
    dh = r.dh[...]
    for third in range(3):
        part = dqkv[:, 512 * third : 512 * third + 512]
        dh = dh + dot_nt(part, wide(w1, 4 * third, 4))
        v0[2 + third : 3 + third, :] = jnp.sum(part.astype(f32), axis=0, keepdims=True)
    dh = unroll(dh, r.wide_f, x)
    scaled = dh * r.gain[...]
    dyf = dy.astype(f32)
    r.gt[...] = dyf + inv * (
        scaled
        - jnp.mean(scaled, axis=1, keepdims=True)
        - normed * jnp.mean(scaled * normed, axis=1, keepdims=True)
    )
    dsum = jnp.sum(dyf, axis=0, keepdims=True)
    v0[0:1, :] = jnp.sum(dh * normed, axis=0, keepdims=True)
    v0[1:2, :] = jnp.sum(dh, axis=0, keepdims=True)
    v0[5:6, :] = dsum
    v0[10:11, :] = dsum
    v0[11:16, :] = jnp.zeros((5, 512), f32)
    chip.wait()
    vcp = [send(v0, v1, vs.at[0], vr.at[0], other_core())]

    def add(i):
        a, b = i // 4, i % 4
        both = ga[a, b, s, :, 0:80].astype(f32) + rcm[a, b, :, 0:80].astype(f32)
        hi, lo = split(both[:, 48:64] + both[:, 64:80])
        hbuf[a, b, :, 0:48] = both[:, 0:48].astype(bf16)
        hbuf[a, b, :, 48:64] = hi
        hbuf[a, b, :, 64:80] = lo

    loop(0, 16, add)
    sums = Reduce(hbuf, ATT_PARTS, r.att_bufs, r.as_, r.ar)
    sums.begin(0)
    mt = momenta(r)

    def vec_stage(k, buf, axis):
        for cp in vcp:
            cp.wait()
        vcp.clear()
        if k == 0:
            v = v0[...] + v1[...]
        else:
            last = (vy, vz)[k - 1]
            v = (last[0] + last[1]) + (last[2] + last[3])
        place = {"y": y, "z": z, "x": x}[axis]
        buf[place] = v
        for d in (1, 2, 3):
            vcp.append(
                send(buf.at[place], buf.at[place], vs.at[3 * k + d], vr.at[3 * k + d], moved(axis, d))
            )

    sums.end(0)
    sums.begin(1)
    vec_stage(0, vy, "y")
    sums.end(1)
    sums.begin(2)
    vec_stage(1, vz, "z")
    g = sums.end(2)
    gx[0:32, :] = g[0]
    gx[32:48, :] = g[1]
    gx[48:64, :] = g[2]
    grad = gx[...]
    u = (1.0 + MU) * grad + (MU * MU) * mt
    ub = u.astype(bf16)
    hi, lo = split(u[48:64])
    us[0, 0:48] = ub[0:48]
    us[0, 48:64] = jnp.zeros((16, 128), bf16)
    us[1, 0:16] = hi
    us[1, 16:32] = lo
    us[1, 32:64] = jnp.zeros((32, 128), bf16)
    us[2] = ub[64:128]
    us[3] = ub[128:192]
    cps = []
    for d in (1, 2, 3):
        cps.append(send(us.at[(x + d) % 4], ur.at[x], xs.at[d - 1], xr.at[d - 1], moved("x", d)))
    vec_stage(2, vx, "x")
    ur[x] = us[x]
    r.gxa[y, z, s] = grad.astype(bf16)
    for cp in cps:
        cp.wait()
    for k in range(4):
        piece = ur[k]

        @pl.when(x != 3)
        def _(k=k, piece=piece):
            ua[:, y, z, s, :, 128 * k : 128 * k + 128] = piece.reshape(4, 16, 128)

        @pl.when(x == 3)
        def _(k=k, piece=piece):
            for b in range(4):
                ua[k, y, z, s, :, 128 * b : 128 * b + 128] = piece[16 * b : 16 * b + 16]

    gather = Gather(
        [
            (lambda a, b, e: ua.at[pl.ds(0, 2), a, b, e], True),
            (lambda a, b, e: ua.at[pl.ds(2, 2), a, b, e], False),
        ],
        r.sc, r.rc,
    )
    gather.begin()
    for cp in vcp:
        cp.wait()
    r.vec[...] = (vx[0] + vx[1]) + (vx[2] + vx[3])
    gather.turn()
    gather.pass_on()
    gather.end()


def dot3(a, b):
    (ah, al), (bh, bl) = a, b
    return dot(ah, bh) + (dot(ah, bl) + dot(al, bh))


def newton_phase(r):
    y, z, s, x = coords()
    ua, ga, oa, a_ref = r.w3, r.gxa, r.oa, r.a
    ah, al, ph, pl_, th, tl, uh, ul = r.ah, r.al, r.ph, r.pl, r.th, r.tl, r.uh, r.ul
    os, rows, xs, xr = r.os, r.rows, r.os_s, r.os_r
    grads = Gather(
        [
            (lambda a, b, e: ga.at[a, b, e, pl.ds(0, 96)], True),
            (lambda a, b, e: ga.at[a, b, e, pl.ds(96, 96)], False),
        ],
        r.sd, r.rd,
    )
    grads.begin()

    def load(hi, lo):
        return hi[...], lo[...]

    def store(hi, lo, v):
        h, l = split(v)
        hi[...] = h
        lo[...] = l

    @pl.when(x == 1)
    def _():
        uh[...] = ua[0].reshape(512, 512)
        ul[...] = ua[1].reshape(512, 512)
        h, l = uh[...], ul[...]
        a_ref[...] = dot_tn(h, h) + (dot_tn(h, l) + dot_tn(l, h))

    @pl.when(x != 1)
    def _():
        u = ua[...].reshape(2048, 512)
        a_ref[...] = dot_tn(u, u)

    row = lax.broadcasted_iota(jnp.int32, (512, 512), 0)
    col = lax.broadcasted_iota(jnp.int32, (512, 512), 1)
    eye = row == col
    a = a_ref[...]
    square = jnp.sum(jnp.sum(jnp.where(eye, a, 0.0), axis=0, keepdims=True), axis=1, keepdims=True)
    scale = 1.0 / (jnp.sqrt(square) + 1e-07)
    a_ref[...] = a * (scale * scale)
    mine = ua[:, y, z, s].reshape(64, 512).astype(f32) * scale

    def poly():
        store(ah, al, a_ref[...])
        sq = dot3(load(ah, al), load(ah, al))
        return C2 * a_ref[...] + C3 * sq + jnp.where(eye, C1, 0.0)

    def step(_, mine):
        store(ph, pl_, poly())
        pair = load(ph, pl_)
        store(th, tl, dot3(pair, load(ah, al)))
        a_ref[...] = dot3(pair, load(th, tl))
        return dot3(split(mine), pair)

    mine = lax.fori_loop(0, 2, step, mine)
    grads.turn()
    mine = lax.fori_loop(2, NS_ITERS - 1, step, mine)
    grads.pass_on()
    store(ph, pl_, poly())
    mine = dot3(split(mine), load(ph, pl_))
    side = jnp.where(x == 0, math.sqrt(1536.0), jnp.where(x == 1, math.sqrt(512.0), math.sqrt(2048.0)))
    mine = mine * (0.2 * side)
    mine = jnp.concatenate(
        [jnp.where(x == 1, mine[0:16] + mine[16:32], mine[0:16]), mine[16:64]], axis=0
    ).astype(bf16)
    for k in range(4):
        by_lanes = mine[:, 128 * k : 128 * k + 128]
        by_rows = jnp.concatenate(
            [mine[16 * k : 16 * k + 16, 128 * b : 128 * b + 128] for b in range(4)], axis=0
        )
        os[k] = jnp.where(x == 3, by_rows, by_lanes)
    cps = []
    for d in (1, 2, 3):
        cps.append(send(os.at[(x + d) % 4], rows.at[x], xs.at[d - 1], xr.at[d - 1], moved("x", d)))
    rows[x] = os[x]
    grads.end()
    for cp in cps:
        cp.wait()
    oa[y, z, s, 0:48] = rows[0, 0:48]
    oa[y, z, s, 48:64] = rows[1, 0:16]
    oa[y, z, s, 64:128] = rows[2]
    oa[y, z, s, 128:192] = rows[3]
    update = Gather(
        [
            (lambda a, b, e: oa.at[a, b, e, pl.ds(0, 96)], True),
            (lambda a, b, e: oa.at[a, b, e, pl.ds(96, 96)], False),
        ],
        r.se, r.re,
    )
    update.begin()
    update.turn()
    update.pass_on()
    update.end()


def scratch_list():
    V = pltpu.VMEM
    piece = (HEADS, TOK, 128)
    out = [
        ("fq", V((128, 1536), f32)), ("fo", V((128, 512), f32)),
        ("fi", V((128, 2048), f32)), ("ff", V((512, 512), f32)),
        ("x", V((TOK, D), bf16)), ("dy", V((TOK, D), bf16)),
        ("w1", V((4, 4, 4, 2, 64, 128), bf16)), ("w2", V((4, 4, 4, 2, 64, 128), bf16)),
        ("w3", V((4, 4, 4, 2, 16, 512), bf16)),
        ("kvs", V(piece, bf16)), ("qds", V(piece, bf16)),
        ("kv", V((GROUP, 128), bf16)), ("qd", V((NQB, QB, 128), bf16)),
        ("hid", V((TOK, D), bf16)), ("wide_f", V((TOK, D), f32)),
        ("co", V((TOK, 128), f32)), ("s1", V((TOK, 128), f32)), ("s2", V((TOK, 128), f32)),
        ("res", V((TOK, D), f32)), ("dh", V((TOK, D), f32)),
        ("gm", V((4, 4, 2, 4, 128, 128), bf16)),
        ("rcm", V((4, 4, 4, 128, 128), bf16)), ("hbuf", V((4, 4, 4, 128, 128), bf16)),
        ("kvt", V((128, GROUP), bf16)), ("acc", V((GROUP, 128), f32)),
        ("s_sc", V((GROUP, QB), f32)), ("p_sc", V((GROUP, QB), f32)),
        ("m_sc", V((GROUP // HB, 8, QB), f32)), ("cqs", V((NQB, QB, 128), bf16)),
        ("half", V((16, TOK, 128), bf16)), ("other", V((16, TOK, 128), bf16)),
        ("both", V((16, TOK, 128), bf16)),
        ("cq", V(piece, bf16)), ("kr", V((HEADS, 2, TOK, 128), bf16)),
        ("dqkv", V((TOK, 1536), bf16)),
        ("mwin", V((128, 512), f32)), ("mtr", V((512, 128), f32)), ("mfin", V((16, 512), f32)),
        ("gx", V((192, 128), f32)),
        ("us", V((4, 64, 128), bf16)), ("ur", V((4, 64, 128), bf16)),
        ("os", V((4, 64, 128), bf16)), ("rows", V((4, 64, 128), bf16)),
        ("v0", V((16, 512), f32)), ("v1", V((16, 512), f32)),
        ("vy", V((4, 16, 512), f32)), ("vz", V((4, 16, 512), f32)), ("vx", V((4, 16, 512), f32)),
        ("a", V((512, 512), f32)),
    ]
    out += [(k, V((512, 512), bf16)) for k in ("ah", "al", "ph", "pl", "th", "tl", "uh", "ul")]
    for name, shape in (
        ("lsem", (6,)), ("msem", (4,)), ("xs", (3, 3)), ("xr", (3, 3)),
        ("sa", (2, 10)), ("ra", (2, 10)), ("sb", (2, 10)), ("rb", (2, 10)),
        ("sc", (2, 10)), ("rc", (2, 10)), ("sd", (2, 10)), ("rd", (2, 10)),
        ("se", (2, 10)), ("re", (2, 10)),
        ("own_sem", None), ("ks", (16,)), ("kvr", (16,)), ("qs", (24,)), ("qr", None),
        ("cs", (16,)), ("cr", (16,)),
        ("m_s", (2,)), ("m_r", (2,)), ("ms", (3, 3, 3)), ("mr", (3, 3, 3)),
        ("as_", (3, 3, 3)), ("ar", (3, 3, 3)),
        ("ws", (3,)), ("wr", (3,)), ("bs", (16,)), ("br", None), ("rqs", (NQB, 4)), ("rqr", None),
        ("vs", (10,)), ("vr", (10,)), ("us_s", (3,)), ("us_r", (3,)), ("os_s", (3,)), ("os_r", (3,)),
    ):
        out.append((name, DMA if shape is None else DMA(shape)))
    out += [(f"mlp{i}", v) for i, v in enumerate(Reduce.scratch(MLP_PARTS))]
    out += [(f"att{i}", v) for i, v in enumerate(Reduce.scratch(ATT_PARTS))]
    return out


INPUTS = (
    "starts", "x_in", "dy_in", "gain", "shift", "bias", "wq", "wo", "wi", "wf", "mq", "mo", "mi", "mf",
)
OUTPUTS = ("out", "gt", "gxa", "oa", "vec")


def step_kernel(names, *refs):
    r = types.SimpleNamespace(**dict(zip(names, refs)))
    r.mlp_bufs = [getattr(r, f"mlp{i}") for i in range(5 * len(MLP_PARTS))]
    r.att_bufs = [getattr(r, f"att{i}") for i in range(5 * len(ATT_PARTS))]
    chip = front_phase(r)
    attention_phase(r, chip)
    back_phase(r)
    newton_phase(r)


def train_step(*args):
    scratch = scratch_list()
    names = INPUTS + OUTPUTS + tuple(k for k, _ in scratch)
    return pl.pallas_call(
        functools.partial(step_kernel, names),
        out_shape=tuple(
            jax.ShapeDtypeStruct(shape, t)
            for shape, t in (
                ((TOK, D), bf16), ((TOK, D), f32),
                ((4, 4, 2, 192, 128), bf16), ((4, 4, 2, 192, 128), bf16), ((16, 512), f32),
            )
        ),
        in_specs=[SM, ANY, ANY, VM, VM, VM] + [ANY] * 8,
        out_specs=(VM,) * 5,
        scratch_shapes=[v for _, v in scratch],
        compiler_params=pltpu.CompilerParams(
            vmem_limit_bytes=63 * 2**20, collective_id=1, has_side_effects=True
        ),
        name="train_step",
    )(*args)


def update_kernel(
    gx, oa, wq, wo, wi, wf, mq, mo, mi, mf, nmq, nwq, nmo, nwo, nmi, nwi, nmf, nwf
):
    for lo, n, w, m, nm, nw in (
        (0, 48, wq, mq, nmq, nwq),
        (48, 16, wo, mo, nmo, nwo),
        (64, 64, wi, mi, nmi, nwi),
    ):
        grad = gx[:, lo : lo + n, :].astype(f32).reshape(8 * n, 128).T
        turned = oa[:, lo : lo + n, :].astype(f32).reshape(8 * n, 128).T
        nm[...] = MU * m[...] + grad
        nw[...] = (1.0 - LR * WD) * w[...] - LR * turned
    for b in range(4):
        cols = slice(128 * b, 128 * b + 128)
        rows = slice(128 + 16 * b, 144 + 16 * b)
        grad = gx[:, rows, :].astype(f32).reshape(128, 128)
        turned = oa[:, rows, :].astype(f32).reshape(128, 128)
        nmf[:, cols] = MU * mf[:, cols] + grad
        nwf[:, cols] = (1.0 - LR * WD) * wf[:, cols] - LR * turned


def update(gx, oa, weights, moments):
    piece = pl.BlockSpec((8, 192, 128), lambda i: (i, 0, 0))
    blocks = [
        pl.BlockSpec((128, 384), lambda i: (0, i)),
        pl.BlockSpec((128, 128), lambda i: (0, i)),
        pl.BlockSpec((128, 512), lambda i: (0, i)),
        pl.BlockSpec((128, 512), lambda i: (i, 0)),
    ]
    outs, specs = [], []
    for w, b in zip(weights, blocks):
        outs += [jax.ShapeDtypeStruct(w.shape, f32)] * 2
        specs += [b, b]
    return pl.pallas_call(
        update_kernel,
        grid=(4,),
        out_shape=tuple(outs),
        in_specs=[piece, piece] + blocks + blocks,
        out_specs=tuple(specs),
        compiler_params=pltpu.CompilerParams(vmem_limit_bytes=60 * 2**20),
        name="update_weights",
    )(gx, oa, *weights, *moments)


def body(
    tokens, cotangent, ln_gain, ln_bias, biases, w_qkv, w_out, w_in, w_fin,
    mom_qkv, mom_out, mom_in, mom_fin, vec_mom, starts,
):
    weights = (w_qkv, w_out, w_in, w_fin)
    moments = (mom_qkv, mom_out, mom_in, mom_fin)
    block_out, grad_tokens, gx, oa, vec_sum = train_step(
        starts, tokens, cotangent, ln_gain[None, :], ln_bias[None, :], biases[None, :],
        *weights, *moments,
    )
    new = update(gx.reshape(32, 192, 128), oa.reshape(32, 192, 128), weights, moments)
    vec_moment = VMU * vec_mom + vec_sum.reshape(-1)[:5632]
    vec_new = jnp.concatenate([ln_gain, ln_bias, biases]) - VLR * vec_moment
    return (block_out, grad_tokens, *new, vec_moment, vec_new)


def solution(mesh):
    tok = P(("wsh", "ctx"), None)
    row = P("wsh", None)
    return jax.shard_map(
        body,
        mesh=mesh,
        in_specs=(tok, tok, P(), P(), P()) + (row,) * 8 + (P(), P()),
        out_specs=(tok, tok) + (row,) * 8 + (P(), P()),
        check_vma=False,
    )
```

```python
import functools
import math
import types

import jax
import jax.numpy as jnp
from jax import lax
from jax.experimental import pallas as pl
from jax.experimental.pallas import tpu as pltpu
from jax.sharding import PartitionSpec as P

f32 = jnp.float32
bf16 = jnp.bfloat16
MESH = pl.DeviceIdType.MESH
HEADS = 8
HD = 64
ROT = 16
D = 512
TOK = 192
GROUP = 6144
QB = 256
NQB = 6
HB = 128
UU = 8
TT = 4
NS_ITERS = 5
C1, C2, C3 = 3.4445, -4.775, 2.0315
MU, LR, WD = 0.95, 0.6, 0.01
VMU, VLR = 0.9, 0.0005
R_QKV, R_OUT, R_IN, R_FIN = 48, 16, 64, 64

VM = pl.BlockSpec(memory_space=pltpu.VMEM)
SM = pl.BlockSpec(memory_space=pltpu.SMEM)
ANY = pl.BlockSpec(memory_space=pl.ANY)
DMA = pltpu.SemaphoreType.DMA


def dot(a, b):
    return jnp.dot(a, b, preferred_element_type=f32)


def dot_nt(a, b):
    return lax.dot_general(a, b, (((1,), (1,)), ((), ())), preferred_element_type=f32)


def dot_tn(a, b):
    return lax.dot_general(a, b, (((0,), (0,)), ((), ())), preferred_element_type=f32)


def coords():
    c = lax.axis_index("ctx")
    return c // 8, (c // 2) % 4, c % 2, lax.axis_index("wsh")


def at(y, z, s, x):
    return {"ctx": (y * 4 + z) * 2 + s, "wsh": x}


def tell(partners):
    sem = pltpu.get_barrier_semaphore()
    for p in partners:
        pl.semaphore_signal(sem, inc=1, device_id=p, device_id_type=MESH)


def tell_slab():
    c = lax.axis_index("ctx")
    sem = pltpu.get_barrier_semaphore()

    def one(d, _):
        pl.semaphore_signal(
            sem, inc=1, device_id={"ctx": lax.rem(c + d, 32)}, device_id_type=MESH
        )
        return 0

    lax.fori_loop(1, 32, one, 0)


def met(count):
    pl.semaphore_wait(pltpu.get_barrier_semaphore(), count)


def wait_for(ref, sem):
    pltpu.make_async_copy(ref, ref, sem).wait()


def loop(lo, hi, f):
    def step(i, _):
        f(i)
        return 0

    lax.fori_loop(lo, hi, step, 0)


AXES = ("y", "z", "x")


def moved(axis, d):
    y, z, s, x = coords()
    if axis == "y":
        return at((y + d) % 4, z, s, x)
    if axis == "z":
        return at(y, (z + d) % 4, s, x)
    return at(y, z, s, (x + d) % 4)


def other_core():
    y, z, s, x = coords()
    return at(y, z, 1 - s, x)


def lines(axes=AXES):
    return [moved(a, d) for a in axes for d in (1, 2, 3)]


def send(src, dst, ss, rs, dev):
    cp = pltpu.make_async_remote_copy(
        src_ref=src, dst_ref=dst, send_sem=ss, recv_sem=rs, device_id=dev, device_id_type=MESH
    )
    cp.start()
    return cp


ALL = slice(None)


class Gather:
    def __init__(self, items, ss, rs):
        self.items, self.ss, self.rs = items, ss, rs

    def begin(self):
        y, z, s, x = coords()
        self.first = []
        for i, (get, y_first) in enumerate(self.items):
            piece = get(y, z, s)
            for d in (1, 2, 3):
                to = moved("y" if y_first else "z", d)
                self.first.append(
                    send(piece, piece, self.ss.at[i, d - 1], self.rs.at[i, d - 1], to)
                )

    def turn(self):
        y, z, s, x = coords()
        for cp in self.first:
            cp.wait()
        self.second, self.across = {}, []
        for i, (get, y_first) in enumerate(self.items):
            piece = get(ALL, z, s) if y_first else get(y, ALL, s)
            for d in (1, 2, 3):
                to = moved("z" if y_first else "y", d)
                self.second[i, d] = send(
                    piece, piece, self.ss.at[i, d + 2], self.rs.at[i, d + 2], to
                )
        for i, (get, y_first) in enumerate(self.items):
            piece = get(ALL, z, s) if y_first else get(y, ALL, s)
            self.across.append(
                send(piece, piece, self.ss.at[i, 6], self.rs.at[i, 6], other_core())
            )

    def pass_on(self):
        y, z, s, x = coords()
        for d in (1, 3, 2):
            for i, (get, y_first) in enumerate(self.items):
                self.second[i, d].wait_recv()
                piece = get(ALL, (z - d) % 4, s) if y_first else get((y - d) % 4, ALL, s)
                self.across.append(
                    send(piece, piece, self.ss.at[i, 6 + d], self.rs.at[i, 6 + d], other_core())
                )

    def end(self):
        for cp in self.second.values():
            cp.wait_send()
        for cp in self.across:
            cp.wait()

    @staticmethod
    def sems(n):
        return [DMA((n, 10)), DMA((n, 10))]


def split(v):
    hi = v.astype(bf16)
    return hi, (v - hi.astype(f32)).astype(bf16)


class Reduce:
    def __init__(self, src, parts, bufs, ss, rs):
        self.src, self.parts, self.ss, self.rs = src, parts, ss, rs
        y, z, s, x = coords()
        self.me = {"y": y, "z": z, "x": x}
        self.bufs = [bufs[5 * i : 5 * i + 5] for i in range(len(parts))]

    @staticmethod
    def scratch(parts):
        out = []
        for lo, n, order, paired in parts:
            out += [
                pltpu.VMEM((3, 4, 4, n, 128), bf16),
                pltpu.VMEM((4, 4, n, 128), bf16),
                pltpu.VMEM((3, 4, n, 128), bf16),
                pltpu.VMEM((4, n, 128), bf16),
                pltpu.VMEM((3, n, 128), bf16),
            ]
        return out

    @staticmethod
    def sems(parts):
        return [DMA((3, len(parts), 3)), DMA((3, len(parts), 3))]

    @staticmethod
    def summed(pieces, paired):
        v = functools.reduce(lambda a, b: a + b, [p.astype(f32) for p in pieces])
        if not paired:
            return v.astype(bf16)
        half = v.shape[-2] // 2
        return jnp.concatenate(split(v[..., :half, :] + v[..., half:, :]), axis=-2)

    def begin(self, stage):
        self.cps = []
        for d in (2, 1, 3):
            for i, (lo, n, order, paired) in enumerate(self.parts):
                r1, h1, r2, h2, r3 = self.bufs[i]
                axis = order[stage]
                place = (self.me[axis] + d) % 4
                left = [a for a in AXES if a not in order[:stage]]
                index = tuple(place if a == axis else ALL for a in left)
                if stage == 0:
                    src = self.src.at[index + (pl.ds(lo, n),)]
                else:
                    src = (h1, h2)[stage - 1].at[index]
                self.cps.append(
                    send(
                        src, (r1, r2, r3)[stage].at[d - 1],
                        self.ss.at[stage, i, d - 1], self.rs.at[stage, i, d - 1], moved(axis, d),
                    )
                )

    def end(self, stage):
        for cp in self.cps:
            cp.wait()
        out = []
        for i, (lo, n, order, paired) in enumerate(self.parts):
            r1, h1, r2, h2, r3 = self.bufs[i]
            mine = self.me[order[stage]]
            if stage == 0:
                axis = AXES.index(order[0])

                def add(a, _, axis=axis, mine=mine, lo=lo, n=n, paired=paired, r1=r1, h1=h1):
                    index = [a, ALL]
                    index.insert(axis, mine)
                    own = self.src[tuple(index) + (slice(lo, lo + n),)]
                    h1[a] = self.summed([own, r1[0, a], r1[1, a], r1[2, a]], paired)
                    return 0

                lax.fori_loop(0, 4, add, 0)
            elif stage == 1:
                left = [a for a in AXES if a != order[0]]
                first = left.index(order[1]) == 0
                own = h1[mine] if first else h1[:, mine]
                h2[...] = self.summed([own, r2[0], r2[1], r2[2]], paired)
            else:
                v = h2[mine].astype(f32) + r3[0].astype(f32) + r3[1].astype(f32) + r3[2].astype(f32)
                if paired:
                    v = v[: n // 2] + v[n // 2 :]
                out.append(v)
        return out


MLP_PARTS = ((0, 48, ("y", "z", "x"), False), (48, 48, ("z", "x", "y"), False), (96, 32, ("x", "y", "z"), False))
ATT_PARTS = ((0, 32, ("y", "z", "x"), False), (32, 16, ("z", "x", "y"), False), (48, 32, ("x", "y", "z"), True))


def norm_parts(x_ref, gain, shift):
    xf = x_ref[...].astype(f32)
    centered = xf - jnp.mean(xf, axis=1, keepdims=True)
    inv = lax.rsqrt(jnp.mean(centered * centered, axis=1, keepdims=True) + 1e-05)
    normed = centered * inv
    hidden = (normed * gain + shift).astype(bf16)
    return xf, inv, normed, hidden


def turn(v, co, s1, s2):
    return v * co + pltpu.roll(v, 120, 1) * s1 + pltpu.roll(v, 8, 1) * s2


def rolled(ref, x):
    parts = [ref[:, pl.ds(pl.multiple_of((x + d) % 4 * 128, 128), 128)] for d in range(4)]
    return jnp.concatenate(parts, axis=1)


def unroll(v, ref, x):
    for d in range(4):
        ref[:, pl.ds(pl.multiple_of((x + d) % 4 * 128, 128), 128)] = v[:, 128 * d : 128 * d + 128]
    return ref[...]


def rotary(starts_ref, x, c):
    bnd = starts_ref[x] - x * GROUP
    place = c * TOK + lax.broadcasted_iota(jnp.int32, (TOK, 128), 0)
    pos = (place - jnp.where(place >= bnd, bnd, 0)).astype(f32)
    lane = lax.broadcasted_iota(jnp.int32, (TOK, 128), 1) % HD
    freq = jnp.zeros((TOK, 128), f32)
    for i in range(ROT // 2):
        freq = jnp.where(lane % 8 == i, 10000.0 ** (-2.0 * i / ROT), freq)
    angle = pos * jnp.where(lane < ROT, freq, 0.0)
    co, si = jnp.cos(angle), jnp.sin(angle)
    return co, jnp.where(lane < 8, -si, 0.0), jnp.where(lane < 8, 0.0, si)


def wide(w, first, count):
    blocks = [w[(first + i) // 4, (first + i) % 4].reshape(512, 128) for i in range(count)]
    return jnp.concatenate(blocks, axis=1) if count > 1 else blocks[0]


def query_home(piece):
    block = piece // 4
    part = block % 8
    low = part < 4
    return jnp.where(low, part, 7 - part), 2 * (block // 8) + jnp.where(low, 0, 1), piece % 4


def query_block(t, j):
    if isinstance(t, int):
        return 8 * (t // 2) + (j if t % 2 == 0 else 7 - j)
    return 8 * (t // 2) + jnp.where(t % 2 == 0, j, 7 - j)


def front_phase(r):
    y, z, s, x = coords()
    c = lax.axis_index("ctx")
    p = c // 2
    w1, w2, w3, kvs, qds, kv, qd = r.w1, r.w2, r.w3, r.kvs, r.qds, r.kv, r.qd
    ks, kr, qs, qr, cs, cr = r.ks, r.kvr, r.qs, r.qr, r.cs, r.cr
    bias_ref = r.bias
    tell_slab()
    tell(lines(("x",)))
    loads = [
        pltpu.make_async_copy(src, dst, r.lsem.at[k])
        for k, (src, dst) in enumerate(
            ((r.wq, r.fq), (r.wo, r.fo), (r.wi, r.fi), (r.wf, r.ff), (r.x_in, r.x), (r.dy_in, r.dy))
        )
    ]
    for cp in loads:
        cp.start()
    momenta_begin(r)
    for cp in loads:
        cp.wait()
    for b in range(16):
        w = r.fq[:, 128 * b : 128 * b + 128] if b < 12 else r.fo[:, 128 * b - 1536 : 128 * b - 1408]
        w1[b // 4, b % 4, 0] = w.astype(bf16).reshape(2, 64, 128)
        w2[b // 4, b % 4, 0] = r.fi[:, 128 * b : 128 * b + 128].astype(bf16).reshape(2, 64, 128)
    w3[0] = r.ff[...].astype(bf16).reshape(4, 4, 2, 16, 512)
    met(34)
    cps = []
    for i, piece in enumerate(
        (lambda d: w1.at[y, z, d, s], lambda d: w2.at[y, z, d, s], lambda d: w3.at[d, y, z, s])
    ):
        cps.append([
            send(piece(0), piece(4 - d), r.xs.at[i, d - 1], r.xr.at[i, d - 1], moved("x", d))
            for d in (1, 2, 3)
        ])
    co, s1, s2 = rotary(r.starts, x, c)
    r.co[...], r.s1[...], r.s2[...] = co, s1, s2
    xf, inv, normed, hidden = norm_parts(r.x, r.gain[...], r.shift[...])
    r.hid[...] = hidden
    hidden_r = rolled(r.hid, x)
    dy = r.dy[...]
    for cp in cps[0]:
        cp.wait()
    others = pl.ds(1, 3)
    early = Gather(
        [
            (lambda a, b, e: w1.at[a, b, others, e, pl.ds(0, 32)], True),
            (lambda a, b, e: w1.at[a, b, others, e, pl.ds(32, 32)], False),
        ],
        r.sa, r.ra,
    )
    late = Gather(
        [
            (lambda a, b, e: w2.at[a, b, others, e], True),
            (lambda a, b, e: w3.at[others, a, b, e], False),
        ],
        r.sb, r.rb,
    )
    early.begin()
    early.turn()
    early.pass_on()
    for cp in cps[1] + cps[2]:
        cp.wait()
    late.begin()
    early.end()
    left = lax.broadcasted_iota(jnp.int32, (TOK, 128), 1) < 64
    dctx = unroll(dot_nt(dy, wide(w1, 12, 4)), r.wide_f, x)
    for half in range(2):
        if half == 1:
            late.turn()
        thirds = []
        for third in range(3):
            b = third * 4 + 2 * half
            thirds.append(dot(hidden_r, wide(w1, b, 2)) + bias_ref[b * 128 : b * 128 + 256][None, :])
        for e in range(2):
            lanes = slice(128 * e, 128 * e + 128)
            q = turn(thirds[0][:, lanes], co, s1, s2).astype(bf16).astype(f32) * 0.125
            k = turn(thirds[1][:, lanes], co, s1, s2)
            v = thirds[2][:, lanes]
            pair = 2 * half + e
            g = dctx[:, pair * 128 : pair * 128 + 128]
            h = 2 * pair
            kvs[h] = jnp.where(left, k, pltpu.roll(v, 64, 1)).astype(bf16)
            kvs[h + 1] = jnp.where(left, pltpu.roll(k, 64, 1), v).astype(bf16)
            qds[h] = jnp.where(left, q, pltpu.roll(g, 64, 1)).astype(bf16)
            qds[h + 1] = jnp.where(left, pltpu.roll(q, 64, 1), g).astype(bf16)

    def kv_copy(d):
        to = lax.rem(p + d, 16)
        return pltpu.make_async_remote_copy(
            src_ref=kvs.at[to // 2], dst_ref=kv.at[pl.ds(c * TOK, TOK)], send_sem=ks, recv_sem=kr,
            device_id={"ctx": to * 2 + s}, device_id_type=MESH,
        )

    def across(d):
        block = kv.at[pl.ds((lax.rem(p + 16 - d, 16) * 2 + s) * TOK, TOK)]
        return pltpu.make_async_remote_copy(
            src_ref=block, dst_ref=block, send_sem=cs, recv_sem=cr,
            device_id={"ctx": p * 2 + 1 - s}, device_id_type=MESH,
        )

    def each_query(k, what):
        h, i = k // 3, k % 3
        j, t, quarter = query_home(3 * c + i)
        to = 4 * h + j
        src = qds.at[h, pl.ds(64 * i, 64)]
        dst = qd.at[t, pl.ds(64 * quarter, 64)]

        @pl.when(to == c)
        def _():
            if what == "start":
                pltpu.make_async_copy(src, dst, qr).start()

        @pl.when(to != c)
        def _():
            cp = pltpu.make_async_remote_copy(
                src_ref=src, dst_ref=dst, send_sem=qs.at[k], recv_sem=qr,
                device_id={"ctx": to}, device_id_type=MESH,
            )
            if what == "start":
                cp.start()
            else:
                cp.wait_send()

    own = pltpu.make_async_copy(kvs.at[p // 2], kv.at[pl.ds(c * TOK, TOK)], r.own_sem)
    own.start()
    loop(1, 16, lambda d: kv_copy(d).start())
    loop(0, 24, lambda k: each_query(k, "start"))
    own.wait()

    r.acc[...] = jnp.zeros_like(r.acc)
    late.pass_on()
    late.end()
    root = math.sqrt(2.0 / math.pi)
    mlp = jnp.zeros((TOK, D), f32)
    dh = jnp.zeros((TOK, D), f32)
    for i in range(4):
        if i == 2:
            wait_for(kv.at[pl.ds(0, 15 * TOK)], kr)
            loop(0, 16, lambda d: across(d).start())
        w_in = wide(w2, 4 * i, 4)
        w_fin = w3[(i + 4 - x) % 4].reshape(512, 512)
        pre = dot(hidden_r, w_in) + bias_ref[2048 + 512 * i : 2560 + 512 * i][None, :]
        sq = pre * pre
        th = jnp.tanh(root * (pre + 0.044715 * (pre * sq)))
        act = (0.5 * pre * (1.0 + th)).astype(bf16)
        slope = 0.5 * (1.0 + th) + (0.5 * root) * pre * (1.0 - th * th) * (
            1.0 + (3.0 * 0.044715) * sq
        )
        dpre = (dot_nt(dy, w_fin) * slope).astype(bf16)
        mlp = mlp + dot(act, w_fin)
        dh = dh + dot_nt(dpre, w_in)
        r.v0[6 + i : 7 + i, :] = jnp.sum(dpre.astype(f32), axis=0, keepdims=True)
        g_in = dot_tn(dpre, hidden).astype(bf16).reshape(4, 2, 64, 512)
        g_fin = dot_tn(act, dy).astype(bf16).reshape(4, 4, 2, 16, 512)
        for b in range(4):
            lanes = slice(128 * b, 128 * b + 128)
            r.gm[i, :, :, b, 0:64] = g_in[..., lanes]
            r.gm[:, :, :, i, 64 + 16 * b : 80 + 16 * b] = g_fin[..., lanes]
    r.res[...] = xf + mlp + (bias_ref[4096:4608] + bias_ref[1536:2048])[None, :]
    r.dh[...] = dh
    chip = send(r.gm.at[:, :, 1 - s], r.rcm, r.m_s.at[0], r.m_r.at[0], other_core())
    wait_for(kv.at[pl.ds(0, 15 * TOK)], ks)
    loop(0, 24, lambda k: each_query(k, "wait"))
    wait_for(qd, qr)
    wait_for(kv.at[pl.ds(0, 16 * TOK)], cs)
    wait_for(kv.at[pl.ds(0, 16 * TOK)], cr)
    return chip


RETURNS = ((11, 16), (6, 11), (0, 6))


def attention_phase(r, chip):
    kvt, acc, s_sc, p_sc, m_sc, cqs = r.kvt, r.acc, r.s_sc, r.p_sc, r.m_sc, r.cqs
    half, other, both, rcm, hbuf = r.half, r.other, r.both, r.rcm, r.hbuf
    cq, kr, kv_ref, qd_ref, gm_ref = r.cq, r.kr, r.kv, r.qd, r.gm
    ws, wr, ss, sr, qs, qr = r.ws, r.wr, r.bs, r.br, r.rqs, r.rqr
    y, z, s, x = coords()
    c = lax.axis_index("ctx")
    p = c // 2
    h = c // 4
    j = c % 4
    n = kv_ref.shape[0]
    bnd = r.starts[x] - x * GROUP

    def prepare(i, _):
        o = pl.multiple_of(i * QB, QB)
        kvt[:, pl.ds(o, QB)] = kv_ref[pl.ds(o, QB), :].T
        return 0

    lax.fori_loop(0, n // QB, prepare, 0)
    lane = lax.broadcasted_iota(jnp.int32, (QB, 128), 1)

    def block(t):
        qb = query_block(t, j)
        qd = qd_ref[t]
        w1 = jnp.where(lane < 64, qd, jnp.zeros_like(qd))
        w2 = jnp.where(lane < 64, jnp.zeros_like(qd), qd)
        q_t = w1.T
        d_t = w2.T

        def scores(kt, masked, carry, tiles, first=False):
            m8, l8, r8 = carry
            for u in range(2 * tiles):
                o = pl.multiple_of(kt * QB + u * HB, HB)
                rows = kv_ref[pl.ds(o, HB), :]
                s = dot(rows, q_t)
                if masked and not (first and u > 1):
                    kp = o + lax.broadcasted_iota(jnp.int32, (HB, QB), 0)
                    qp = qb * QB + lax.broadcasted_iota(jnp.int32, (HB, QB), 1)
                    s = jnp.where((kp <= qp) & ((kp >= bnd) == (qp >= bnd)), s, -1e30)
                s = s.reshape(HB // 8, 8, QB)
                dp = dot(rows, d_t)
                p_sc[pl.ds(o, HB), :] = dp
                mn = jnp.maximum(m8, jnp.max(s, axis=0))
                e = jnp.exp(s - mn[None])
                s_sc[pl.ds(o, HB), :] = e.reshape(HB, QB)
                m_sc[2 * kt + u] = mn
                al = jnp.exp(m8 - mn)
                l8 = l8 * al + jnp.sum(e, axis=0)
                r8 = r8 * al + jnp.sum(e * dp.reshape(HB // 8, 8, QB), axis=0)
                m8 = mn
            return m8, l8, r8

        zero = jnp.zeros((8, QB), f32)
        base = t // 2 * 8
        tail = (qb - base) // TT + 1
        carry = lax.fori_loop(
            0, tail, lambda g, c: scores(base + TT * g, True, c, TT),
            (jnp.full((8, QB), -1e30, f32), zero, zero),
        )
        if base > 0:
            carry = scores(0, True, carry, UU, True)
        carry = lax.fori_loop(
            1, base // UU, lambda g, c: scores(g * UU, False, c, UU), carry
        )
        m8, l8, r8 = carry
        m = jnp.max(m8, axis=0, keepdims=True)
        w = jnp.exp(m8 - m)
        l = jnp.sum(l8 * w, axis=0, keepdims=True)
        lse = m + jnp.log(l)
        rd = jnp.sum(r8 * w, axis=0, keepdims=True) / l

        def grads(kt, carry, tiles):
            c_t, g_t = carry
            for u in range(tiles):
                o = pl.multiple_of((kt + u) * QB, QB)
                e = s_sc[pl.ds(o, QB), :].reshape(2, HB // 8, 8, QB)
                w0 = jnp.exp(m_sc[2 * (kt + u)] - lse)
                w1_ = jnp.exp(m_sc[2 * (kt + u) + 1] - lse)
                p = jnp.concatenate([e[0] * w0[None], e[1] * w1_[None]], axis=0).reshape(QB, QB)
                pb = p.astype(bf16)
                ds = (p * (p_sc[pl.ds(o, QB), :] - rd)).astype(bf16)
                c_t = c_t + dot(kvt[64:128, pl.ds(o, QB)], pb)
                g_t = g_t + dot(kvt[0:64, pl.ds(o, QB)], ds)
                acc[pl.ds(o, QB), :] += dot(ds, w1) + dot(pb, w2)
            return c_t, g_t

        z = jnp.zeros((64, QB), f32)
        c = lax.fori_loop(0, base // UU, lambda g, c: grads(g * UU, c, UU), (z, z))
        c_t, g_t = lax.fori_loop(0, tail, lambda g, c: grads(base + TT * g, c, TT), c)
        cqs[t] = jnp.concatenate([g_t * 0.125, c_t], axis=0).T.astype(bf16)

    def each_query(t, quarter, what):
        piece = 4 * query_block(t, j) + quarter
        to, i = piece // 3, piece % 3
        src = cqs.at[t, pl.ds(64 * quarter, 64)]
        dst = cq.at[h, pl.ds(64 * i, 64)]

        @pl.when(to == c)
        def _():
            if what == "start":
                pltpu.make_async_copy(src, dst, qr).start()

        @pl.when(to != c)
        def _():
            cp = pltpu.make_async_remote_copy(
                src_ref=src, dst_ref=dst, send_sem=qs.at[t, quarter], recv_sem=qr,
                device_id={"ctx": to}, device_id_type=MESH,
            )
            if what == "start":
                cp.start()
            else:
                cp.wait_send()

    def return_queries(t):
        loop(0, 4, lambda quarter: each_query(t, quarter, "start"))

    swaps = {}

    def exchange(g):
        lo, hi = RETURNS[g]

        def low(i):
            o = pl.multiple_of((2 * i + 1 - s) * TOK, TOK)
            half[i] = acc[pl.ds(o, TOK), :].astype(bf16)

        loop(lo, hi, low)
        part = pl.ds(lo, hi - lo)
        swaps[g] = send(half.at[part], other.at[part], ws.at[g], wr.at[g], other_core())

    def block_copy(i):
        return pltpu.make_async_remote_copy(
            src_ref=both.at[i], dst_ref=kr.at[h, p % 2], send_sem=ss, recv_sem=sr,
            device_id={"ctx": i * 2 + s}, device_id_type=MESH,
        )

    def push(g):
        lo, hi = RETURNS[g]
        swaps[g].wait()

        def one(i):
            o = pl.multiple_of((2 * i + s) * TOK, TOK)
            both[i] = (acc[pl.ds(o, TOK), :] + other[i].astype(f32)).astype(bf16)

            @pl.when(i == p)
            def _():
                pltpu.make_async_copy(both.at[i], kr.at[h, p % 2], sr).start()

            @pl.when(i != p)
            def _():
                block_copy(i).start()

        loop(lo, hi, one)

    def add(i):
        a, b = i // 4, i % 4
        hbuf[a, b] = (gm_ref[a, b, s].astype(f32) + rcm[a, b].astype(f32)).astype(bf16)

    chip.wait()
    loop(0, 16, add)
    sums = Reduce(hbuf, MLP_PARTS, r.mlp_bufs, r.ms, r.mr)
    sums.begin(0)
    block(5)
    return_queries(5)
    block(4)
    return_queries(4)
    exchange(0)
    block(3)
    return_queries(3)
    push(0)
    sums.end(0)
    sums.begin(1)
    block(2)
    return_queries(2)
    exchange(1)
    block(1)
    return_queries(1)
    push(1)
    block(0)
    return_queries(0)
    exchange(2)
    push(2)
    sums.end(1)
    sums.begin(2)
    wait_for(both.at[pl.ds(0, 15)], ss)
    for t in range(NQB):
        loop(0, 4, lambda quarter, t=t: each_query(t, quarter, "wait"))
    wait_for(cq, qr)
    wait_for(kr, sr)
    return sums


def momenta_starts():
    c = lax.axis_index("ctx")
    return jnp.minimum(48 * c // 128, 10), 16 * c // 128, 64 * c // 128


def momenta_loads(r):
    c = lax.axis_index("ctx")
    starts = momenta_starts()
    loads = []
    for k, (m, width) in enumerate(((r.mq, 256), (r.mo, 128), (r.mi, 128))):
        first = pl.multiple_of(starts[k] * 128, 128)
        loads.append(
            pltpu.make_async_copy(
                m.at[:, pl.ds(first, width)],
                r.mwin.at[:, pl.ds((0, 256, 384)[k], width)],
                r.msem.at[k],
            )
        )
    loads.append(pltpu.make_async_copy(r.mf.at[pl.ds(16 * c, 16)], r.mfin, r.msem.at[3]))
    return loads


def momenta_begin(r):
    for cp in momenta_loads(r):
        cp.start()


def momenta(r):
    c = lax.axis_index("ctx")
    for cp in momenta_loads(r):
        cp.wait()
    r.mtr[...] = r.mwin[...].T
    offset = 48 * c - momenta_starts()[0] * 128
    return jnp.concatenate(
        [
            r.mtr[pl.ds(pl.multiple_of(offset, 16), 48), :],
            r.mtr[pl.ds(pl.multiple_of(256 + 16 * c % 128, 16), 16), :],
            r.mtr[pl.ds(pl.multiple_of(384 + 64 * c % 128, 64), 64), :],
        ]
        + [r.mfin[:, 128 * b : 128 * b + 128] for b in range(4)],
        axis=0,
    )


def back_phase(r, mlp_sums):
    dqkv, gx, us, ur, v0, v1, vy, vz, vx = r.dqkv, r.gx, r.us, r.ur, r.v0, r.v1, r.vy, r.vz, r.vx
    cq_ref, kr_ref, w1, ga, rcm, hbuf = r.cq, r.kr, r.w1, r.gm, r.rcm, r.hbuf
    vs, vr, xs, xr, ua = r.vs, r.vr, r.us_s, r.us_r, r.w3
    att = pl.ds(0, 80)
    y, z, s, x = coords()
    c = lax.axis_index("ctx")
    xf, inv, normed, hidden = norm_parts(r.x, r.gain[...], r.shift[...])
    dy = r.dy[...]
    co, s1, s2 = r.co[...], -r.s1[...], -r.s2[...]
    left = lax.broadcasted_iota(jnp.int32, (TOK, 128), 1) < 64
    ctx = []
    for pair in range(4):
        a = cq_ref[2 * pair].astype(f32)
        b = cq_ref[2 * pair + 1].astype(f32)
        e = kr_ref[2 * pair, 0].astype(f32) + kr_ref[2 * pair, 1].astype(f32)
        f = kr_ref[2 * pair + 1, 0].astype(f32) + kr_ref[2 * pair + 1, 1].astype(f32)
        dq = jnp.where(left, a, pltpu.roll(b, 64, 1))
        dk = jnp.where(left, e, pltpu.roll(f, 64, 1))
        dqkv[:, 128 * pair : 128 * pair + 128] = turn(dq, co, s1, s2).astype(bf16)
        dqkv[:, 512 + 128 * pair : 640 + 128 * pair] = turn(dk, co, s1, s2).astype(bf16)
        dqkv[:, 1024 + 128 * pair : 1152 + 128 * pair] = jnp.where(
            left, pltpu.roll(e, 64, 1), f
        ).astype(bf16)
        ctx.append(jnp.where(left, pltpu.roll(a, 64, 1), b).astype(bf16))
    ctx = jnp.concatenate(ctx, axis=1)
    r.hid[...] = ctx
    hi, lo = split(dot_tn(dy, ctx))
    hi, lo = hi.reshape(4, 4, 2, 16, 512), lo.reshape(4, 4, 2, 16, 512)
    for b in range(4):
        lanes = slice(128 * b, 128 * b + 128)
        ga[:, :, :, b, 48:64] = hi[..., lanes]
        ga[:, :, :, b, 64:80] = lo[..., lanes]
    for i in range(4):
        part = dqkv[:, 384 * i : 384 * i + 384]
        g = dot_tn(part, hidden).astype(bf16).reshape(4, 2, 48, 512)
        for b in range(4):
            ga[i, :, :, b, 0:48] = g[..., 128 * b : 128 * b + 128]
    chip = send(ga.at[:, :, 1 - s, :, att], rcm.at[:, :, :, att], r.m_s.at[1], r.m_r.at[1], other_core())
    r.out[...] = (r.res[...] + dot(rolled(r.hid, x), wide(w1, 12, 4))).astype(bf16)
    dh = r.dh[...]
    for third in range(3):
        part = dqkv[:, 512 * third : 512 * third + 512]
        dh = dh + dot_nt(part, wide(w1, 4 * third, 4))
        v0[2 + third : 3 + third, :] = jnp.sum(part.astype(f32), axis=0, keepdims=True)
    dh = unroll(dh, r.wide_f, x)
    scaled = dh * r.gain[...]
    dyf = dy.astype(f32)
    r.gt[...] = dyf + inv * (
        scaled
        - jnp.mean(scaled, axis=1, keepdims=True)
        - normed * jnp.mean(scaled * normed, axis=1, keepdims=True)
    )
    dsum = jnp.sum(dyf, axis=0, keepdims=True)
    v0[0:1, :] = jnp.sum(dh * normed, axis=0, keepdims=True)
    v0[1:2, :] = jnp.sum(dh, axis=0, keepdims=True)
    v0[5:6, :] = dsum
    v0[10:11, :] = dsum
    v0[11:16, :] = jnp.zeros((5, 512), f32)
    chip.wait()
    vcp = [send(v0, v1, vs.at[0], vr.at[0], other_core())]

    def add(i):
        a, b = i // 4, i % 4
        both = ga[a, b, s, :, 0:80].astype(f32) + rcm[a, b, :, 0:80].astype(f32)
        hi, lo = split(both[:, 48:64] + both[:, 64:80])
        hbuf[a, b, :, 0:48] = both[:, 0:48].astype(bf16)
        hbuf[a, b, :, 48:64] = hi
        hbuf[a, b, :, 64:80] = lo

    loop(0, 16, add)
    sums = Reduce(hbuf, ATT_PARTS, r.att_bufs, r.as_, r.ar)
    sums.begin(0)
    mt = momenta(r)

    def vec_stage(k, buf, axis):
        for cp in vcp:
            cp.wait()
        vcp.clear()
        if k == 0:
            v = v0[...] + v1[...]
        else:
            last = (vy, vz)[k - 1]
            v = (last[0] + last[1]) + (last[2] + last[3])
        place = {"y": y, "z": z, "x": x}[axis]
        buf[place] = v
        for d in (1, 2, 3):
            vcp.append(
                send(buf.at[place], buf.at[place], vs.at[3 * k + d], vr.at[3 * k + d], moved(axis, d))
            )

    sums.end(0)
    sums.begin(1)
    vec_stage(0, vy, "y")
    sums.end(1)
    sums.begin(2)
    vec_stage(1, vz, "z")
    lo = 64
    for v in mlp_sums.end(2):
        gx[lo : lo + v.shape[0], :] = v
        lo += v.shape[0]
    g = sums.end(2)
    gx[0:32, :] = g[0]
    gx[32:48, :] = g[1]
    gx[48:64, :] = g[2]
    grad = gx[...]
    u = (1.0 + MU) * grad + (MU * MU) * mt
    ub = u.astype(bf16)
    hi, lo = split(u[48:64])
    us[0, 0:48] = ub[0:48]
    us[0, 48:64] = jnp.zeros((16, 128), bf16)
    us[1, 0:16] = hi
    us[1, 16:32] = lo
    us[1, 32:64] = jnp.zeros((32, 128), bf16)
    us[2] = ub[64:128]
    us[3] = ub[128:192]
    cps = []
    for d in (1, 2, 3):
        cps.append(send(us.at[(x + d) % 4], ur.at[x], xs.at[d - 1], xr.at[d - 1], moved("x", d)))
    vec_stage(2, vx, "x")
    ur[x] = us[x]
    r.gxa[y, z, s] = grad.astype(bf16)
    for cp in cps:
        cp.wait()
    for k in range(4):
        piece = ur[k]

        @pl.when(x != 3)
        def _(k=k, piece=piece):
            ua[:, y, z, s, :, 128 * k : 128 * k + 128] = piece.reshape(4, 16, 128)

        @pl.when(x == 3)
        def _(k=k, piece=piece):
            for b in range(4):
                ua[k, y, z, s, :, 128 * b : 128 * b + 128] = piece[16 * b : 16 * b + 16]

    gather = Gather(
        [
            (lambda a, b, e: ua.at[pl.ds(0, 2), a, b, e], True),
            (lambda a, b, e: ua.at[pl.ds(2, 2), a, b, e], False),
        ],
        r.sa, r.ra,
    )
    gather.begin()
    for cp in vcp:
        cp.wait()
    r.vec[...] = (vx[0] + vx[1]) + (vx[2] + vx[3])
    gather.turn()
    gather.pass_on()
    gather.end()


def dot3(a, b):
    (ah, al), (bh, bl) = a, b
    return dot(ah, bh) + (dot(ah, bl) + dot(al, bh))


def newton_phase(r):
    y, z, s, x = coords()
    ua, ga, oa, a_ref = r.w3, r.gxa, r.oa, r.a
    ah, al, ph, pl_, th, tl, uh, ul = r.ah, r.al, r.ph, r.pl, r.th, r.tl, r.uh, r.ul
    os, rows, xs, xr = r.os, r.rows, r.os_s, r.os_r
    grads = Gather(
        [
            (lambda a, b, e: ga.at[a, b, e, pl.ds(0, 96)], True),
            (lambda a, b, e: ga.at[a, b, e, pl.ds(96, 96)], False),
        ],
        r.sb, r.rb,
    )
    grads.begin()

    def load(hi, lo):
        return hi[...], lo[...]

    def store(hi, lo, v):
        h, l = split(v)
        hi[...] = h
        lo[...] = l

    @pl.when(x == 1)
    def _():
        uh[...] = ua[0].reshape(512, 512)
        ul[...] = ua[1].reshape(512, 512)
        h, l = uh[...], ul[...]
        a_ref[...] = dot_tn(h, h) + (dot_tn(h, l) + dot_tn(l, h))

    @pl.when(x != 1)
    def _():
        u = ua[...].reshape(2048, 512)
        a_ref[...] = dot_tn(u, u)

    row = lax.broadcasted_iota(jnp.int32, (512, 512), 0)
    col = lax.broadcasted_iota(jnp.int32, (512, 512), 1)
    eye = row == col
    a = a_ref[...]
    square = jnp.sum(jnp.sum(jnp.where(eye, a, 0.0), axis=0, keepdims=True), axis=1, keepdims=True)
    scale = 1.0 / (jnp.sqrt(square) + 1e-07)
    a_ref[...] = a * (scale * scale)
    mine = ua[:, y, z, s].reshape(64, 512).astype(f32) * scale

    def poly():
        store(ah, al, a_ref[...])
        sq = dot3(load(ah, al), load(ah, al))
        return C2 * a_ref[...] + C3 * sq + jnp.where(eye, C1, 0.0)

    def step(_, mine):
        store(ph, pl_, poly())
        pair = load(ph, pl_)
        store(th, tl, dot3(pair, load(ah, al)))
        a_ref[...] = dot3(pair, load(th, tl))
        return dot3(split(mine), pair)

    mine = lax.fori_loop(0, 2, step, mine)
    grads.turn()
    mine = lax.fori_loop(2, NS_ITERS - 1, step, mine)
    grads.pass_on()
    store(ph, pl_, poly())
    mine = dot3(split(mine), load(ph, pl_))
    side = jnp.where(x == 0, math.sqrt(1536.0), jnp.where(x == 1, math.sqrt(512.0), math.sqrt(2048.0)))
    mine = mine * (0.2 * side)
    mine = jnp.concatenate(
        [jnp.where(x == 1, mine[0:16] + mine[16:32], mine[0:16]), mine[16:64]], axis=0
    ).astype(bf16)
    for k in range(4):
        by_lanes = mine[:, 128 * k : 128 * k + 128]
        by_rows = jnp.concatenate(
            [mine[16 * k : 16 * k + 16, 128 * b : 128 * b + 128] for b in range(4)], axis=0
        )
        os[k] = jnp.where(x == 3, by_rows, by_lanes)
    cps = []
    for d in (1, 2, 3):
        cps.append(send(os.at[(x + d) % 4], rows.at[x], xs.at[d - 1], xr.at[d - 1], moved("x", d)))
    rows[x] = os[x]
    grads.end()
    for cp in cps:
        cp.wait()
    oa[y, z, s, 0:48] = rows[0, 0:48]
    oa[y, z, s, 48:64] = rows[1, 0:16]
    oa[y, z, s, 64:128] = rows[2]
    oa[y, z, s, 128:192] = rows[3]
    update = Gather(
        [
            (lambda a, b, e: oa.at[a, b, e, pl.ds(0, 96)], True),
            (lambda a, b, e: oa.at[a, b, e, pl.ds(96, 96)], False),
        ],
        r.se, r.re,
    )
    update.begin()
    update.turn()
    update.pass_on()
    update.end()


def scratch_list():
    V = pltpu.VMEM
    piece = (HEADS, TOK, 128)
    out = [
        ("fq", V((128, 1536), f32)), ("fo", V((128, 512), f32)),
        ("fi", V((128, 2048), f32)), ("ff", V((512, 512), f32)),
        ("x", V((TOK, D), bf16)), ("dy", V((TOK, D), bf16)),
        ("w1", V((4, 4, 4, 2, 64, 128), bf16)), ("w2", V((4, 4, 4, 2, 64, 128), bf16)),
        ("w3", V((4, 4, 4, 2, 16, 512), bf16)),
        ("kvs", V(piece, bf16)), ("qds", V(piece, bf16)),
        ("kv", V((GROUP, 128), bf16)), ("qd", V((NQB, QB, 128), bf16)),
        ("hid", V((TOK, D), bf16)), ("wide_f", V((TOK, D), f32)),
        ("co", V((TOK, 128), f32)), ("s1", V((TOK, 128), f32)), ("s2", V((TOK, 128), f32)),
        ("res", V((TOK, D), f32)), ("dh", V((TOK, D), f32)),
        ("gm", V((4, 4, 2, 4, 128, 128), bf16)),
        ("rcm", V((4, 4, 4, 128, 128), bf16)), ("hbuf", V((4, 4, 4, 128, 128), bf16)),
        ("kvt", V((128, GROUP), bf16)), ("acc", V((GROUP, 128), f32)),
        ("s_sc", V((GROUP, QB), f32)), ("p_sc", V((GROUP, QB), f32)),
        ("m_sc", V((GROUP // HB, 8, QB), f32)), ("cqs", V((NQB, QB, 128), bf16)),
        ("half", V((16, TOK, 128), bf16)), ("other", V((16, TOK, 128), bf16)),
        ("both", V((16, TOK, 128), bf16)),
        ("cq", V(piece, bf16)), ("kr", V((HEADS, 2, TOK, 128), bf16)),
        ("dqkv", V((TOK, 1536), bf16)),
        ("mwin", V((128, 512), f32)), ("mtr", V((512, 128), f32)), ("mfin", V((16, 512), f32)),
        ("gx", V((192, 128), f32)),
        ("us", V((4, 64, 128), bf16)), ("ur", V((4, 64, 128), bf16)),
        ("os", V((4, 64, 128), bf16)), ("rows", V((4, 64, 128), bf16)),
        ("v0", V((16, 512), f32)), ("v1", V((16, 512), f32)),
        ("vy", V((4, 16, 512), f32)), ("vz", V((4, 16, 512), f32)), ("vx", V((4, 16, 512), f32)),
        ("a", V((512, 512), f32)),
    ]
    out += [(k, V((512, 512), bf16)) for k in ("ah", "al", "ph", "pl", "th", "tl", "uh", "ul")]
    for name, shape in (
        ("lsem", (6,)), ("msem", (4,)), ("xs", (3, 3)), ("xr", (3, 3)),
        ("sa", (2, 10)), ("ra", (2, 10)), ("sb", (2, 10)), ("rb", (2, 10)),
        ("se", (2, 10)), ("re", (2, 10)),
        ("own_sem", None), ("ks", None), ("kvr", None), ("qs", (24,)), ("qr", None),
        ("cs", None), ("cr", None),
        ("m_s", (2,)), ("m_r", (2,)), ("ms", (3, 3, 3)), ("mr", (3, 3, 3)), ("as_", (3, 3, 3)), ("ar", (3, 3, 3)),
        ("ws", (3,)), ("wr", (3,)), ("bs", None), ("br", None), ("rqs", (NQB, 4)), ("rqr", None),
        ("vs", (10,)), ("vr", (10,)), ("us_s", (3,)), ("us_r", (3,)), ("os_s", (3,)), ("os_r", (3,)),
    ):
        out.append((name, DMA if shape is None else DMA(shape)))
    out += [(f"mlp{i}", v) for i, v in enumerate(Reduce.scratch(MLP_PARTS))]
    out += [(f"att{i}", v) for i, v in enumerate(Reduce.scratch(ATT_PARTS))]
    return out


INPUTS = (
    "starts", "x_in", "dy_in", "gain", "shift", "bias", "wq", "wo", "wi", "wf", "mq", "mo", "mi", "mf",
)
OUTPUTS = ("out", "gt", "gxa", "oa", "vec")


def step_kernel(names, *refs):
    r = types.SimpleNamespace(**dict(zip(names, refs)))
    r.mlp_bufs = [getattr(r, f"mlp{i}") for i in range(5 * len(MLP_PARTS))]
    r.att_bufs = [getattr(r, f"att{i}") for i in range(5 * len(ATT_PARTS))]
    chip = front_phase(r)
    back_phase(r, attention_phase(r, chip))
    newton_phase(r)


def train_step(*args):
    scratch = scratch_list()
    names = INPUTS + OUTPUTS + tuple(k for k, _ in scratch)
    return pl.pallas_call(
        functools.partial(step_kernel, names),
        out_shape=tuple(
            jax.ShapeDtypeStruct(shape, t)
            for shape, t in (
                ((TOK, D), bf16), ((TOK, D), f32),
                ((4, 4, 2, 192, 128), bf16), ((4, 4, 2, 192, 128), bf16), ((16, 512), f32),
            )
        ),
        in_specs=[SM, ANY, ANY, VM, VM, VM] + [ANY] * 8,
        out_specs=(VM,) * 5,
        scratch_shapes=[v for _, v in scratch],
        compiler_params=pltpu.CompilerParams(
            vmem_limit_bytes=63 * 2**20, collective_id=1, has_side_effects=True
        ),
        name="train_step",
    )(*args)


def update_kernel(
    gx, oa, out, gt, wq, wo, wi, wf, mq, mo, mi, mf, vec, vm, gain, shift, bias,
    out_to, gt_to, nmq, nwq, nmo, nwo, nmi, nwi, nmf, nwf, nvm, nvec,
):
    out_to[...] = out[...]
    gt_to[...] = gt[...]

    @pl.when(pl.program_id(0) == 0)
    def _():
        for k in range(11):
            part = slice(512 * k, 512 * k + 512)
            v = VMU * vm[part] + vec[k]
            old = (gain[...], shift[...])[k] if k < 2 else bias[512 * k - 1024 : 512 * k - 512]
            nvm[part] = v
            nvec[part] = old - VLR * v

    for lo, n, w, m, nm, nw in (
        (0, 48, wq, mq, nmq, nwq),
        (48, 16, wo, mo, nmo, nwo),
        (64, 64, wi, mi, nmi, nwi),
    ):
        grad = gx[:, lo : lo + n, :].astype(f32).reshape(8 * n, 128).T
        turned = oa[:, lo : lo + n, :].astype(f32).reshape(8 * n, 128).T
        nm[...] = MU * m[...] + grad
        nw[...] = (1.0 - LR * WD) * w[...] - LR * turned
    for b in range(4):
        cols = slice(128 * b, 128 * b + 128)
        rows = slice(128 + 16 * b, 144 + 16 * b)
        grad = gx[:, rows, :].astype(f32).reshape(128, 128)
        turned = oa[:, rows, :].astype(f32).reshape(128, 128)
        nmf[:, cols] = MU * mf[:, cols] + grad
        nwf[:, cols] = (1.0 - LR * WD) * wf[:, cols] - LR * turned


def update(gx, oa, out, gt, weights, moments, vec, vec_mom, gain, shift, biases):
    def whole(v):
        return pl.BlockSpec(v.shape, lambda i, n=v.ndim: (0,) * n)

    piece = pl.BlockSpec((8, 192, 128), lambda i: (i, 0, 0))
    rows = pl.BlockSpec((48, D), lambda i: (i, 0))
    blocks = [
        pl.BlockSpec((128, 384), lambda i: (0, i)),
        pl.BlockSpec((128, 128), lambda i: (0, i)),
        pl.BlockSpec((128, 512), lambda i: (0, i)),
        pl.BlockSpec((128, 512), lambda i: (i, 0)),
    ]
    shape = lambda v: jax.ShapeDtypeStruct(v.shape, v.dtype)
    outs, specs = [shape(out), shape(gt)], [rows, rows]
    for w, b in zip(weights, blocks):
        outs += [shape(w)] * 2
        specs += [b, b]
    outs += [shape(vec_mom)] * 2
    specs += [whole(vec_mom)] * 2
    vectors = (vec, vec_mom, gain, shift, biases)
    return pl.pallas_call(
        update_kernel,
        grid=(4,),
        out_shape=tuple(outs),
        in_specs=[piece, piece, rows, rows] + blocks + blocks + [whole(v) for v in vectors],
        out_specs=tuple(specs),
        compiler_params=pltpu.CompilerParams(vmem_limit_bytes=60 * 2**20),
        name="update_weights",
    )(gx, oa, out, gt, *weights, *moments, *vectors)


def body(
    tokens, cotangent, ln_gain, ln_bias, biases, w_qkv, w_out, w_in, w_fin,
    mom_qkv, mom_out, mom_in, mom_fin, vec_mom, starts,
):
    weights = (w_qkv, w_out, w_in, w_fin)
    moments = (mom_qkv, mom_out, mom_in, mom_fin)
    block_out, grad_tokens, gx, oa, vec_sum = train_step(
        starts, tokens, cotangent, ln_gain[None, :], ln_bias[None, :], biases, *weights, *moments
    )
    return update(
        gx.reshape(32, 192, 128), oa.reshape(32, 192, 128), block_out, grad_tokens,
        weights, moments, vec_sum, vec_mom, ln_gain, ln_bias, biases,
    )


def solution(mesh):
    tok = P(("wsh", "ctx"), None)
    row = P("wsh", None)
    return jax.shard_map(
        body,
        mesh=mesh,
        in_specs=(tok, tok, P(), P(), P()) + (row,) * 8 + (P(), P()),
        out_specs=(tok, tok) + (row,) * 8 + (P(), P()),
        check_vma=False,
    )
```

```python
import functools
import math
import types

import jax
import jax.numpy as jnp
from jax import lax
from jax.experimental import pallas as pl
from jax.experimental.pallas import tpu as pltpu
from jax.sharding import PartitionSpec as P

f32 = jnp.float32
bf16 = jnp.bfloat16
MESH = pl.DeviceIdType.MESH
HEADS = 8
HD = 64
ROT = 16
D = 512
TOK = 192
GROUP = 6144
QB = 256
NQB = 6
HB = 128
UU = 8
TT = 4
NS_ITERS = 5
C1, C2, C3 = 3.4445, -4.775, 2.0315
MU, LR, WD = 0.95, 0.6, 0.01
VMU, VLR = 0.9, 0.0005
R_QKV, R_OUT, R_IN, R_FIN = 48, 16, 64, 64

VM = pl.BlockSpec(memory_space=pltpu.VMEM)
SM = pl.BlockSpec(memory_space=pltpu.SMEM)
ANY = pl.BlockSpec(memory_space=pl.ANY)
DMA = pltpu.SemaphoreType.DMA


def dot(a, b):
    return jnp.dot(a, b, preferred_element_type=f32)


def dot_nt(a, b):
    return lax.dot_general(a, b, (((1,), (1,)), ((), ())), preferred_element_type=f32)


def dot_tn(a, b):
    return lax.dot_general(a, b, (((0,), (0,)), ((), ())), preferred_element_type=f32)


def coords():
    c = lax.axis_index("ctx")
    return c // 8, (c // 2) % 4, c % 2, lax.axis_index("wsh")


def at(y, z, s, x):
    return {"ctx": (y * 4 + z) * 2 + s, "wsh": x}


def tell(partners):
    sem = pltpu.get_barrier_semaphore()
    for p in partners:
        pl.semaphore_signal(sem, inc=1, device_id=p, device_id_type=MESH)


def tell_slab():
    c = lax.axis_index("ctx")
    sem = pltpu.get_barrier_semaphore()

    def one(d, _):
        pl.semaphore_signal(
            sem, inc=1, device_id={"ctx": lax.rem(c + d, 32)}, device_id_type=MESH
        )
        return 0

    lax.fori_loop(1, 32, one, 0)


def met(count):
    pl.semaphore_wait(pltpu.get_barrier_semaphore(), count)


def wait_for(ref, sem):
    pltpu.make_async_copy(ref, ref, sem).wait()


def loop(lo, hi, f):
    def step(i, _):
        f(i)
        return 0

    lax.fori_loop(lo, hi, step, 0)


AXES = ("y", "z", "x")


def moved(axis, d):
    y, z, s, x = coords()
    if axis == "y":
        return at((y + d) % 4, z, s, x)
    if axis == "z":
        return at(y, (z + d) % 4, s, x)
    return at(y, z, s, (x + d) % 4)


def other_core():
    y, z, s, x = coords()
    return at(y, z, 1 - s, x)


def lines(axes=AXES):
    return [moved(a, d) for a in axes for d in (1, 2, 3)]


def send(src, dst, ss, rs, dev):
    cp = pltpu.make_async_remote_copy(
        src_ref=src, dst_ref=dst, send_sem=ss, recv_sem=rs, device_id=dev, device_id_type=MESH
    )
    cp.start()
    return cp


ALL = slice(None)


class Gather:
    def __init__(self, items, ss, rs):
        self.items, self.ss, self.rs = items, ss, rs

    def begin(self):
        y, z, s, x = coords()
        for i, (get, y_first) in enumerate(self.items):
            piece = get(y, z, s)
            for d in (1, 2, 3):
                send(
                    piece, piece, self.ss.at[i, 0], self.rs.at[i, 0], moved("y" if y_first else "z", d)
                )

    def turn(self):
        y, z, s, x = coords()
        three = pl.ds(0, 3)
        for i, (get, y_first) in enumerate(self.items):
            pieces = get(three, z, s) if y_first else get(y, three, s)
            wait_for(pieces, self.ss.at[i, 0])
            wait_for(pieces, self.rs.at[i, 0])
        self.second = {}
        for i, (get, y_first) in enumerate(self.items):
            piece = get(ALL, z, s) if y_first else get(y, ALL, s)
            for d in (1, 2, 3):
                to = moved("z" if y_first else "y", d)
                self.second[i, d] = send(piece, piece, self.ss.at[i, 1], self.rs.at[i, d], to)
        for i, (get, y_first) in enumerate(self.items):
            piece = get(ALL, z, s) if y_first else get(y, ALL, s)
            send(piece, piece, self.ss.at[i, 2], self.rs.at[i, 4], other_core())

    def pass_on(self):
        y, z, s, x = coords()
        for d in (1, 3, 2):
            for i, (get, y_first) in enumerate(self.items):
                self.second[i, d].wait_recv()
                piece = get(ALL, (z - d) % 4, s) if y_first else get((y - d) % 4, ALL, s)
                send(piece, piece, self.ss.at[i, 2], self.rs.at[i, 4], other_core())

    def end(self):
        three = pl.ds(0, 3)
        for i, (get, y_first) in enumerate(self.items):
            wait_for(get(ALL, three, 0) if y_first else get(three, ALL, 0), self.ss.at[i, 1])
            wait_for(get(ALL, ALL, 0), self.ss.at[i, 2])
            wait_for(get(ALL, ALL, 0), self.rs.at[i, 4])


def split(v):
    hi = v.astype(bf16)
    return hi, (v - hi.astype(f32)).astype(bf16)


class Reduce:
    def __init__(self, src, parts, bufs, ss, rs):
        self.src, self.parts, self.ss, self.rs = src, parts, ss, rs
        y, z, s, x = coords()
        self.me = {"y": y, "z": z, "x": x}
        self.bufs = [bufs[5 * i : 5 * i + 5] for i in range(len(parts))]

    @staticmethod
    def scratch(parts):
        out = []
        for lo, n, order, paired in parts:
            out += [
                pltpu.VMEM((3, 4, 4, n, 128), bf16),
                pltpu.VMEM((4, 4, n, 128), bf16),
                pltpu.VMEM((3, 4, n, 128), bf16),
                pltpu.VMEM((4, n, 128), bf16),
                pltpu.VMEM((3, n, 128), bf16),
            ]
        return out

    @staticmethod
    def summed(pieces, paired):
        v = functools.reduce(lambda a, b: a + b, [p.astype(f32) for p in pieces])
        if not paired:
            return v.astype(bf16)
        half = v.shape[-2] // 2
        return jnp.concatenate(split(v[..., :half, :] + v[..., half:, :]), axis=-2)

    def begin(self, stage):
        for d in (2, 1, 3):
            for i, (lo, n, order, paired) in enumerate(self.parts):
                r1, h1, r2, h2, r3 = self.bufs[i]
                axis = order[stage]
                place = (self.me[axis] + d) % 4
                left = [a for a in AXES if a not in order[:stage]]
                index = tuple(place if a == axis else ALL for a in left)
                if stage == 0:
                    src = self.src.at[index + (pl.ds(lo, n),)]
                else:
                    src = (h1, h2)[stage - 1].at[index]
                send(
                    src, (r1, r2, r3)[stage].at[d - 1],
                    self.ss.at[stage, i], self.rs.at[stage, i], moved(axis, d),
                )

    def end(self, stage):
        out = []
        for i, (lo, n, order, paired) in enumerate(self.parts):
            r1, h1, r2, h2, r3 = self.bufs[i]
            wait_for((r1, r2, r3)[stage], self.ss.at[stage, i])
            wait_for((r1, r2, r3)[stage], self.rs.at[stage, i])
            mine = self.me[order[stage]]
            if stage == 0:
                axis = AXES.index(order[0])

                def add(a, _, axis=axis, mine=mine, lo=lo, n=n, paired=paired, r1=r1, h1=h1):
                    index = [a, ALL]
                    index.insert(axis, mine)
                    own = self.src[tuple(index) + (slice(lo, lo + n),)]
                    h1[a] = self.summed([own, r1[0, a], r1[1, a], r1[2, a]], paired)
                    return 0

                lax.fori_loop(0, 4, add, 0)
            elif stage == 1:
                left = [a for a in AXES if a != order[0]]
                first = left.index(order[1]) == 0
                own = h1[mine] if first else h1[:, mine]
                h2[...] = self.summed([own, r2[0], r2[1], r2[2]], paired)
            else:
                v = h2[mine].astype(f32) + r3[0].astype(f32) + r3[1].astype(f32) + r3[2].astype(f32)
                if paired:
                    v = v[: n // 2] + v[n // 2 :]
                out.append(v)
        return out


MLP_PARTS = ((0, 48, ("y", "z", "x"), False), (48, 48, ("z", "x", "y"), False), (96, 32, ("x", "y", "z"), False))
ATT_PARTS = ((0, 32, ("y", "z", "x"), False), (32, 16, ("z", "x", "y"), False), (48, 32, ("x", "y", "z"), True))


def norm_parts(x_ref, gain, shift):
    xf = x_ref[...].astype(f32)
    centered = xf - jnp.mean(xf, axis=1, keepdims=True)
    inv = lax.rsqrt(jnp.mean(centered * centered, axis=1, keepdims=True) + 1e-05)
    normed = centered * inv
    hidden = (normed * gain + shift).astype(bf16)
    return xf, inv, normed, hidden


def turn(v, co, s1, s2):
    return v * co + pltpu.roll(v, 120, 1) * s1 + pltpu.roll(v, 8, 1) * s2


def rolled(ref, x):
    parts = [ref[:, pl.ds(pl.multiple_of((x + d) % 4 * 128, 128), 128)] for d in range(4)]
    return jnp.concatenate(parts, axis=1)


def unroll(v, ref, x):
    for d in range(4):
        ref[:, pl.ds(pl.multiple_of((x + d) % 4 * 128, 128), 128)] = v[:, 128 * d : 128 * d + 128]
    return ref[...]


def rotary(starts_ref, x, c):
    bnd = starts_ref[x] - x * GROUP
    place = c * TOK + lax.broadcasted_iota(jnp.int32, (TOK, 128), 0)
    pos = (place - jnp.where(place >= bnd, bnd, 0)).astype(f32)
    lane = lax.broadcasted_iota(jnp.int32, (TOK, 128), 1) % HD
    freq = jnp.zeros((TOK, 128), f32)
    for i in range(ROT // 2):
        freq = jnp.where(lane % 8 == i, 10000.0 ** (-2.0 * i / ROT), freq)
    angle = pos * jnp.where(lane < ROT, freq, 0.0)
    co, si = jnp.cos(angle), jnp.sin(angle)
    return co, jnp.where(lane < 8, -si, 0.0), jnp.where(lane < 8, 0.0, si)


def wide(w, first, count):
    blocks = [w[(first + i) // 4, (first + i) % 4].reshape(512, 128) for i in range(count)]
    return jnp.concatenate(blocks, axis=1) if count > 1 else blocks[0]


def query_home(piece):
    block = piece // 4
    part = block % 8
    low = part < 4
    return jnp.where(low, part, 7 - part), 2 * (block // 8) + jnp.where(low, 0, 1), piece % 4


def query_block(t, j):
    if isinstance(t, int):
        return 8 * (t // 2) + (j if t % 2 == 0 else 7 - j)
    return 8 * (t // 2) + jnp.where(t % 2 == 0, j, 7 - j)


def front_phase(r):
    y, z, s, x = coords()
    c = lax.axis_index("ctx")
    p = c // 2
    w1, w2, w3, kvs, qds, kv, qd = r.w1, r.w2, r.w3, r.kvs, r.qds, r.kv, r.qd
    ks, kr, qs, qr, cs, cr = r.ks, r.kvr, r.qs, r.qr, r.cs, r.cr
    bias_ref = r.bias
    tell_slab()
    tell(lines(("x",)))
    loads = [
        pltpu.make_async_copy(src, dst, r.lsem.at[k])
        for k, (src, dst) in enumerate(
            ((r.wq, r.fq), (r.wo, r.fo), (r.wi, r.fi), (r.wf, r.ff), (r.x_in, r.x), (r.dy_in, r.dy))
        )
    ]
    for cp in loads:
        cp.start()
    momenta_begin(r)
    for cp in loads:
        cp.wait()
    for b in range(16):
        w = r.fq[:, 128 * b : 128 * b + 128] if b < 12 else r.fo[:, 128 * b - 1536 : 128 * b - 1408]
        w1[b // 4, b % 4, 0] = w.astype(bf16).reshape(2, 64, 128)
        w2[b // 4, b % 4, 0] = r.fi[:, 128 * b : 128 * b + 128].astype(bf16).reshape(2, 64, 128)
    w3[0] = r.ff[...].astype(bf16).reshape(4, 4, 2, 16, 512)
    met(34)
    slab, direct = pl.ds(0, 32), pl.ds(32, 32)

    def along_x(k, piece):
        return [
            send(piece(0), piece(4 - d), r.xs.at[k, d - 1], r.xr.at[k, d - 1], moved("x", d))
            for d in (1, 2, 3)
        ]

    low, high = pl.ds(0, 256), pl.ds(256, 256)
    own_cps = along_x(0, lambda d: w1.at[y, z, d, s, slab])
    late_cps = along_x(4, lambda d: w3.at[d, y, z, s, :, high])
    direct_cps = along_x(1, lambda d: w1.at[:, :, d, s, direct])
    co, s1, s2 = rotary(r.starts, x, c)
    r.co[...], r.s1[...], r.s2[...] = co, s1, s2
    xf, inv, normed, hidden = norm_parts(r.x, r.gain[...], r.shift[...])
    r.hid[...] = hidden
    hidden_r = rolled(r.hid, x)
    dy = r.dy[...]
    for cp in own_cps:
        cp.wait()
    others = pl.ds(1, 3)
    early = Gather(
        [
            (lambda a, b, e: w1.at[a, b, others, e, pl.ds(0, 16)], True),
            (lambda a, b, e: w1.at[a, b, others, e, pl.ds(16, 16)], False),
        ],
        r.sa, r.ra,
    )
    late = Gather(
        [
            (lambda a, b, e: w3.at[others, a, b, e, :, pl.ds(256, 128)], True),
            (lambda a, b, e: w3.at[others, a, b, e, :, pl.ds(384, 128)], False),
        ],
        r.sb, r.rb,
    )

    def to_core(k, cps, piece):
        out = []
        for d in (1, 3, 2):
            cps[d - 1].wait_recv()
            got = piece(4 - d)
            out.append(send(got, got, r.ys.at[k, d - 1], r.yr.at[k, d - 1], other_core()))
        for cp in cps:
            cp.wait_send()
        return out

    early.begin()
    early.turn()
    passed = to_core(0, direct_cps, lambda d: w1.at[:, :, d, s, direct])
    in_cps = along_x(2, lambda d: w2.at[:, :, d, s])
    fin_cps = along_x(3, lambda d: w3.at[d, :, :, s, :, low])
    early.pass_on()
    for cp in late_cps:
        cp.wait()
    late.begin()
    early.end()
    for cp in passed:
        cp.wait()
    left = lax.broadcasted_iota(jnp.int32, (TOK, 128), 1) < 64
    dctx = unroll(dot_nt(dy, wide(w1, 12, 4)), r.wide_f, x)
    for half in range(2):
        thirds = []
        for third in range(3):
            b = third * 4 + 2 * half
            thirds.append(dot(hidden_r, wide(w1, b, 2)) + bias_ref[b * 128 : b * 128 + 256][None, :])
        for e in range(2):
            lanes = slice(128 * e, 128 * e + 128)
            q = turn(thirds[0][:, lanes], co, s1, s2).astype(bf16).astype(f32) * 0.125
            k = turn(thirds[1][:, lanes], co, s1, s2)
            v = thirds[2][:, lanes]
            pair = 2 * half + e
            g = dctx[:, pair * 128 : pair * 128 + 128]
            h = 2 * pair
            kvs[h] = jnp.where(left, k, pltpu.roll(v, 64, 1)).astype(bf16)
            kvs[h + 1] = jnp.where(left, pltpu.roll(k, 64, 1), v).astype(bf16)
            qds[h] = jnp.where(left, q, pltpu.roll(g, 64, 1)).astype(bf16)
            qds[h + 1] = jnp.where(left, pltpu.roll(q, 64, 1), g).astype(bf16)

    def kv_copy(d):
        to = lax.rem(p + d, 16)
        return pltpu.make_async_remote_copy(
            src_ref=kvs.at[to // 2], dst_ref=kv.at[pl.ds(c * TOK, TOK)], send_sem=ks, recv_sem=kr,
            device_id={"ctx": to * 2 + s}, device_id_type=MESH,
        )

    def across(d):
        block = kv.at[pl.ds((lax.rem(p + 16 - d, 16) * 2 + s) * TOK, TOK)]
        return pltpu.make_async_remote_copy(
            src_ref=block, dst_ref=block, send_sem=cs, recv_sem=cr,
            device_id={"ctx": p * 2 + 1 - s}, device_id_type=MESH,
        )

    def each_query(k):
        h, i = k // 3, k % 3
        j, t, quarter = query_home(3 * c + i)
        to = 4 * h + j
        src = qds.at[h, pl.ds(64 * i, 64)]
        dst = qd.at[t, pl.ds(64 * quarter, 64)]

        @pl.when(to == c)
        def _():
            pltpu.make_async_copy(src, dst, qr).start()
            pltpu.make_async_copy(src, r.spare.at[i], qs).start()

        @pl.when(to != c)
        def _():
            pltpu.make_async_remote_copy(
                src_ref=src, dst_ref=dst, send_sem=qs, recv_sem=qr,
                device_id={"ctx": to}, device_id_type=MESH,
            ).start()

    own = pltpu.make_async_copy(kvs.at[p // 2], kv.at[pl.ds(c * TOK, TOK)], r.own_sem)
    own.start()
    late.turn()
    loop(1, 16, lambda d: kv_copy(d).start())
    loop(0, 24, each_query)
    own.wait()

    r.acc[...] = jnp.zeros_like(r.acc)
    late.pass_on()
    late.end()
    passed = to_core(1, in_cps, lambda d: w2.at[:, :, d, s])
    passed += to_core(2, fin_cps, lambda d: w3.at[d, :, :, s, :, low])
    for cp in passed:
        cp.wait()
    root = math.sqrt(2.0 / math.pi)
    mlp = jnp.zeros((TOK, D), f32)
    dh = jnp.zeros((TOK, D), f32)
    for i in range(4):
        if i == 2:
            wait_for(kv.at[pl.ds(0, 15 * TOK)], kr)
            loop(0, 16, lambda d: across(d).start())
        w_in = wide(w2, 4 * i, 4)
        w_fin = w3[(i + 4 - x) % 4].reshape(512, 512)
        pre = dot(hidden_r, w_in) + bias_ref[2048 + 512 * i : 2560 + 512 * i][None, :]
        sq = pre * pre
        th = jnp.tanh(root * (pre + 0.044715 * (pre * sq)))
        act = (0.5 * pre * (1.0 + th)).astype(bf16)
        slope = 0.5 * (1.0 + th) + (0.5 * root) * pre * (1.0 - th * th) * (
            1.0 + (3.0 * 0.044715) * sq
        )
        dpre = (dot_nt(dy, w_fin) * slope).astype(bf16)
        mlp = mlp + dot(act, w_fin)
        dh = dh + dot_nt(dpre, w_in)
        r.v0[6 + i : 7 + i, :] = jnp.sum(dpre.astype(f32), axis=0, keepdims=True)
        g_in = dot_tn(dpre, hidden).astype(bf16).reshape(4, 2, 64, 512)
        g_fin = dot_tn(act, dy).astype(bf16).reshape(4, 4, 2, 16, 512)
        for b in range(4):
            lanes = slice(128 * b, 128 * b + 128)
            r.gm[i, :, :, b, 0:64] = g_in[..., lanes]
            r.gm[:, :, :, i, 64 + 16 * b : 80 + 16 * b] = g_fin[..., lanes]
    r.res[...] = xf + mlp + (bias_ref[4096:4608] + bias_ref[1536:2048])[None, :]
    r.dh[...] = dh
    chip = send(r.gm.at[:, :, 1 - s], r.rcm, r.m_s.at[0], r.m_r.at[0], other_core())
    wait_for(kv.at[pl.ds(0, 15 * TOK)], ks)
    wait_for(qd, qs)
    wait_for(qd, qr)
    wait_for(kv.at[pl.ds(0, 16 * TOK)], cs)
    wait_for(kv.at[pl.ds(0, 16 * TOK)], cr)
    return chip


RETURNS = ((14, 16), (11, 14), (8, 11), (6, 8), (3, 6), (0, 3))


def attention_phase(r, chip):
    kvt, acc, s_sc, p_sc, m_sc, cqs = r.kvt, r.acc, r.s_sc, r.p_sc, r.m_sc, r.cqs
    half, other, both, rcm, hbuf = r.half, r.other, r.both, r.rcm, r.hbuf
    cq, kr, kv_ref, qd_ref, gm_ref = r.cq, r.kr, r.kv, r.qd, r.gm
    ws, wr, ss, sr, qs, qr = r.ws, r.wr, r.bs, r.br, r.rqs, r.rqr
    y, z, s, x = coords()
    c = lax.axis_index("ctx")
    p = c // 2
    h = c // 4
    j = c % 4
    n = kv_ref.shape[0]
    bnd = r.starts[x] - x * GROUP

    def prepare(i, _):
        o = pl.multiple_of(i * QB, QB)
        kvt[:, pl.ds(o, QB)] = kv_ref[pl.ds(o, QB), :].T
        return 0

    lax.fori_loop(0, n // QB, prepare, 0)
    lane = lax.broadcasted_iota(jnp.int32, (QB, 128), 1)

    def block(t):
        qb = query_block(t, j)
        qd = qd_ref[t]
        w1 = jnp.where(lane < 64, qd, jnp.zeros_like(qd))
        w2 = jnp.where(lane < 64, jnp.zeros_like(qd), qd)
        q_t = w1.T
        d_t = w2.T

        def scores(kt, masked, carry, tiles, first=False):
            m8, l8, r8 = carry
            for u in range(2 * tiles):
                o = pl.multiple_of(kt * QB + u * HB, HB)
                rows = kv_ref[pl.ds(o, HB), :]
                s = dot(rows, q_t)
                if masked and not (first and u > 1):
                    kp = o + lax.broadcasted_iota(jnp.int32, (HB, QB), 0)
                    qp = qb * QB + lax.broadcasted_iota(jnp.int32, (HB, QB), 1)
                    s = jnp.where((kp <= qp) & ((kp >= bnd) == (qp >= bnd)), s, -1e30)
                s = s.reshape(HB // 8, 8, QB)
                dp = dot(rows, d_t)
                p_sc[pl.ds(o, HB), :] = dp
                mn = jnp.maximum(m8, jnp.max(s, axis=0))
                e = jnp.exp(s - mn[None])
                s_sc[pl.ds(o, HB), :] = e.reshape(HB, QB)
                m_sc[2 * kt + u] = mn
                al = jnp.exp(m8 - mn)
                l8 = l8 * al + jnp.sum(e, axis=0)
                r8 = r8 * al + jnp.sum(e * dp.reshape(HB // 8, 8, QB), axis=0)
                m8 = mn
            return m8, l8, r8

        zero = jnp.zeros((8, QB), f32)
        base = t // 2 * 8
        tail = (qb - base) // TT + 1
        carry = lax.fori_loop(
            0, tail, lambda g, c: scores(base + TT * g, True, c, TT),
            (jnp.full((8, QB), -1e30, f32), zero, zero),
        )
        if base > 0:
            carry = scores(0, True, carry, UU, True)
        carry = lax.fori_loop(
            1, base // UU, lambda g, c: scores(g * UU, False, c, UU), carry
        )
        m8, l8, r8 = carry
        m = jnp.max(m8, axis=0, keepdims=True)
        w = jnp.exp(m8 - m)
        l = jnp.sum(l8 * w, axis=0, keepdims=True)
        lse = m + jnp.log(l)
        rd = jnp.sum(r8 * w, axis=0, keepdims=True) / l

        def grads(kt, carry, tiles):
            c_t, g_t = carry
            for u in range(tiles):
                o = pl.multiple_of((kt + u) * QB, QB)
                e = s_sc[pl.ds(o, QB), :].reshape(2, HB // 8, 8, QB)
                w0 = jnp.exp(m_sc[2 * (kt + u)] - lse)
                w1_ = jnp.exp(m_sc[2 * (kt + u) + 1] - lse)
                p = jnp.concatenate([e[0] * w0[None], e[1] * w1_[None]], axis=0).reshape(QB, QB)
                pb = p.astype(bf16)
                ds = (p * (p_sc[pl.ds(o, QB), :] - rd)).astype(bf16)
                c_t = c_t + dot(kvt[64:128, pl.ds(o, QB)], pb)
                g_t = g_t + dot(kvt[0:64, pl.ds(o, QB)], ds)
                acc[pl.ds(o, QB), :] += dot(ds, w1) + dot(pb, w2)
            return c_t, g_t

        z = jnp.zeros((64, QB), f32)
        c = lax.fori_loop(0, base // UU, lambda g, c: grads(g * UU, c, UU), (z, z))
        c_t, g_t = lax.fori_loop(0, tail, lambda g, c: grads(base + TT * g, c, TT), c)
        cqs[t] = jnp.concatenate([g_t * 0.125, c_t], axis=0).T.astype(bf16)

    def each_query(t, quarter):
        piece = 4 * query_block(t, j) + quarter
        to, i = piece // 3, piece % 3
        src = cqs.at[t, pl.ds(64 * quarter, 64)]
        dst = cq.at[h, pl.ds(64 * i, 64)]

        @pl.when(to == c)
        def _():
            pltpu.make_async_copy(src, dst, qr).start()
            pltpu.make_async_copy(src, r.spare.at[3 + i], qs).start()

        @pl.when(to != c)
        def _():
            pltpu.make_async_remote_copy(
                src_ref=src, dst_ref=dst, send_sem=qs, recv_sem=qr,
                device_id={"ctx": to}, device_id_type=MESH,
            ).start()

    def return_queries(t):
        loop(0, 4, lambda quarter: each_query(t, quarter))

    swaps = {}

    def exchange(g):
        lo, hi = RETURNS[g]

        def low(i):
            o = pl.multiple_of((2 * i + 1 - s) * TOK, TOK)
            half[i] = acc[pl.ds(o, TOK), :].astype(bf16)

        loop(lo, hi, low)
        part = pl.ds(lo, hi - lo)
        swaps[g] = send(half.at[part], other.at[part], ws.at[g], wr.at[g], other_core())

    def block_copy(i):
        return pltpu.make_async_remote_copy(
            src_ref=both.at[i], dst_ref=kr.at[h, p % 2], send_sem=ss, recv_sem=sr,
            device_id={"ctx": i * 2 + s}, device_id_type=MESH,
        )

    def push(g):
        lo, hi = RETURNS[g]
        swaps[g].wait()

        def one(i):
            o = pl.multiple_of((2 * i + s) * TOK, TOK)
            both[i] = (acc[pl.ds(o, TOK), :] + other[i].astype(f32)).astype(bf16)

            @pl.when(i == p)
            def _():
                pltpu.make_async_copy(both.at[i], kr.at[h, p % 2], sr).start()

            @pl.when(i != p)
            def _():
                block_copy(i).start()

        loop(lo, hi, one)

    def add(i):
        a, b = i // 4, i % 4
        hbuf[a, b] = (gm_ref[a, b, s].astype(f32) + rcm[a, b].astype(f32)).astype(bf16)

    chip.wait()
    loop(0, 16, add)
    sums = Reduce(hbuf, MLP_PARTS, r.mlp_bufs, r.ms, r.mr)
    sums.begin(0)
    for k in range(NQB):
        block(NQB - 1 - k)
        return_queries(NQB - 1 - k)
        exchange(k)
        if k > 0:
            push(k - 1)
        if k == 2:
            sums.end(0)
            sums.begin(1)
    push(NQB - 1)
    wait_for(both.at[pl.ds(0, 15)], ss)
    wait_for(cq, qs)
    wait_for(cq, qr)
    wait_for(kr, sr)
    sums.end(1)
    sums.begin(2)
    return sums


def momenta_starts():
    c = lax.axis_index("ctx")
    return jnp.minimum(48 * c // 128, 10), 16 * c // 128, 64 * c // 128


def momenta_loads(r):
    c = lax.axis_index("ctx")
    starts = momenta_starts()
    loads = []
    for k, (m, width) in enumerate(((r.mq, 256), (r.mo, 128), (r.mi, 128))):
        first = pl.multiple_of(starts[k] * 128, 128)
        loads.append(
            pltpu.make_async_copy(
                m.at[:, pl.ds(first, width)],
                r.mwin.at[:, pl.ds((0, 256, 384)[k], width)],
                r.msem.at[k],
            )
        )
    loads.append(pltpu.make_async_copy(r.mf.at[pl.ds(16 * c, 16)], r.mfin, r.msem.at[3]))
    return loads


def momenta_begin(r):
    for cp in momenta_loads(r):
        cp.start()


def momenta(r):
    c = lax.axis_index("ctx")
    for cp in momenta_loads(r):
        cp.wait()
    r.mtr[...] = r.mwin[...].T
    offset = 48 * c - momenta_starts()[0] * 128
    return jnp.concatenate(
        [
            r.mtr[pl.ds(pl.multiple_of(offset, 16), 48), :],
            r.mtr[pl.ds(pl.multiple_of(256 + 16 * c % 128, 16), 16), :],
            r.mtr[pl.ds(pl.multiple_of(384 + 64 * c % 128, 64), 64), :],
        ]
        + [r.mfin[:, 128 * b : 128 * b + 128] for b in range(4)],
        axis=0,
    )


def back_phase(r, mlp_sums):
    dqkv, gx, us, ur, v0, v1, vy, vz, vx = r.dqkv, r.gx, r.us, r.ur, r.v0, r.v1, r.vy, r.vz, r.vx
    cq_ref, kr_ref, w1, ga, rcm, hbuf = r.cq, r.kr, r.w1, r.gm, r.rcm, r.hbuf
    vs, vr, xs, xr, ua = r.vs, r.vr, r.us_s, r.us_r, r.w3
    att = pl.ds(0, 80)
    y, z, s, x = coords()
    c = lax.axis_index("ctx")
    xf, inv, normed, hidden = norm_parts(r.x, r.gain[...], r.shift[...])
    dy = r.dy[...]
    co, s1, s2 = r.co[...], -r.s1[...], -r.s2[...]
    left = lax.broadcasted_iota(jnp.int32, (TOK, 128), 1) < 64
    ctx = []
    for pair in range(4):
        a = cq_ref[2 * pair].astype(f32)
        b = cq_ref[2 * pair + 1].astype(f32)
        e = kr_ref[2 * pair, 0].astype(f32) + kr_ref[2 * pair, 1].astype(f32)
        f = kr_ref[2 * pair + 1, 0].astype(f32) + kr_ref[2 * pair + 1, 1].astype(f32)
        dq = jnp.where(left, a, pltpu.roll(b, 64, 1))
        dk = jnp.where(left, e, pltpu.roll(f, 64, 1))
        dqkv[:, 128 * pair : 128 * pair + 128] = turn(dq, co, s1, s2).astype(bf16)
        dqkv[:, 512 + 128 * pair : 640 + 128 * pair] = turn(dk, co, s1, s2).astype(bf16)
        dqkv[:, 1024 + 128 * pair : 1152 + 128 * pair] = jnp.where(
            left, pltpu.roll(e, 64, 1), f
        ).astype(bf16)
        ctx.append(jnp.where(left, pltpu.roll(a, 64, 1), b).astype(bf16))
    ctx = jnp.concatenate(ctx, axis=1)
    r.hid[...] = ctx
    hi, lo = split(dot_tn(dy, ctx))
    hi, lo = hi.reshape(4, 4, 2, 16, 512), lo.reshape(4, 4, 2, 16, 512)
    for b in range(4):
        lanes = slice(128 * b, 128 * b + 128)
        ga[:, :, :, b, 48:64] = hi[..., lanes]
        ga[:, :, :, b, 64:80] = lo[..., lanes]
    for i in range(4):
        part = dqkv[:, 384 * i : 384 * i + 384]
        g = dot_tn(part, hidden).astype(bf16).reshape(4, 2, 48, 512)
        for b in range(4):
            ga[i, :, :, b, 0:48] = g[..., 128 * b : 128 * b + 128]
    chip = send(ga.at[:, :, 1 - s, :, att], rcm.at[:, :, :, att], r.m_s.at[1], r.m_r.at[1], other_core())
    r.out[...] = (r.res[...] + dot(rolled(r.hid, x), wide(w1, 12, 4))).astype(bf16)
    dh = r.dh[...]
    for third in range(3):
        part = dqkv[:, 512 * third : 512 * third + 512]
        dh = dh + dot_nt(part, wide(w1, 4 * third, 4))
        v0[2 + third : 3 + third, :] = jnp.sum(part.astype(f32), axis=0, keepdims=True)
    dh = unroll(dh, r.wide_f, x)
    scaled = dh * r.gain[...]
    dyf = dy.astype(f32)
    r.gt[...] = dyf + inv * (
        scaled
        - jnp.mean(scaled, axis=1, keepdims=True)
        - normed * jnp.mean(scaled * normed, axis=1, keepdims=True)
    )
    dsum = jnp.sum(dyf, axis=0, keepdims=True)
    v0[0:1, :] = jnp.sum(dh * normed, axis=0, keepdims=True)
    v0[1:2, :] = jnp.sum(dh, axis=0, keepdims=True)
    v0[5:6, :] = dsum
    v0[10:11, :] = dsum
    v0[11:16, :] = jnp.zeros((5, 512), f32)
    chip.wait()
    vcp = [send(v0, v1, vs.at[0], vr.at[0], other_core())]

    def add(i):
        a, b = i // 4, i % 4
        both = ga[a, b, s, :, 0:80].astype(f32) + rcm[a, b, :, 0:80].astype(f32)
        hi, lo = split(both[:, 48:64] + both[:, 64:80])
        hbuf[a, b, :, 0:48] = both[:, 0:48].astype(bf16)
        hbuf[a, b, :, 48:64] = hi
        hbuf[a, b, :, 64:80] = lo

    loop(0, 16, add)
    sums = Reduce(hbuf, ATT_PARTS, r.att_bufs, r.as_, r.ar)
    sums.begin(0)
    mt = momenta(r)

    def vec_stage(k, buf, axis):
        for cp in vcp:
            cp.wait()
        vcp.clear()
        if k == 0:
            v = v0[...] + v1[...]
        else:
            last = (vy, vz)[k - 1]
            v = (last[0] + last[1]) + (last[2] + last[3])
        place = {"y": y, "z": z, "x": x}[axis]
        buf[place] = v
        for d in (1, 2, 3):
            vcp.append(
                send(buf.at[place], buf.at[place], vs.at[3 * k + d], vr.at[3 * k + d], moved(axis, d))
            )

    sums.end(0)
    sums.begin(1)
    vec_stage(0, vy, "y")
    sums.end(1)
    sums.begin(2)
    vec_stage(1, vz, "z")
    lo = 64
    for v in mlp_sums.end(2):
        gx[lo : lo + v.shape[0], :] = v
        lo += v.shape[0]
    g = sums.end(2)
    gx[0:32, :] = g[0]
    gx[32:48, :] = g[1]
    gx[48:64, :] = g[2]
    grad = gx[...]
    u = (1.0 + MU) * grad + (MU * MU) * mt
    ub = u.astype(bf16)
    hi, lo = split(u[48:64])
    us[0, 0:48] = ub[0:48]
    us[0, 48:64] = jnp.zeros((16, 128), bf16)
    us[1, 0:16] = hi
    us[1, 16:32] = lo
    us[1, 32:64] = jnp.zeros((32, 128), bf16)
    us[2] = ub[64:128]
    us[3] = ub[128:192]
    cps = []
    for d in (1, 2, 3):
        cps.append(send(us.at[(x + d) % 4], ur.at[x], xs.at[d - 1], xr.at[d - 1], moved("x", d)))
    vec_stage(2, vx, "x")
    ur[x] = us[x]
    r.gxa[y, z, s] = grad.astype(bf16)
    for cp in cps:
        cp.wait()
    for k in range(4):
        piece = ur[k]

        @pl.when(x != 3)
        def _(k=k, piece=piece):
            ua[:, y, z, s, :, 128 * k : 128 * k + 128] = piece.reshape(4, 16, 128)

        @pl.when(x == 3)
        def _(k=k, piece=piece):
            for b in range(4):
                ua[k, y, z, s, :, 128 * b : 128 * b + 128] = piece[16 * b : 16 * b + 16]

    gather = Gather(
        [
            (lambda a, b, e: ua.at[pl.ds(0, 2), a, b, e], True),
            (lambda a, b, e: ua.at[pl.ds(2, 2), a, b, e], False),
        ],
        r.sa, r.ra,
    )
    gather.begin()
    for cp in vcp:
        cp.wait()
    r.vec[...] = (vx[0] + vx[1]) + (vx[2] + vx[3])
    gather.turn()
    gather.pass_on()
    gather.end()


def dot3(a, b):
    (ah, al), (bh, bl) = a, b
    return dot(ah, bh) + (dot(ah, bl) + dot(al, bh))


def newton_phase(r):
    y, z, s, x = coords()
    ua, ga, oa, a_ref = r.w3, r.gxa, r.oa, r.a
    ah, al, ph, pl_, th, tl, uh, ul = r.ah, r.al, r.ph, r.pl, r.th, r.tl, r.uh, r.ul
    os, rows, xs, xr = r.os, r.rows, r.os_s, r.os_r
    grads = Gather(
        [
            (lambda a, b, e: ga.at[a, b, e, pl.ds(0, 96)], True),
            (lambda a, b, e: ga.at[a, b, e, pl.ds(96, 96)], False),
        ],
        r.sb, r.rb,
    )
    grads.begin()

    def load(hi, lo):
        return hi[...], lo[...]

    def store(hi, lo, v):
        h, l = split(v)
        hi[...] = h
        lo[...] = l

    @pl.when(x == 1)
    def _():
        uh[...] = ua[0].reshape(512, 512)
        ul[...] = ua[1].reshape(512, 512)
        h, l = uh[...], ul[...]
        a_ref[...] = dot_tn(h, h) + (dot_tn(h, l) + dot_tn(l, h))

    @pl.when(x != 1)
    def _():
        u = ua[...].reshape(2048, 512)
        a_ref[...] = dot_tn(u, u)

    row = lax.broadcasted_iota(jnp.int32, (512, 512), 0)
    col = lax.broadcasted_iota(jnp.int32, (512, 512), 1)
    eye = row == col
    a = a_ref[...]
    square = jnp.sum(jnp.sum(jnp.where(eye, a, 0.0), axis=0, keepdims=True), axis=1, keepdims=True)
    scale = 1.0 / (jnp.sqrt(square) + 1e-07)
    a_ref[...] = a * (scale * scale)
    mine = ua[:, y, z, s].reshape(64, 512).astype(f32) * scale

    def poly():
        store(ah, al, a_ref[...])
        sq = dot3(load(ah, al), load(ah, al))
        return C2 * a_ref[...] + C3 * sq + jnp.where(eye, C1, 0.0)

    def step(_, mine):
        store(ph, pl_, poly())
        pair = load(ph, pl_)
        store(th, tl, dot3(pair, load(ah, al)))
        a_ref[...] = dot3(pair, load(th, tl))
        return dot3(split(mine), pair)

    mine = lax.fori_loop(0, 2, step, mine)
    grads.turn()
    mine = lax.fori_loop(2, NS_ITERS - 1, step, mine)
    grads.pass_on()
    store(ph, pl_, poly())
    mine = dot3(split(mine), load(ph, pl_))
    side = jnp.where(x == 0, math.sqrt(1536.0), jnp.where(x == 1, math.sqrt(512.0), math.sqrt(2048.0)))
    mine = mine * (0.2 * side)
    mine = jnp.concatenate(
        [jnp.where(x == 1, mine[0:16] + mine[16:32], mine[0:16]), mine[16:64]], axis=0
    ).astype(bf16)
    for k in range(4):
        by_lanes = mine[:, 128 * k : 128 * k + 128]
        by_rows = jnp.concatenate(
            [mine[16 * k : 16 * k + 16, 128 * b : 128 * b + 128] for b in range(4)], axis=0
        )
        os[k] = jnp.where(x == 3, by_rows, by_lanes)
    cps = []
    for d in (1, 2, 3):
        cps.append(send(os.at[(x + d) % 4], rows.at[x], xs.at[d - 1], xr.at[d - 1], moved("x", d)))
    rows[x] = os[x]
    grads.end()
    for cp in cps:
        cp.wait()
    oa[y, z, s, 0:48] = rows[0, 0:48]
    oa[y, z, s, 48:64] = rows[1, 0:16]
    oa[y, z, s, 64:128] = rows[2]
    oa[y, z, s, 128:192] = rows[3]
    update = Gather(
        [
            (lambda a, b, e: oa.at[a, b, e, pl.ds(0, 96)], True),
            (lambda a, b, e: oa.at[a, b, e, pl.ds(96, 96)], False),
        ],
        r.se, r.re,
    )
    update.begin()
    update.turn()
    update.pass_on()
    update.end()


def scratch_list():
    V = pltpu.VMEM
    piece = (HEADS, TOK, 128)
    out = [
        ("fq", V((128, 1536), f32)), ("fo", V((128, 512), f32)),
        ("fi", V((128, 2048), f32)), ("ff", V((512, 512), f32)),
        ("x", V((TOK, D), bf16)), ("dy", V((TOK, D), bf16)),
        ("w1", V((4, 4, 4, 2, 64, 128), bf16)), ("w2", V((4, 4, 4, 2, 64, 128), bf16)),
        ("w3", V((4, 4, 4, 2, 16, 512), bf16)),
        ("kvs", V(piece, bf16)), ("qds", V(piece, bf16)),
        ("kv", V((GROUP, 128), bf16)), ("qd", V((NQB, QB, 128), bf16)),
        ("hid", V((TOK, D), bf16)), ("wide_f", V((TOK, D), f32)),
        ("co", V((TOK, 128), f32)), ("s1", V((TOK, 128), f32)), ("s2", V((TOK, 128), f32)),
        ("res", V((TOK, D), f32)), ("dh", V((TOK, D), f32)),
        ("gm", V((4, 4, 2, 4, 128, 128), bf16)),
        ("rcm", V((4, 4, 4, 128, 128), bf16)), ("hbuf", V((4, 4, 4, 128, 128), bf16)),
        ("kvt", V((128, GROUP), bf16)), ("acc", V((GROUP, 128), f32)),
        ("s_sc", V((GROUP, QB), f32)), ("p_sc", V((GROUP, QB), f32)),
        ("m_sc", V((GROUP // HB, 8, QB), f32)), ("cqs", V((NQB, QB, 128), bf16)),
        ("half", V((16, TOK, 128), bf16)), ("other", V((16, TOK, 128), bf16)),
        ("both", V((16, TOK, 128), bf16)),
        ("spare", V((6, 64, 128), bf16)),
        ("cq", V(piece, bf16)), ("kr", V((HEADS, 2, TOK, 128), bf16)),
        ("dqkv", V((TOK, 1536), bf16)),
        ("mwin", V((128, 512), f32)), ("mtr", V((512, 128), f32)), ("mfin", V((16, 512), f32)),
        ("gx", V((192, 128), f32)),
        ("us", V((4, 64, 128), bf16)), ("ur", V((4, 64, 128), bf16)),
        ("os", V((4, 64, 128), bf16)), ("rows", V((4, 64, 128), bf16)),
        ("v0", V((16, 512), f32)), ("v1", V((16, 512), f32)),
        ("vy", V((4, 16, 512), f32)), ("vz", V((4, 16, 512), f32)), ("vx", V((4, 16, 512), f32)),
        ("a", V((512, 512), f32)),
    ]
    out += [(k, V((512, 512), bf16)) for k in ("ah", "al", "ph", "pl", "th", "tl", "uh", "ul")]
    for name, shape in (
        ("lsem", (6,)), ("msem", (4,)), ("xs", (5, 3)), ("xr", (5, 3)), ("ys", (3, 3)), ("yr", (3, 3)),
        ("sa", (2, 3)), ("ra", (2, 5)), ("sb", (2, 3)), ("rb", (2, 5)),
        ("se", (2, 3)), ("re", (2, 5)),
        ("own_sem", None), ("ks", None), ("kvr", None), ("qs", None), ("qr", None),
        ("cs", None), ("cr", None),
        ("m_s", (2,)), ("m_r", (2,)), ("ms", (3, 3)), ("mr", (3, 3)), ("as_", (3, 3)), ("ar", (3, 3)),
        ("ws", (6,)), ("wr", (6,)), ("bs", None), ("br", None), ("rqs", None), ("rqr", None),
        ("vs", (10,)), ("vr", (10,)), ("us_s", (3,)), ("us_r", (3,)), ("os_s", (3,)), ("os_r", (3,)),
    ):
        out.append((name, DMA if shape is None else DMA(shape)))
    out += [(f"mlp{i}", v) for i, v in enumerate(Reduce.scratch(MLP_PARTS))]
    out += [(f"att{i}", v) for i, v in enumerate(Reduce.scratch(ATT_PARTS))]
    return out


INPUTS = (
    "starts", "x_in", "dy_in", "gain", "shift", "bias", "wq", "wo", "wi", "wf", "mq", "mo", "mi", "mf",
)
OUTPUTS = ("out", "gt", "gxa", "oa", "vec")


def step_kernel(names, *refs):
    r = types.SimpleNamespace(**dict(zip(names, refs)))
    r.mlp_bufs = [getattr(r, f"mlp{i}") for i in range(5 * len(MLP_PARTS))]
    r.att_bufs = [getattr(r, f"att{i}") for i in range(5 * len(ATT_PARTS))]
    chip = front_phase(r)
    back_phase(r, attention_phase(r, chip))
    newton_phase(r)


def train_step(*args):
    scratch = scratch_list()
    names = INPUTS + OUTPUTS + tuple(k for k, _ in scratch)
    return pl.pallas_call(
        functools.partial(step_kernel, names),
        out_shape=tuple(
            jax.ShapeDtypeStruct(shape, t)
            for shape, t in (
                ((TOK, D), bf16), ((TOK, D), f32),
                ((4, 4, 2, 192, 128), bf16), ((4, 4, 2, 192, 128), bf16), ((16, 512), f32),
            )
        ),
        in_specs=[SM, ANY, ANY, VM, VM, VM] + [ANY] * 8,
        out_specs=(VM,) * 5,
        scratch_shapes=[v for _, v in scratch],
        compiler_params=pltpu.CompilerParams(
            vmem_limit_bytes=63 * 2**20, collective_id=1, has_side_effects=True
        ),
        name="train_step",
    )(*args)


def update_kernel(
    gx, oa, out, gt, wq, wo, wi, wf, mq, mo, mi, mf, vec, vm, gain, shift, bias,
    out_to, gt_to, nmq, nwq, nmo, nwo, nmi, nwi, nmf, nwf, nvm, nvec,
):
    out_to[...] = out[...]
    gt_to[...] = gt[...]

    @pl.when(pl.program_id(0) == 0)
    def _():
        for k in range(11):
            part = slice(512 * k, 512 * k + 512)
            v = VMU * vm[part] + vec[k]
            old = (gain[...], shift[...])[k] if k < 2 else bias[512 * k - 1024 : 512 * k - 512]
            nvm[part] = v
            nvec[part] = old - VLR * v

    for lo, n, w, m, nm, nw in (
        (0, 48, wq, mq, nmq, nwq),
        (48, 16, wo, mo, nmo, nwo),
        (64, 64, wi, mi, nmi, nwi),
    ):
        grad = gx[:, lo : lo + n, :].astype(f32).reshape(8 * n, 128).T
        turned = oa[:, lo : lo + n, :].astype(f32).reshape(8 * n, 128).T
        nm[...] = MU * m[...] + grad
        nw[...] = (1.0 - LR * WD) * w[...] - LR * turned
    for b in range(4):
        cols = slice(128 * b, 128 * b + 128)
        rows = slice(128 + 16 * b, 144 + 16 * b)
        grad = gx[:, rows, :].astype(f32).reshape(128, 128)
        turned = oa[:, rows, :].astype(f32).reshape(128, 128)
        nmf[:, cols] = MU * mf[:, cols] + grad
        nwf[:, cols] = (1.0 - LR * WD) * wf[:, cols] - LR * turned


def update(gx, oa, out, gt, weights, moments, vec, vec_mom, gain, shift, biases):
    def whole(v):
        return pl.BlockSpec(v.shape, lambda i, n=v.ndim: (0,) * n)

    piece = pl.BlockSpec((8, 192, 128), lambda i: (i, 0, 0))
    rows = pl.BlockSpec((48, D), lambda i: (i, 0))
    blocks = [
        pl.BlockSpec((128, 384), lambda i: (0, i)),
        pl.BlockSpec((128, 128), lambda i: (0, i)),
        pl.BlockSpec((128, 512), lambda i: (0, i)),
        pl.BlockSpec((128, 512), lambda i: (i, 0)),
    ]
    shape = lambda v: jax.ShapeDtypeStruct(v.shape, v.dtype)
    outs, specs = [shape(out), shape(gt)], [rows, rows]
    for w, b in zip(weights, blocks):
        outs += [shape(w)] * 2
        specs += [b, b]
    outs += [shape(vec_mom)] * 2
    specs += [whole(vec_mom)] * 2
    vectors = (vec, vec_mom, gain, shift, biases)
    return pl.pallas_call(
        update_kernel,
        grid=(4,),
        out_shape=tuple(outs),
        in_specs=[piece, piece, rows, rows] + blocks + blocks + [whole(v) for v in vectors],
        out_specs=tuple(specs),
        compiler_params=pltpu.CompilerParams(vmem_limit_bytes=60 * 2**20),
        name="update_weights",
    )(gx, oa, out, gt, *weights, *moments, *vectors)


def body(
    tokens, cotangent, ln_gain, ln_bias, biases, w_qkv, w_out, w_in, w_fin,
    mom_qkv, mom_out, mom_in, mom_fin, vec_mom, starts,
):
    weights = (w_qkv, w_out, w_in, w_fin)
    moments = (mom_qkv, mom_out, mom_in, mom_fin)
    block_out, grad_tokens, gx, oa, vec_sum = train_step(
        starts, tokens, cotangent, ln_gain[None, :], ln_bias[None, :], biases, *weights, *moments
    )
    return update(
        gx.reshape(32, 192, 128), oa.reshape(32, 192, 128), block_out, grad_tokens,
        weights, moments, vec_sum, vec_mom, ln_gain, ln_bias, biases,
    )


def solution(mesh):
    tok = P(("wsh", "ctx"), None)
    row = P("wsh", None)
    return jax.shard_map(
        body,
        mesh=mesh,
        in_specs=(tok, tok, P(), P(), P()) + (row,) * 8 + (P(), P()),
        out_specs=(tok, tok) + (row,) * 8 + (P(), P()),
        check_vma=False,
    )
```

```python
import functools
import math
import types

import jax
import jax.numpy as jnp
from jax import lax
from jax.experimental import pallas as pl
from jax.experimental.pallas import tpu as pltpu
from jax.sharding import PartitionSpec as P

f32 = jnp.float32
bf16 = jnp.bfloat16
MESH = pl.DeviceIdType.MESH
HEADS = 8
HD = 64
ROT = 16
D = 512
TOK = 192
GROUP = 6144
QB = 256
NQB = 6
HB = 128
UU = 8
TT = 4
NS_ITERS = 5
C1, C2, C3 = 3.4445, -4.775, 2.0315
MU, LR, WD = 0.95, 0.6, 0.01
VMU, VLR = 0.9, 0.0005
R_QKV, R_OUT, R_IN, R_FIN = 48, 16, 64, 64

VM = pl.BlockSpec(memory_space=pltpu.VMEM)
SM = pl.BlockSpec(memory_space=pltpu.SMEM)
ANY = pl.BlockSpec(memory_space=pl.ANY)
DMA = pltpu.SemaphoreType.DMA


def dot(a, b):
    return jnp.dot(a, b, preferred_element_type=f32)


def dot_nt(a, b):
    return lax.dot_general(a, b, (((1,), (1,)), ((), ())), preferred_element_type=f32)


def dot_tn(a, b):
    return lax.dot_general(a, b, (((0,), (0,)), ((), ())), preferred_element_type=f32)


def coords():
    c = lax.axis_index("ctx")
    return c // 8, (c // 2) % 4, c % 2, lax.axis_index("wsh")


def at(y, z, s, x):
    return {"ctx": (y * 4 + z) * 2 + s, "wsh": x}


def tell(partners):
    sem = pltpu.get_barrier_semaphore()
    for p in partners:
        pl.semaphore_signal(sem, inc=1, device_id=p, device_id_type=MESH)


def tell_slab():
    c = lax.axis_index("ctx")
    sem = pltpu.get_barrier_semaphore()

    def one(d, _):
        pl.semaphore_signal(
            sem, inc=1, device_id={"ctx": lax.rem(c + d, 32)}, device_id_type=MESH
        )
        return 0

    lax.fori_loop(1, 32, one, 0)


def met(count):
    pl.semaphore_wait(pltpu.get_barrier_semaphore(), count)


def wait_for(ref, sem):
    pltpu.make_async_copy(ref, ref, sem).wait()


def loop(lo, hi, f):
    def step(i, _):
        f(i)
        return 0

    lax.fori_loop(lo, hi, step, 0)


AXES = ("y", "z", "x")


def moved(axis, d):
    y, z, s, x = coords()
    if axis == "y":
        return at((y + d) % 4, z, s, x)
    if axis == "z":
        return at(y, (z + d) % 4, s, x)
    return at(y, z, s, (x + d) % 4)


def other_core():
    y, z, s, x = coords()
    return at(y, z, 1 - s, x)


def lines(axes=AXES):
    return [moved(a, d) for a in axes for d in (1, 2, 3)]


def send(src, dst, ss, rs, dev):
    cp = pltpu.make_async_remote_copy(
        src_ref=src, dst_ref=dst, send_sem=ss, recv_sem=rs, device_id=dev, device_id_type=MESH
    )
    cp.start()
    return cp


ALL = slice(None)


class Gather:
    def __init__(self, items, ss, rs):
        self.items, self.ss, self.rs = items, ss, rs

    def begin(self):
        y, z, s, x = coords()
        for i, (get, y_first) in enumerate(self.items):
            piece = get(y, z, s)
            for d in (1, 2, 3):
                send(
                    piece, piece, self.ss.at[i, 0], self.rs.at[i, 0], moved("y" if y_first else "z", d)
                )

    def turn(self):
        y, z, s, x = coords()
        three = pl.ds(0, 3)
        for i, (get, y_first) in enumerate(self.items):
            pieces = get(three, z, s) if y_first else get(y, three, s)
            wait_for(pieces, self.ss.at[i, 0])
            wait_for(pieces, self.rs.at[i, 0])
        self.second = {}
        for i, (get, y_first) in enumerate(self.items):
            piece = get(ALL, z, s) if y_first else get(y, ALL, s)
            for d in (1, 2, 3):
                to = moved("z" if y_first else "y", d)
                self.second[i, d] = send(piece, piece, self.ss.at[i, 1], self.rs.at[i, d], to)
        for i, (get, y_first) in enumerate(self.items):
            piece = get(ALL, z, s) if y_first else get(y, ALL, s)
            send(piece, piece, self.ss.at[i, 2], self.rs.at[i, 4], other_core())

    def pass_on(self):
        y, z, s, x = coords()
        for d in (1, 3, 2):
            for i, (get, y_first) in enumerate(self.items):
                self.second[i, d].wait_recv()
                piece = get(ALL, (z - d) % 4, s) if y_first else get((y - d) % 4, ALL, s)
                send(piece, piece, self.ss.at[i, 2], self.rs.at[i, 4], other_core())

    def end(self):
        three = pl.ds(0, 3)
        for i, (get, y_first) in enumerate(self.items):
            wait_for(get(ALL, three, 0) if y_first else get(three, ALL, 0), self.ss.at[i, 1])
            wait_for(get(ALL, ALL, 0), self.ss.at[i, 2])
            wait_for(get(ALL, ALL, 0), self.rs.at[i, 4])


def split(v):
    hi = v.astype(bf16)
    return hi, (v - hi.astype(f32)).astype(bf16)


class Reduce:
    def __init__(self, src, parts, bufs, ss, rs):
        self.src, self.parts, self.ss, self.rs = src, parts, ss, rs
        y, z, s, x = coords()
        self.me = {"y": y, "z": z, "x": x}
        self.bufs = [bufs[5 * i : 5 * i + 5] for i in range(len(parts))]

    @staticmethod
    def scratch(parts):
        out = []
        for lo, n, order, paired in parts:
            out += [
                pltpu.VMEM((3, 4, 4, n, 128), bf16),
                pltpu.VMEM((4, 4, n, 128), bf16),
                pltpu.VMEM((3, 4, n, 128), bf16),
                pltpu.VMEM((4, n, 128), bf16),
                pltpu.VMEM((3, n, 128), bf16),
            ]
        return out

    @staticmethod
    def summed(pieces, paired):
        v = functools.reduce(lambda a, b: a + b, [p.astype(f32) for p in pieces])
        if not paired:
            return v.astype(bf16)
        half = v.shape[-2] // 2
        return jnp.concatenate(split(v[..., :half, :] + v[..., half:, :]), axis=-2)

    def begin(self, stage):
        for d in (2, 1, 3):
            for i, (lo, n, order, paired) in enumerate(self.parts):
                r1, h1, r2, h2, r3 = self.bufs[i]
                axis = order[stage]
                place = (self.me[axis] + d) % 4
                left = [a for a in AXES if a not in order[:stage]]
                index = tuple(place if a == axis else ALL for a in left)
                if stage == 0:
                    src = self.src.at[index + (pl.ds(lo, n),)]
                else:
                    src = (h1, h2)[stage - 1].at[index]
                send(
                    src, (r1, r2, r3)[stage].at[d - 1],
                    self.ss.at[stage, i], self.rs.at[stage, i], moved(axis, d),
                )

    def end(self, stage):
        out = []
        for i, (lo, n, order, paired) in enumerate(self.parts):
            r1, h1, r2, h2, r3 = self.bufs[i]
            wait_for((r1, r2, r3)[stage], self.ss.at[stage, i])
            wait_for((r1, r2, r3)[stage], self.rs.at[stage, i])
            mine = self.me[order[stage]]
            if stage == 0:
                axis = AXES.index(order[0])

                def add(a, _, axis=axis, mine=mine, lo=lo, n=n, paired=paired, r1=r1, h1=h1):
                    index = [a, ALL]
                    index.insert(axis, mine)
                    own = self.src[tuple(index) + (slice(lo, lo + n),)]
                    h1[a] = self.summed([own, r1[0, a], r1[1, a], r1[2, a]], paired)
                    return 0

                lax.fori_loop(0, 4, add, 0)
            elif stage == 1:
                left = [a for a in AXES if a != order[0]]
                first = left.index(order[1]) == 0
                own = h1[mine] if first else h1[:, mine]
                h2[...] = self.summed([own, r2[0], r2[1], r2[2]], paired)
            else:
                v = h2[mine].astype(f32) + r3[0].astype(f32) + r3[1].astype(f32) + r3[2].astype(f32)
                if paired:
                    v = v[: n // 2] + v[n // 2 :]
                out.append(v)
        return out


MLP_PARTS = ((0, 48, ("y", "z", "x"), False), (48, 48, ("z", "x", "y"), False), (96, 32, ("x", "y", "z"), False))
ATT_PARTS = ((0, 32, ("y", "z", "x"), False), (32, 16, ("z", "x", "y"), False), (48, 32, ("x", "y", "z"), True))


def norm_parts(x_ref, gain, shift):
    xf = x_ref[...].astype(f32)
    centered = xf - jnp.mean(xf, axis=1, keepdims=True)
    inv = lax.rsqrt(jnp.mean(centered * centered, axis=1, keepdims=True) + 1e-05)
    normed = centered * inv
    hidden = (normed * gain + shift).astype(bf16)
    return xf, inv, normed, hidden


def turn(v, co, s1, s2):
    return v * co + pltpu.roll(v, 120, 1) * s1 + pltpu.roll(v, 8, 1) * s2


def rolled(ref, x):
    parts = [ref[:, pl.ds(pl.multiple_of((x + d) % 4 * 128, 128), 128)] for d in range(4)]
    return jnp.concatenate(parts, axis=1)


def unroll(v, ref, x):
    for d in range(4):
        ref[:, pl.ds(pl.multiple_of((x + d) % 4 * 128, 128), 128)] = v[:, 128 * d : 128 * d + 128]
    return ref[...]


def rotary(starts_ref, x, c):
    bnd = starts_ref[x] - x * GROUP
    place = c * TOK + lax.broadcasted_iota(jnp.int32, (TOK, 128), 0)
    pos = (place - jnp.where(place >= bnd, bnd, 0)).astype(f32)
    lane = lax.broadcasted_iota(jnp.int32, (TOK, 128), 1) % HD
    freq = jnp.zeros((TOK, 128), f32)
    for i in range(ROT // 2):
        freq = jnp.where(lane % 8 == i, 10000.0 ** (-2.0 * i / ROT), freq)
    angle = pos * jnp.where(lane < ROT, freq, 0.0)
    co, si = jnp.cos(angle), jnp.sin(angle)
    return co, jnp.where(lane < 8, -si, 0.0), jnp.where(lane < 8, 0.0, si)


def wide(w, first, count):
    blocks = [w[(first + i) // 4, (first + i) % 4].reshape(512, 128) for i in range(count)]
    return jnp.concatenate(blocks, axis=1) if count > 1 else blocks[0]


def query_home(piece):
    block = piece // 4
    part = block % 8
    low = part < 4
    return jnp.where(low, part, 7 - part), 2 * (block // 8) + jnp.where(low, 0, 1), piece % 4


def query_block(t, j):
    if isinstance(t, int):
        return 8 * (t // 2) + (j if t % 2 == 0 else 7 - j)
    return 8 * (t // 2) + jnp.where(t % 2 == 0, j, 7 - j)


def front_phase(r):
    y, z, s, x = coords()
    c = lax.axis_index("ctx")
    p = c // 2
    w1, w2, w3, kvs, qds, kv, qd = r.w1, r.w2, r.w3, r.kvs, r.qds, r.kv, r.qd
    ks, kr, qs, qr, cs, cr = r.ks, r.kvr, r.qs, r.qr, r.cs, r.cr
    bias_ref = r.bias
    tell_slab()
    tell(lines(("x",)))
    loads = [
        pltpu.make_async_copy(src, dst, r.lsem.at[k])
        for k, (src, dst) in enumerate(
            ((r.wq, r.fq), (r.wo, r.fo), (r.wi, r.fi), (r.wf, r.ff), (r.x_in, r.x), (r.dy_in, r.dy))
        )
    ]
    for cp in loads:
        cp.start()
    momenta_begin(r)
    for cp in loads:
        cp.wait()
    for b in range(16):
        w = r.fq[:, 128 * b : 128 * b + 128] if b < 12 else r.fo[:, 128 * b - 1536 : 128 * b - 1408]
        w1[b // 4, b % 4, 0] = w.astype(bf16).reshape(2, 64, 128)
        w2[b // 4, b % 4, 0] = r.fi[:, 128 * b : 128 * b + 128].astype(bf16).reshape(2, 64, 128)
    w3[0] = r.ff[...].astype(bf16).reshape(4, 4, 2, 16, 512)
    met(34)
    slab, direct = pl.ds(0, 32), pl.ds(32, 32)

    def along_x(k, piece):
        return [
            send(piece(0), piece(4 - d), r.xs.at[k, d - 1], r.xr.at[k, d - 1], moved("x", d))
            for d in (1, 2, 3)
        ]

    low, high = pl.ds(0, 256), pl.ds(256, 256)
    own_cps = along_x(0, lambda d: w1.at[y, z, d, s, slab])
    late_cps = along_x(4, lambda d: w3.at[d, y, z, s, :, high])
    direct_cps = along_x(1, lambda d: w1.at[:, :, d, s, direct])
    co, s1, s2 = rotary(r.starts, x, c)
    r.co[...], r.s1[...], r.s2[...] = co, s1, s2
    xf, inv, normed, hidden = norm_parts(r.x, r.gain[...], r.shift[...])
    r.hid[...] = hidden
    hidden_r = rolled(r.hid, x)
    dy = r.dy[...]
    for cp in own_cps:
        cp.wait()
    others = pl.ds(1, 3)
    early = Gather(
        [
            (lambda a, b, e: w1.at[a, b, others, e, pl.ds(0, 16)], True),
            (lambda a, b, e: w1.at[a, b, others, e, pl.ds(16, 16)], False),
        ],
        r.sa, r.ra,
    )
    late = Gather(
        [
            (lambda a, b, e: w3.at[others, a, b, e, :, pl.ds(256, 128)], True),
            (lambda a, b, e: w3.at[others, a, b, e, :, pl.ds(384, 128)], False),
        ],
        r.sb, r.rb,
    )

    def to_core(k, cps, piece):
        out = []
        for d in (1, 3, 2):
            cps[d - 1].wait_recv()
            got = piece(4 - d)
            out.append(send(got, got, r.ys.at[k, d - 1], r.yr.at[k, d - 1], other_core()))
        for cp in cps:
            cp.wait_send()
        return out

    early.begin()
    early.turn()
    passed = to_core(0, direct_cps, lambda d: w1.at[:, :, d, s, direct])
    in_cps = along_x(2, lambda d: w2.at[:, :, d, s])
    fin_cps = along_x(3, lambda d: w3.at[d, :, :, s, :, low])
    early.pass_on()
    for cp in late_cps:
        cp.wait()
    late.begin()
    early.end()
    for cp in passed:
        cp.wait()
    left = lax.broadcasted_iota(jnp.int32, (TOK, 128), 1) < 64
    dctx = unroll(dot_nt(dy, wide(w1, 12, 4)), r.wide_f, x)
    for half in range(2):
        thirds = []
        for third in range(3):
            b = third * 4 + 2 * half
            thirds.append(dot(hidden_r, wide(w1, b, 2)) + bias_ref[b * 128 : b * 128 + 256][None, :])
        for e in range(2):
            lanes = slice(128 * e, 128 * e + 128)
            q = turn(thirds[0][:, lanes], co, s1, s2).astype(bf16).astype(f32) * 0.125
            k = turn(thirds[1][:, lanes], co, s1, s2)
            v = thirds[2][:, lanes]
            pair = 2 * half + e
            g = dctx[:, pair * 128 : pair * 128 + 128]
            h = 2 * pair
            kvs[h] = jnp.where(left, k, pltpu.roll(v, 64, 1)).astype(bf16)
            kvs[h + 1] = jnp.where(left, pltpu.roll(k, 64, 1), v).astype(bf16)
            qds[h] = jnp.where(left, q, pltpu.roll(g, 64, 1)).astype(bf16)
            qds[h + 1] = jnp.where(left, pltpu.roll(q, 64, 1), g).astype(bf16)

    def kv_copy(d):
        to = lax.rem(p + d, 16)
        return pltpu.make_async_remote_copy(
            src_ref=kvs.at[to // 2], dst_ref=kv.at[pl.ds(c * TOK, TOK)], send_sem=ks, recv_sem=kr,
            device_id={"ctx": to * 2 + s}, device_id_type=MESH,
        )

    def across(d):
        block = kv.at[pl.ds((lax.rem(p + 16 - d, 16) * 2 + s) * TOK, TOK)]
        return pltpu.make_async_remote_copy(
            src_ref=block, dst_ref=block, send_sem=cs, recv_sem=cr,
            device_id={"ctx": p * 2 + 1 - s}, device_id_type=MESH,
        )

    def each_query(k):
        h, i = k // 3, k % 3
        j, t, quarter = query_home(3 * c + i)
        to = 4 * h + j
        src = qds.at[h, pl.ds(64 * i, 64)]
        dst = qd.at[t, pl.ds(64 * quarter, 64)]

        @pl.when(to == c)
        def _():
            pltpu.make_async_copy(src, dst, qr).start()
            pltpu.make_async_copy(src, r.spare.at[i], qs).start()

        @pl.when(to != c)
        def _():
            pltpu.make_async_remote_copy(
                src_ref=src, dst_ref=dst, send_sem=qs, recv_sem=qr,
                device_id={"ctx": to}, device_id_type=MESH,
            ).start()

    own = pltpu.make_async_copy(kvs.at[p // 2], kv.at[pl.ds(c * TOK, TOK)], r.own_sem)
    own.start()
    late.turn()
    loop(1, 16, lambda d: kv_copy(d).start())
    loop(0, 24, each_query)
    own.wait()

    r.acc[...] = jnp.zeros_like(r.acc)
    late.pass_on()
    late.end()
    passed = to_core(1, in_cps, lambda d: w2.at[:, :, d, s])
    passed += to_core(2, fin_cps, lambda d: w3.at[d, :, :, s, :, low])
    for cp in passed:
        cp.wait()
    root = math.sqrt(2.0 / math.pi)
    mlp = jnp.zeros((TOK, D), f32)
    dh = jnp.zeros((TOK, D), f32)
    for i in range(4):
        if i == 2:
            wait_for(kv.at[pl.ds(0, 15 * TOK)], kr)
            loop(0, 16, lambda d: across(d).start())
        w_in = wide(w2, 4 * i, 4)
        w_fin = w3[(i + 4 - x) % 4].reshape(512, 512)
        pre = dot(hidden_r, w_in) + bias_ref[2048 + 512 * i : 2560 + 512 * i][None, :]
        sq = pre * pre
        th = jnp.tanh(root * (pre + 0.044715 * (pre * sq)))
        act = (0.5 * pre * (1.0 + th)).astype(bf16)
        slope = 0.5 * (1.0 + th) + (0.5 * root) * pre * (1.0 - th * th) * (
            1.0 + (3.0 * 0.044715) * sq
        )
        dpre = (dot_nt(dy, w_fin) * slope).astype(bf16)
        mlp = mlp + dot(act, w_fin)
        dh = dh + dot_nt(dpre, w_in)
        r.v0[6 + i : 7 + i, :] = jnp.sum(dpre.astype(f32), axis=0, keepdims=True)
        g_in = dot_tn(dpre, hidden).astype(bf16).reshape(4, 2, 64, 512)
        g_fin = dot_tn(act, dy).astype(bf16).reshape(4, 4, 2, 16, 512)
        for b in range(4):
            lanes = slice(128 * b, 128 * b + 128)
            r.gm[i, :, :, b, 0:64] = g_in[..., lanes]
            r.gm[:, :, :, i, 64 + 16 * b : 80 + 16 * b] = g_fin[..., lanes]
    r.res[...] = xf + mlp + (bias_ref[4096:4608] + bias_ref[1536:2048])[None, :]
    r.dh[...] = dh
    chip = send(r.gm.at[:, :, 1 - s], r.rcm, r.m_s.at[0], r.m_r.at[0], other_core())
    wait_for(kv.at[pl.ds(0, 15 * TOK)], ks)
    wait_for(qd, qs)
    wait_for(qd, qr)
    wait_for(kv.at[pl.ds(0, 16 * TOK)], cs)
    wait_for(kv.at[pl.ds(0, 16 * TOK)], cr)
    return chip


RETURNS = ((14, 16), (11, 14), (8, 11), (6, 8), (3, 6), (0, 3))


def attention_phase(r, chip):
    kvt, acc, s_sc, p_sc, m_sc, cqs = r.kvt, r.acc, r.s_sc, r.p_sc, r.m_sc, r.cqs
    half, other, both, rcm, hbuf = r.half, r.other, r.both, r.rcm, r.hbuf
    cq, kr, kv_ref, qd_ref, gm_ref = r.cq, r.kr, r.kv, r.qd, r.gm
    ws, wr, ss, sr, qs, qr = r.ws, r.wr, r.bs, r.br, r.rqs, r.rqr
    y, z, s, x = coords()
    c = lax.axis_index("ctx")
    p = c // 2
    h = c // 4
    j = c % 4
    n = kv_ref.shape[0]
    bnd = r.starts[x] - x * GROUP

    def prepare(i, _):
        o = pl.multiple_of(i * QB, QB)
        kvt[:, pl.ds(o, QB)] = kv_ref[pl.ds(o, QB), :].T
        return 0

    lax.fori_loop(0, n // QB, prepare, 0)
    lane = lax.broadcasted_iota(jnp.int32, (QB, 128), 1)

    def block(t):
        qb = query_block(t, j)
        qd = qd_ref[t]
        w1 = jnp.where(lane < 64, qd, jnp.zeros_like(qd))
        w2 = jnp.where(lane < 64, jnp.zeros_like(qd), qd)
        q_t = w1.T
        d_t = w2.T

        def scores(kt, masked, carry, tiles, first=False):
            m8, l8, r8 = carry
            for u in range(2 * tiles):
                o = pl.multiple_of(kt * QB + u * HB, HB)
                rows = kv_ref[pl.ds(o, HB), :]
                s = dot(rows, q_t)
                if masked and not (first and u > 1):
                    kp = o + lax.broadcasted_iota(jnp.int32, (HB, QB), 0)
                    qp = qb * QB + lax.broadcasted_iota(jnp.int32, (HB, QB), 1)
                    s = jnp.where((kp <= qp) & ((kp >= bnd) == (qp >= bnd)), s, -1e30)
                s = s.reshape(HB // 8, 8, QB)
                dp = dot(rows, d_t)
                p_sc[pl.ds(o, HB), :] = dp
                mn = jnp.maximum(m8, jnp.max(s, axis=0))
                e = jnp.exp(s - mn[None])
                s_sc[pl.ds(o, HB), :] = e.reshape(HB, QB)
                m_sc[2 * kt + u] = mn
                al = jnp.exp(m8 - mn)
                l8 = l8 * al + jnp.sum(e, axis=0)
                r8 = r8 * al + jnp.sum(e * dp.reshape(HB // 8, 8, QB), axis=0)
                m8 = mn
            return m8, l8, r8

        zero = jnp.zeros((8, QB), f32)
        base = t // 2 * 8
        tail = (qb - base) // TT + 1
        carry = lax.fori_loop(
            0, tail, lambda g, c: scores(base + TT * g, True, c, TT),
            (jnp.full((8, QB), -1e30, f32), zero, zero),
        )
        if base > 0:
            carry = scores(0, True, carry, UU, True)
        carry = lax.fori_loop(
            1, base // UU, lambda g, c: scores(g * UU, False, c, UU), carry
        )
        m8, l8, r8 = carry
        m = jnp.max(m8, axis=0, keepdims=True)
        w = jnp.exp(m8 - m)
        l = jnp.sum(l8 * w, axis=0, keepdims=True)
        lse = m + jnp.log(l)
        rd = jnp.sum(r8 * w, axis=0, keepdims=True) / l

        def grads(kt, carry, tiles):
            c_t, g_t = carry
            for u in range(tiles):
                o = pl.multiple_of((kt + u) * QB, QB)
                e = s_sc[pl.ds(o, QB), :].reshape(2, HB // 8, 8, QB)
                w0 = jnp.exp(m_sc[2 * (kt + u)] - lse)
                w1_ = jnp.exp(m_sc[2 * (kt + u) + 1] - lse)
                p = jnp.concatenate([e[0] * w0[None], e[1] * w1_[None]], axis=0).reshape(QB, QB)
                pb = p.astype(bf16)
                ds = (p * (p_sc[pl.ds(o, QB), :] - rd)).astype(bf16)
                c_t = c_t + dot(kvt[64:128, pl.ds(o, QB)], pb)
                g_t = g_t + dot(kvt[0:64, pl.ds(o, QB)], ds)
                acc[pl.ds(o, QB), :] += dot(ds, w1) + dot(pb, w2)
            return c_t, g_t

        z = jnp.zeros((64, QB), f32)
        c = lax.fori_loop(0, base // UU, lambda g, c: grads(g * UU, c, UU), (z, z))
        c_t, g_t = lax.fori_loop(0, tail, lambda g, c: grads(base + TT * g, c, TT), c)
        cqs[t] = jnp.concatenate([g_t * 0.125, c_t], axis=0).T.astype(bf16)

    def each_query(t, quarter):
        piece = 4 * query_block(t, j) + quarter
        to, i = piece // 3, piece % 3
        src = cqs.at[t, pl.ds(64 * quarter, 64)]
        dst = cq.at[h, pl.ds(64 * i, 64)]

        @pl.when(to == c)
        def _():
            pltpu.make_async_copy(src, dst, qr).start()
            pltpu.make_async_copy(src, r.spare.at[3 + i], qs).start()

        @pl.when(to != c)
        def _():
            pltpu.make_async_remote_copy(
                src_ref=src, dst_ref=dst, send_sem=qs, recv_sem=qr,
                device_id={"ctx": to}, device_id_type=MESH,
            ).start()

    def return_queries(t):
        loop(0, 4, lambda quarter: each_query(t, quarter))

    swaps = {}

    def exchange(g):
        lo, hi = RETURNS[g]

        def low(i):
            o = pl.multiple_of((2 * i + 1 - s) * TOK, TOK)
            half[i] = acc[pl.ds(o, TOK), :].astype(bf16)

        loop(lo, hi, low)
        part = pl.ds(lo, hi - lo)
        swaps[g] = send(half.at[part], other.at[part], ws.at[g], wr.at[g], other_core())

    def block_copy(i):
        return pltpu.make_async_remote_copy(
            src_ref=both.at[i], dst_ref=kr.at[h, p % 2], send_sem=ss, recv_sem=sr,
            device_id={"ctx": i * 2 + s}, device_id_type=MESH,
        )

    def push(g):
        lo, hi = RETURNS[g]
        swaps[g].wait()

        def one(i):
            o = pl.multiple_of((2 * i + s) * TOK, TOK)
            both[i] = (acc[pl.ds(o, TOK), :] + other[i].astype(f32)).astype(bf16)

            @pl.when(i == p)
            def _():
                pltpu.make_async_copy(both.at[i], kr.at[h, p % 2], sr).start()

            @pl.when(i != p)
            def _():
                block_copy(i).start()

        loop(lo, hi, one)

    def add(i):
        a, b = i // 4, i % 4
        hbuf[a, b] = (gm_ref[a, b, s].astype(f32) + rcm[a, b].astype(f32)).astype(bf16)

    sums = Reduce(hbuf, MLP_PARTS, r.mlp_bufs, r.ms, r.mr)
    for k in range(NQB):
        block(NQB - 1 - k)
        return_queries(NQB - 1 - k)
        exchange(k)
        if k > 0:
            push(k - 1)
        if k == 0:
            chip.wait()
            loop(0, 16, add)
            sums.begin(0)
        if k == 3:
            sums.end(0)
            sums.begin(1)
    push(NQB - 1)
    wait_for(both.at[pl.ds(0, 15)], ss)
    wait_for(cq, qs)
    wait_for(cq, qr)
    wait_for(kr, sr)
    sums.end(1)
    sums.begin(2)
    return sums


def momenta_starts():
    c = lax.axis_index("ctx")
    return jnp.minimum(48 * c // 128, 10), 16 * c // 128, 64 * c // 128


def momenta_loads(r):
    c = lax.axis_index("ctx")
    starts = momenta_starts()
    loads = []
    for k, (m, width) in enumerate(((r.mq, 256), (r.mo, 128), (r.mi, 128))):
        first = pl.multiple_of(starts[k] * 128, 128)
        loads.append(
            pltpu.make_async_copy(
                m.at[:, pl.ds(first, width)],
                r.mwin.at[:, pl.ds((0, 256, 384)[k], width)],
                r.msem.at[k],
            )
        )
    loads.append(pltpu.make_async_copy(r.mf.at[pl.ds(16 * c, 16)], r.mfin, r.msem.at[3]))
    return loads


def momenta_begin(r):
    for cp in momenta_loads(r):
        cp.start()


def momenta(r):
    c = lax.axis_index("ctx")
    for cp in momenta_loads(r):
        cp.wait()
    r.mtr[...] = r.mwin[...].T
    offset = 48 * c - momenta_starts()[0] * 128
    return jnp.concatenate(
        [
            r.mtr[pl.ds(pl.multiple_of(offset, 16), 48), :],
            r.mtr[pl.ds(pl.multiple_of(256 + 16 * c % 128, 16), 16), :],
            r.mtr[pl.ds(pl.multiple_of(384 + 64 * c % 128, 64), 64), :],
        ]
        + [r.mfin[:, 128 * b : 128 * b + 128] for b in range(4)],
        axis=0,
    )


def leave(r, k):
    src, dst = ((r.out, r.out_to), (r.gt, r.gt_to), (r.gxa, r.gxa_to))[k]
    return pltpu.make_async_copy(src, dst, r.osem.at[k])


def back_phase(r, mlp_sums):
    dqkv, gx, us, ur, v0, v1, vy, vz, vx = r.dqkv, r.gx, r.us, r.ur, r.v0, r.v1, r.vy, r.vz, r.vx
    cq_ref, kr_ref, w1, ga, rcm, hbuf = r.cq, r.kr, r.w1, r.gm, r.rcm, r.hbuf
    vs, vr, xs, xr, ua = r.vs, r.vr, r.us_s, r.us_r, r.w3
    att = pl.ds(0, 80)
    y, z, s, x = coords()
    c = lax.axis_index("ctx")
    xf, inv, normed, hidden = norm_parts(r.x, r.gain[...], r.shift[...])
    dy = r.dy[...]
    co, s1, s2 = r.co[...], -r.s1[...], -r.s2[...]
    left = lax.broadcasted_iota(jnp.int32, (TOK, 128), 1) < 64
    ctx = []
    for pair in range(4):
        a = cq_ref[2 * pair].astype(f32)
        b = cq_ref[2 * pair + 1].astype(f32)
        e = kr_ref[2 * pair, 0].astype(f32) + kr_ref[2 * pair, 1].astype(f32)
        f = kr_ref[2 * pair + 1, 0].astype(f32) + kr_ref[2 * pair + 1, 1].astype(f32)
        dq = jnp.where(left, a, pltpu.roll(b, 64, 1))
        dk = jnp.where(left, e, pltpu.roll(f, 64, 1))
        dqkv[:, 128 * pair : 128 * pair + 128] = turn(dq, co, s1, s2).astype(bf16)
        dqkv[:, 512 + 128 * pair : 640 + 128 * pair] = turn(dk, co, s1, s2).astype(bf16)
        dqkv[:, 1024 + 128 * pair : 1152 + 128 * pair] = jnp.where(
            left, pltpu.roll(e, 64, 1), f
        ).astype(bf16)
        ctx.append(jnp.where(left, pltpu.roll(a, 64, 1), b).astype(bf16))
    ctx = jnp.concatenate(ctx, axis=1)
    r.hid[...] = ctx
    hi, lo = split(dot_tn(dy, ctx))
    hi, lo = hi.reshape(4, 4, 2, 16, 512), lo.reshape(4, 4, 2, 16, 512)
    for b in range(4):
        lanes = slice(128 * b, 128 * b + 128)
        ga[:, :, :, b, 48:64] = hi[..., lanes]
        ga[:, :, :, b, 64:80] = lo[..., lanes]
    for i in range(4):
        part = dqkv[:, 384 * i : 384 * i + 384]
        g = dot_tn(part, hidden).astype(bf16).reshape(4, 2, 48, 512)
        for b in range(4):
            ga[i, :, :, b, 0:48] = g[..., 128 * b : 128 * b + 128]
    chip = send(ga.at[:, :, 1 - s, :, att], rcm.at[:, :, :, att], r.m_s.at[1], r.m_r.at[1], other_core())
    r.out[...] = (r.res[...] + dot(rolled(r.hid, x), wide(w1, 12, 4))).astype(bf16)
    dh = r.dh[...]
    for third in range(3):
        part = dqkv[:, 512 * third : 512 * third + 512]
        dh = dh + dot_nt(part, wide(w1, 4 * third, 4))
        v0[2 + third : 3 + third, :] = jnp.sum(part.astype(f32), axis=0, keepdims=True)
    dh = unroll(dh, r.wide_f, x)
    scaled = dh * r.gain[...]
    dyf = dy.astype(f32)
    r.gt[...] = dyf + inv * (
        scaled
        - jnp.mean(scaled, axis=1, keepdims=True)
        - normed * jnp.mean(scaled * normed, axis=1, keepdims=True)
    )
    leave(r, 0).start()
    leave(r, 1).start()
    dsum = jnp.sum(dyf, axis=0, keepdims=True)
    v0[0:1, :] = jnp.sum(dh * normed, axis=0, keepdims=True)
    v0[1:2, :] = jnp.sum(dh, axis=0, keepdims=True)
    v0[5:6, :] = dsum
    v0[10:11, :] = dsum
    v0[11:16, :] = jnp.zeros((5, 512), f32)
    chip.wait()
    vcp = [send(v0, v1, vs.at[0], vr.at[0], other_core())]

    def add(i):
        a, b = i // 4, i % 4
        both = ga[a, b, s, :, 0:80].astype(f32) + rcm[a, b, :, 0:80].astype(f32)
        hi, lo = split(both[:, 48:64] + both[:, 64:80])
        hbuf[a, b, :, 0:48] = both[:, 0:48].astype(bf16)
        hbuf[a, b, :, 48:64] = hi
        hbuf[a, b, :, 64:80] = lo

    loop(0, 16, add)
    sums = Reduce(hbuf, ATT_PARTS, r.att_bufs, r.as_, r.ar)
    sums.begin(0)
    mt = momenta(r)

    def vec_stage(k, buf, axis):
        for cp in vcp:
            cp.wait()
        vcp.clear()
        if k == 0:
            v = v0[...] + v1[...]
        else:
            last = (vy, vz)[k - 1]
            v = (last[0] + last[1]) + (last[2] + last[3])
        place = {"y": y, "z": z, "x": x}[axis]
        buf[place] = v
        for d in (1, 2, 3):
            vcp.append(
                send(buf.at[place], buf.at[place], vs.at[3 * k + d], vr.at[3 * k + d], moved(axis, d))
            )

    sums.end(0)
    sums.begin(1)
    vec_stage(0, vy, "y")
    sums.end(1)
    sums.begin(2)
    vec_stage(1, vz, "z")
    lo = 64
    for v in mlp_sums.end(2):
        gx[lo : lo + v.shape[0], :] = v
        lo += v.shape[0]
    g = sums.end(2)
    gx[0:32, :] = g[0]
    gx[32:48, :] = g[1]
    gx[48:64, :] = g[2]
    grad = gx[...]
    u = (1.0 + MU) * grad + (MU * MU) * mt
    ub = u.astype(bf16)
    hi, lo = split(u[48:64])
    us[0, 0:48] = ub[0:48]
    us[0, 48:64] = jnp.zeros((16, 128), bf16)
    us[1, 0:16] = hi
    us[1, 16:32] = lo
    us[1, 32:64] = jnp.zeros((32, 128), bf16)
    us[2] = ub[64:128]
    us[3] = ub[128:192]
    cps = []
    for d in (1, 2, 3):
        cps.append(send(us.at[(x + d) % 4], ur.at[x], xs.at[d - 1], xr.at[d - 1], moved("x", d)))
    vec_stage(2, vx, "x")
    ur[x] = us[x]
    r.gxa[y, z, s] = grad.astype(bf16)
    for cp in cps:
        cp.wait()
    for k in range(4):
        piece = ur[k]

        @pl.when(x != 3)
        def _(k=k, piece=piece):
            ua[:, y, z, s, :, 128 * k : 128 * k + 128] = piece.reshape(4, 16, 128)

        @pl.when(x == 3)
        def _(k=k, piece=piece):
            for b in range(4):
                ua[k, y, z, s, :, 128 * b : 128 * b + 128] = piece[16 * b : 16 * b + 16]

    gather = Gather(
        [
            (lambda a, b, e: ua.at[pl.ds(0, 2), a, b, e], True),
            (lambda a, b, e: ua.at[pl.ds(2, 2), a, b, e], False),
        ],
        r.sa, r.ra,
    )
    gather.begin()
    for cp in vcp:
        cp.wait()
    r.vec[...] = (vx[0] + vx[1]) + (vx[2] + vx[3])
    gather.turn()
    gather.pass_on()
    gather.end()


def dot3(a, b):
    (ah, al), (bh, bl) = a, b
    return dot(ah, bh) + (dot(ah, bl) + dot(al, bh))


def newton_phase(r):
    y, z, s, x = coords()
    ua, ga, oa, a_ref = r.w3, r.gxa, r.oa, r.a
    ah, al, ph, pl_, th, tl, uh, ul = r.ah, r.al, r.ph, r.pl, r.th, r.tl, r.uh, r.ul
    os, rows, xs, xr = r.os, r.rows, r.os_s, r.os_r
    grads = Gather(
        [
            (lambda a, b, e: ga.at[a, b, e, pl.ds(0, 96)], True),
            (lambda a, b, e: ga.at[a, b, e, pl.ds(96, 96)], False),
        ],
        r.sb, r.rb,
    )
    grads.begin()

    def load(hi, lo):
        return hi[...], lo[...]

    def store(hi, lo, v):
        h, l = split(v)
        hi[...] = h
        lo[...] = l

    @pl.when(x == 1)
    def _():
        uh[...] = ua[0].reshape(512, 512)
        ul[...] = ua[1].reshape(512, 512)
        h, l = uh[...], ul[...]
        a_ref[...] = dot_tn(h, h) + (dot_tn(h, l) + dot_tn(l, h))

    @pl.when(x != 1)
    def _():
        u = ua[...].reshape(2048, 512)
        a_ref[...] = dot_tn(u, u)

    row = lax.broadcasted_iota(jnp.int32, (512, 512), 0)
    col = lax.broadcasted_iota(jnp.int32, (512, 512), 1)
    eye = row == col
    a = a_ref[...]
    square = jnp.sum(jnp.sum(jnp.where(eye, a, 0.0), axis=0, keepdims=True), axis=1, keepdims=True)
    scale = 1.0 / (jnp.sqrt(square) + 1e-07)
    a_ref[...] = a * (scale * scale)
    mine = ua[:, y, z, s].reshape(64, 512).astype(f32) * scale

    def poly():
        store(ah, al, a_ref[...])
        sq = dot3(load(ah, al), load(ah, al))
        return C2 * a_ref[...] + C3 * sq + jnp.where(eye, C1, 0.0)

    def step(_, mine):
        store(ph, pl_, poly())
        pair = load(ph, pl_)
        store(th, tl, dot3(pair, load(ah, al)))
        a_ref[...] = dot3(pair, load(th, tl))
        return dot3(split(mine), pair)

    mine = lax.fori_loop(0, 2, step, mine)
    grads.turn()
    mine = lax.fori_loop(2, NS_ITERS - 1, step, mine)
    grads.pass_on()
    store(ph, pl_, poly())
    mine = dot3(split(mine), load(ph, pl_))
    side = jnp.where(x == 0, math.sqrt(1536.0), jnp.where(x == 1, math.sqrt(512.0), math.sqrt(2048.0)))
    mine = mine * (0.2 * side)
    mine = jnp.concatenate(
        [jnp.where(x == 1, mine[0:16] + mine[16:32], mine[0:16]), mine[16:64]], axis=0
    ).astype(bf16)
    for k in range(4):
        by_lanes = mine[:, 128 * k : 128 * k + 128]
        by_rows = jnp.concatenate(
            [mine[16 * k : 16 * k + 16, 128 * b : 128 * b + 128] for b in range(4)], axis=0
        )
        os[k] = jnp.where(x == 3, by_rows, by_lanes)
    cps = []
    for d in (1, 2, 3):
        cps.append(send(os.at[(x + d) % 4], rows.at[x], xs.at[d - 1], xr.at[d - 1], moved("x", d)))
    rows[x] = os[x]
    grads.end()
    leave(r, 2).start()
    for cp in cps:
        cp.wait()
    oa[y, z, s, 0:48] = rows[0, 0:48]
    oa[y, z, s, 48:64] = rows[1, 0:16]
    oa[y, z, s, 64:128] = rows[2]
    oa[y, z, s, 128:192] = rows[3]
    update = Gather(
        [
            (lambda a, b, e: oa.at[a, b, e, pl.ds(0, 96)], True),
            (lambda a, b, e: oa.at[a, b, e, pl.ds(96, 96)], False),
        ],
        r.se, r.re,
    )
    update.begin()
    update.turn()
    update.pass_on()
    update.end()
    for k in range(3):
        leave(r, k).wait()


def scratch_list():
    V = pltpu.VMEM
    piece = (HEADS, TOK, 128)
    out = [
        ("fq", V((128, 1536), f32)), ("fo", V((128, 512), f32)),
        ("fi", V((128, 2048), f32)), ("ff", V((512, 512), f32)),
        ("x", V((TOK, D), bf16)), ("dy", V((TOK, D), bf16)),
        ("w1", V((4, 4, 4, 2, 64, 128), bf16)), ("w2", V((4, 4, 4, 2, 64, 128), bf16)),
        ("w3", V((4, 4, 4, 2, 16, 512), bf16)),
        ("kvs", V(piece, bf16)), ("qds", V(piece, bf16)),
        ("kv", V((GROUP, 128), bf16)), ("qd", V((NQB, QB, 128), bf16)),
        ("hid", V((TOK, D), bf16)), ("wide_f", V((TOK, D), f32)),
        ("co", V((TOK, 128), f32)), ("s1", V((TOK, 128), f32)), ("s2", V((TOK, 128), f32)),
        ("res", V((TOK, D), f32)), ("dh", V((TOK, D), f32)),
        ("gm", V((4, 4, 2, 4, 128, 128), bf16)),
        ("rcm", V((4, 4, 4, 128, 128), bf16)), ("hbuf", V((4, 4, 4, 128, 128), bf16)),
        ("kvt", V((128, GROUP), bf16)), ("acc", V((GROUP, 128), f32)),
        ("s_sc", V((GROUP, QB), f32)), ("p_sc", V((GROUP, QB), f32)),
        ("m_sc", V((GROUP // HB, 8, QB), f32)), ("cqs", V((NQB, QB, 128), bf16)),
        ("half", V((16, TOK, 128), bf16)), ("other", V((16, TOK, 128), bf16)),
        ("both", V((16, TOK, 128), bf16)),
        ("spare", V((6, 64, 128), bf16)),
        ("cq", V(piece, bf16)), ("kr", V((HEADS, 2, TOK, 128), bf16)),
        ("dqkv", V((TOK, 1536), bf16)),
        ("mwin", V((128, 512), f32)), ("mtr", V((512, 128), f32)), ("mfin", V((16, 512), f32)),
        ("gx", V((192, 128), f32)),
        ("us", V((4, 64, 128), bf16)), ("ur", V((4, 64, 128), bf16)),
        ("os", V((4, 64, 128), bf16)), ("rows", V((4, 64, 128), bf16)),
        ("v0", V((16, 512), f32)), ("v1", V((16, 512), f32)),
        ("vy", V((4, 16, 512), f32)), ("vz", V((4, 16, 512), f32)), ("vx", V((4, 16, 512), f32)),
        ("a", V((512, 512), f32)),
        ("out", V((TOK, D), bf16)), ("gt", V((TOK, D), f32)),
        ("gxa", V((4, 4, 2, 192, 128), bf16)),
    ]
    out += [(k, V((512, 512), bf16)) for k in ("ah", "al", "ph", "pl", "th", "tl", "uh", "ul")]
    for name, shape in (
        ("lsem", (6,)), ("osem", (3,)), ("msem", (4,)), ("xs", (5, 3)), ("xr", (5, 3)), ("ys", (3, 3)), ("yr", (3, 3)),
        ("sa", (2, 3)), ("ra", (2, 5)), ("sb", (2, 3)), ("rb", (2, 5)),
        ("se", (2, 3)), ("re", (2, 5)),
        ("own_sem", None), ("ks", None), ("kvr", None), ("qs", None), ("qr", None),
        ("cs", None), ("cr", None),
        ("m_s", (2,)), ("m_r", (2,)), ("ms", (3, 3)), ("mr", (3, 3)), ("as_", (3, 3)), ("ar", (3, 3)),
        ("ws", (6,)), ("wr", (6,)), ("bs", None), ("br", None), ("rqs", None), ("rqr", None),
        ("vs", (10,)), ("vr", (10,)), ("us_s", (3,)), ("us_r", (3,)), ("os_s", (3,)), ("os_r", (3,)),
    ):
        out.append((name, DMA if shape is None else DMA(shape)))
    out += [(f"mlp{i}", v) for i, v in enumerate(Reduce.scratch(MLP_PARTS))]
    out += [(f"att{i}", v) for i, v in enumerate(Reduce.scratch(ATT_PARTS))]
    return out


INPUTS = (
    "starts", "x_in", "dy_in", "gain", "shift", "bias", "wq", "wo", "wi", "wf", "mq", "mo", "mi", "mf",
)
OUTPUTS = ("out_to", "gt_to", "gxa_to", "oa", "vec")


def step_kernel(names, *refs):
    r = types.SimpleNamespace(**dict(zip(names, refs)))
    r.mlp_bufs = [getattr(r, f"mlp{i}") for i in range(5 * len(MLP_PARTS))]
    r.att_bufs = [getattr(r, f"att{i}") for i in range(5 * len(ATT_PARTS))]
    chip = front_phase(r)
    back_phase(r, attention_phase(r, chip))
    newton_phase(r)


def train_step(*args):
    scratch = scratch_list()
    names = INPUTS + OUTPUTS + tuple(k for k, _ in scratch)
    return pl.pallas_call(
        functools.partial(step_kernel, names),
        out_shape=tuple(
            jax.ShapeDtypeStruct(shape, t)
            for shape, t in (
                ((TOK, D), bf16), ((TOK, D), f32),
                ((4, 4, 2, 192, 128), bf16), ((4, 4, 2, 192, 128), bf16), ((16, 512), f32),
            )
        ),
        in_specs=[SM, ANY, ANY, VM, VM, VM] + [ANY] * 8,
        out_specs=(ANY, ANY, ANY, VM, VM),
        scratch_shapes=[v for _, v in scratch],
        compiler_params=pltpu.CompilerParams(
            vmem_limit_bytes=63 * 2**20, collective_id=1, has_side_effects=True
        ),
        name="train_step",
    )(*args)


def update_kernel(
    gx, oa, out, gt, wq, wo, wi, wf, mq, mo, mi, mf, vec, vm, gain, shift, bias,
    out_to, gt_to, nmq, nwq, nmo, nwo, nmi, nwi, nmf, nwf, nvm, nvec,
):
    out_to[...] = out[...]
    gt_to[...] = gt[...]

    @pl.when(pl.program_id(0) == 0)
    def _():
        for k in range(11):
            part = slice(512 * k, 512 * k + 512)
            v = VMU * vm[part] + vec[k]
            old = (gain[...], shift[...])[k] if k < 2 else bias[512 * k - 1024 : 512 * k - 512]
            nvm[part] = v
            nvec[part] = old - VLR * v

    for lo, n, w, m, nm, nw in (
        (0, 48, wq, mq, nmq, nwq),
        (48, 16, wo, mo, nmo, nwo),
        (64, 64, wi, mi, nmi, nwi),
    ):
        grad = gx[:, lo : lo + n, :].astype(f32).reshape(8 * n, 128).T
        turned = oa[:, lo : lo + n, :].astype(f32).reshape(8 * n, 128).T
        nm[...] = MU * m[...] + grad
        nw[...] = (1.0 - LR * WD) * w[...] - LR * turned
    for b in range(4):
        cols = slice(128 * b, 128 * b + 128)
        rows = slice(128 + 16 * b, 144 + 16 * b)
        grad = gx[:, rows, :].astype(f32).reshape(128, 128)
        turned = oa[:, rows, :].astype(f32).reshape(128, 128)
        nmf[:, cols] = MU * mf[:, cols] + grad
        nwf[:, cols] = (1.0 - LR * WD) * wf[:, cols] - LR * turned


def update(gx, oa, out, gt, weights, moments, vec, vec_mom, gain, shift, biases):
    def whole(v):
        return pl.BlockSpec(v.shape, lambda i, n=v.ndim: (0,) * n)

    piece = pl.BlockSpec((8, 192, 128), lambda i: (i, 0, 0))
    rows = pl.BlockSpec((48, D), lambda i: (i, 0))
    blocks = [
        pl.BlockSpec((128, 384), lambda i: (0, i)),
        pl.BlockSpec((128, 128), lambda i: (0, i)),
        pl.BlockSpec((128, 512), lambda i: (0, i)),
        pl.BlockSpec((128, 512), lambda i: (i, 0)),
    ]
    shape = lambda v: jax.ShapeDtypeStruct(v.shape, v.dtype)
    outs, specs = [shape(out), shape(gt)], [rows, rows]
    for w, b in zip(weights, blocks):
        outs += [shape(w)] * 2
        specs += [b, b]
    outs += [shape(vec_mom)] * 2
    specs += [whole(vec_mom)] * 2
    vectors = (vec, vec_mom, gain, shift, biases)
    return pl.pallas_call(
        update_kernel,
        grid=(4,),
        out_shape=tuple(outs),
        in_specs=[piece, piece, rows, rows] + blocks + blocks + [whole(v) for v in vectors],
        out_specs=tuple(specs),
        compiler_params=pltpu.CompilerParams(vmem_limit_bytes=60 * 2**20),
        name="update_weights",
    )(gx, oa, out, gt, *weights, *moments, *vectors)


def body(
    tokens, cotangent, ln_gain, ln_bias, biases, w_qkv, w_out, w_in, w_fin,
    mom_qkv, mom_out, mom_in, mom_fin, vec_mom, starts,
):
    weights = (w_qkv, w_out, w_in, w_fin)
    moments = (mom_qkv, mom_out, mom_in, mom_fin)
    block_out, grad_tokens, gx, oa, vec_sum = train_step(
        starts, tokens, cotangent, ln_gain[None, :], ln_bias[None, :], biases, *weights, *moments
    )
    return update(
        gx.reshape(32, 192, 128), oa.reshape(32, 192, 128), block_out, grad_tokens,
        weights, moments, vec_sum, vec_mom, ln_gain, ln_bias, biases,
    )


def solution(mesh):
    tok = P(("wsh", "ctx"), None)
    row = P("wsh", None)
    return jax.shard_map(
        body,
        mesh=mesh,
        in_specs=(tok, tok, P(), P(), P()) + (row,) * 8 + (P(), P()),
        out_specs=(tok, tok) + (row,) * 8 + (P(), P()),
        check_vma=False,
    )
```

```python
import functools
import math
import types

import jax
import jax.numpy as jnp
from jax import lax
from jax.experimental import pallas as pl
from jax.experimental.pallas import tpu as pltpu
from jax.sharding import PartitionSpec as P

f32 = jnp.float32
bf16 = jnp.bfloat16
MESH = pl.DeviceIdType.MESH
HEADS = 8
HD = 64
ROT = 16
D = 512
TOK = 192
GROUP = 6144
QB = 256
NQB = 6
HB = 128
UU = 8
TT = 4
NS_ITERS = 5
C1, C2, C3 = 3.4445, -4.775, 2.0315
MU, LR, WD = 0.95, 0.6, 0.01
VMU, VLR = 0.9, 0.0005
R_QKV, R_OUT, R_IN, R_FIN = 48, 16, 64, 64

VM = pl.BlockSpec(memory_space=pltpu.VMEM)
SM = pl.BlockSpec(memory_space=pltpu.SMEM)
ANY = pl.BlockSpec(memory_space=pl.ANY)
DMA = pltpu.SemaphoreType.DMA


def dot(a, b):
    return jnp.dot(a, b, preferred_element_type=f32)


def dot_nt(a, b):
    return lax.dot_general(a, b, (((1,), (1,)), ((), ())), preferred_element_type=f32)


def dot_tn(a, b):
    return lax.dot_general(a, b, (((0,), (0,)), ((), ())), preferred_element_type=f32)


def coords():
    c = lax.axis_index("ctx")
    return c // 8, (c // 2) % 4, c % 2, lax.axis_index("wsh")


def at(y, z, s, x):
    return {"ctx": (y * 4 + z) * 2 + s, "wsh": x}


def tell(partners):
    sem = pltpu.get_barrier_semaphore()
    for p in partners:
        pl.semaphore_signal(sem, inc=1, device_id=p, device_id_type=MESH)


def tell_slab():
    c = lax.axis_index("ctx")
    sem = pltpu.get_barrier_semaphore()

    def one(d, _):
        pl.semaphore_signal(
            sem, inc=1, device_id={"ctx": lax.rem(c + d, 32)}, device_id_type=MESH
        )
        return 0

    lax.fori_loop(1, 32, one, 0)


def met(count):
    pl.semaphore_wait(pltpu.get_barrier_semaphore(), count)


def wait_for(ref, sem):
    pltpu.make_async_copy(ref, ref, sem).wait()


def loop(lo, hi, f):
    def step(i, _):
        f(i)
        return 0

    lax.fori_loop(lo, hi, step, 0)


AXES = ("y", "z", "x")


def moved(axis, d):
    y, z, s, x = coords()
    if axis == "y":
        return at((y + d) % 4, z, s, x)
    if axis == "z":
        return at(y, (z + d) % 4, s, x)
    return at(y, z, s, (x + d) % 4)


def other_core():
    y, z, s, x = coords()
    return at(y, z, 1 - s, x)


def lines(axes=AXES):
    return [moved(a, d) for a in axes for d in (1, 2, 3)]


def send(src, dst, ss, rs, dev):
    cp = pltpu.make_async_remote_copy(
        src_ref=src, dst_ref=dst, send_sem=ss, recv_sem=rs, device_id=dev, device_id_type=MESH
    )
    cp.start()
    return cp


ALL = slice(None)


class Gather:
    def __init__(self, items, ss, rs):
        self.items, self.ss, self.rs = items, ss, rs

    def begin(self):
        y, z, s, x = coords()
        for i, (get, y_first) in enumerate(self.items):
            piece = get(y, z, s)
            for d in (1, 2, 3):
                send(
                    piece, piece, self.ss.at[i, 0], self.rs.at[i, 0], moved("y" if y_first else "z", d)
                )

    def turn(self):
        y, z, s, x = coords()
        three = pl.ds(0, 3)
        for i, (get, y_first) in enumerate(self.items):
            pieces = get(three, z, s) if y_first else get(y, three, s)
            wait_for(pieces, self.ss.at[i, 0])
            wait_for(pieces, self.rs.at[i, 0])
        self.second = {}
        for i, (get, y_first) in enumerate(self.items):
            piece = get(ALL, z, s) if y_first else get(y, ALL, s)
            for d in (1, 2, 3):
                to = moved("z" if y_first else "y", d)
                self.second[i, d] = send(piece, piece, self.ss.at[i, 1], self.rs.at[i, d], to)
        for i, (get, y_first) in enumerate(self.items):
            piece = get(ALL, z, s) if y_first else get(y, ALL, s)
            send(piece, piece, self.ss.at[i, 2], self.rs.at[i, 4], other_core())

    def pass_on(self):
        y, z, s, x = coords()
        for d in (1, 3, 2):
            for i, (get, y_first) in enumerate(self.items):
                self.second[i, d].wait_recv()
                piece = get(ALL, (z - d) % 4, s) if y_first else get((y - d) % 4, ALL, s)
                send(piece, piece, self.ss.at[i, 2], self.rs.at[i, 4], other_core())

    def end(self):
        three = pl.ds(0, 3)
        for i, (get, y_first) in enumerate(self.items):
            wait_for(get(ALL, three, 0) if y_first else get(three, ALL, 0), self.ss.at[i, 1])
            wait_for(get(ALL, ALL, 0), self.ss.at[i, 2])
            wait_for(get(ALL, ALL, 0), self.rs.at[i, 4])


def split(v):
    hi = v.astype(bf16)
    return hi, (v - hi.astype(f32)).astype(bf16)


class Reduce:
    def __init__(self, src, parts, bufs, ss, rs):
        self.src, self.parts, self.ss, self.rs = src, parts, ss, rs
        y, z, s, x = coords()
        self.me = {"y": y, "z": z, "x": x}
        self.bufs = [bufs[5 * i : 5 * i + 5] for i in range(len(parts))]

    @staticmethod
    def scratch(parts):
        out = []
        for lo, n, order, paired in parts:
            out += [
                pltpu.VMEM((3, 4, 4, n, 128), bf16),
                pltpu.VMEM((4, 4, n, 128), bf16),
                pltpu.VMEM((3, 4, n, 128), bf16),
                pltpu.VMEM((4, n, 128), bf16),
                pltpu.VMEM((3, n, 128), bf16),
            ]
        return out

    @staticmethod
    def summed(pieces, paired):
        v = functools.reduce(lambda a, b: a + b, [p.astype(f32) for p in pieces])
        if not paired:
            return v.astype(bf16)
        half = v.shape[-2] // 2
        return jnp.concatenate(split(v[..., :half, :] + v[..., half:, :]), axis=-2)

    def begin(self, stage):
        for d in (2, 1, 3):
            for i, (lo, n, order, paired) in enumerate(self.parts):
                r1, h1, r2, h2, r3 = self.bufs[i]
                axis = order[stage]
                place = (self.me[axis] + d) % 4
                left = [a for a in AXES if a not in order[:stage]]
                index = tuple(place if a == axis else ALL for a in left)
                if stage == 0:
                    src = self.src.at[index + (pl.ds(lo, n),)]
                else:
                    src = (h1, h2)[stage - 1].at[index]
                send(
                    src, (r1, r2, r3)[stage].at[d - 1],
                    self.ss.at[stage, i], self.rs.at[stage, i], moved(axis, d),
                )

    def end(self, stage):
        out = []
        for i, (lo, n, order, paired) in enumerate(self.parts):
            r1, h1, r2, h2, r3 = self.bufs[i]
            wait_for((r1, r2, r3)[stage], self.ss.at[stage, i])
            wait_for((r1, r2, r3)[stage], self.rs.at[stage, i])
            mine = self.me[order[stage]]
            if stage == 0:
                axis = AXES.index(order[0])

                def add(a, _, axis=axis, mine=mine, lo=lo, n=n, paired=paired, r1=r1, h1=h1):
                    index = [a, ALL]
                    index.insert(axis, mine)
                    own = self.src[tuple(index) + (slice(lo, lo + n),)]
                    h1[a] = self.summed([own, r1[0, a], r1[1, a], r1[2, a]], paired)
                    return 0

                lax.fori_loop(0, 4, add, 0)
            elif stage == 1:
                left = [a for a in AXES if a != order[0]]
                first = left.index(order[1]) == 0
                own = h1[mine] if first else h1[:, mine]
                h2[...] = self.summed([own, r2[0], r2[1], r2[2]], paired)
            else:
                v = h2[mine].astype(f32) + r3[0].astype(f32) + r3[1].astype(f32) + r3[2].astype(f32)
                if paired:
                    v = v[: n // 2] + v[n // 2 :]
                out.append(v)
        return out


MLP_PARTS = ((0, 48, ("y", "z", "x"), False), (48, 48, ("z", "x", "y"), False), (96, 32, ("x", "y", "z"), False))
ATT_PARTS = ((0, 32, ("y", "z", "x"), False), (32, 16, ("z", "x", "y"), False), (48, 32, ("x", "y", "z"), True))


def norm_parts(x_ref, gain, shift):
    xf = x_ref[...].astype(f32)
    centered = xf - jnp.mean(xf, axis=1, keepdims=True)
    inv = lax.rsqrt(jnp.mean(centered * centered, axis=1, keepdims=True) + 1e-05)
    normed = centered * inv
    hidden = (normed * gain + shift).astype(bf16)
    return xf, inv, normed, hidden


def turn(v, co, s1, s2):
    return v * co + pltpu.roll(v, 120, 1) * s1 + pltpu.roll(v, 8, 1) * s2


def rolled(ref, x):
    parts = [ref[:, pl.ds(pl.multiple_of((x + d) % 4 * 128, 128), 128)] for d in range(4)]
    return jnp.concatenate(parts, axis=1)


def unroll(v, ref, x):
    for d in range(4):
        ref[:, pl.ds(pl.multiple_of((x + d) % 4 * 128, 128), 128)] = v[:, 128 * d : 128 * d + 128]
    return ref[...]


def rotary(starts_ref, x, c):
    bnd = starts_ref[x] - x * GROUP
    place = c * TOK + lax.broadcasted_iota(jnp.int32, (TOK, 128), 0)
    pos = (place - jnp.where(place >= bnd, bnd, 0)).astype(f32)
    lane = lax.broadcasted_iota(jnp.int32, (TOK, 128), 1) % HD
    freq = jnp.zeros((TOK, 128), f32)
    for i in range(ROT // 2):
        freq = jnp.where(lane % 8 == i, 10000.0 ** (-2.0 * i / ROT), freq)
    angle = pos * jnp.where(lane < ROT, freq, 0.0)
    co, si = jnp.cos(angle), jnp.sin(angle)
    return co, jnp.where(lane < 8, -si, 0.0), jnp.where(lane < 8, 0.0, si)


def wide(w, first, count):
    blocks = [w[(first + i) // 4, (first + i) % 4].reshape(512, 128) for i in range(count)]
    return jnp.concatenate(blocks, axis=1) if count > 1 else blocks[0]


def query_home(piece):
    block = piece // 4
    part = block % 8
    low = part < 4
    return jnp.where(low, part, 7 - part), 2 * (block // 8) + jnp.where(low, 0, 1), piece % 4


def query_block(t, j):
    if isinstance(t, int):
        return 8 * (t // 2) + (j if t % 2 == 0 else 7 - j)
    return 8 * (t // 2) + jnp.where(t % 2 == 0, j, 7 - j)


def front_phase(r):
    y, z, s, x = coords()
    c = lax.axis_index("ctx")
    p = c // 2
    w1, w2, w3, kvs, qds, kv, qd = r.w1, r.w2, r.w3, r.kvs, r.qds, r.kv, r.qd
    ks, kr, qs, qr, cs, cr = r.ks, r.kvr, r.qs, r.qr, r.cs, r.cr
    bias_ref = r.bias
    tell_slab()
    tell(lines(("x",)))
    loads = [
        pltpu.make_async_copy(src, dst, r.lsem.at[k])
        for k, (src, dst) in enumerate(
            ((r.wq, r.fq), (r.wo, r.fo), (r.wi, r.fi), (r.wf, r.ff), (r.x_in, r.x), (r.dy_in, r.dy))
        )
    ]
    for cp in loads:
        cp.start()
    momenta_begin(r)
    for cp in loads:
        cp.wait()
    for b in range(16):
        w = r.fq[:, 128 * b : 128 * b + 128] if b < 12 else r.fo[:, 128 * b - 1536 : 128 * b - 1408]
        w1[b // 4, b % 4, 0] = w.astype(bf16).reshape(2, 64, 128)
        w2[b // 4, b % 4, 0] = r.fi[:, 128 * b : 128 * b + 128].astype(bf16).reshape(2, 64, 128)
    w3[0] = r.ff[...].astype(bf16).reshape(4, 4, 2, 16, 512)
    met(34)
    slab, direct = pl.ds(0, 32), pl.ds(32, 32)

    def along_x(k, piece):
        return [
            send(piece(0), piece(4 - d), r.xs.at[k, d - 1], r.xr.at[k, d - 1], moved("x", d))
            for d in (1, 2, 3)
        ]

    low, high = pl.ds(0, 256), pl.ds(256, 256)
    own_cps = along_x(0, lambda d: w1.at[y, z, d, s, slab])
    late_cps = along_x(4, lambda d: w3.at[d, y, z, s, :, high])
    direct_cps = along_x(1, lambda d: w1.at[:, :, d, s, direct])
    co, s1, s2 = rotary(r.starts, x, c)
    r.co[...], r.s1[...], r.s2[...] = co, s1, s2
    xf, inv, normed, hidden = norm_parts(r.x, r.gain[...], r.shift[...])
    r.hid[...] = hidden
    hidden_r = rolled(r.hid, x)
    dy = r.dy[...]
    for cp in own_cps:
        cp.wait()
    others = pl.ds(1, 3)
    early = Gather(
        [
            (lambda a, b, e: w1.at[a, b, others, e, pl.ds(0, 16)], True),
            (lambda a, b, e: w1.at[a, b, others, e, pl.ds(16, 16)], False),
        ],
        r.sa, r.ra,
    )
    late = Gather(
        [
            (lambda a, b, e: w3.at[others, a, b, e, :, pl.ds(256, 128)], True),
            (lambda a, b, e: w3.at[others, a, b, e, :, pl.ds(384, 128)], False),
        ],
        r.sb, r.rb,
    )

    def to_core(k, cps, piece):
        out = []
        for d in (1, 3, 2):
            cps[d - 1].wait_recv()
            got = piece(4 - d)
            out.append(send(got, got, r.ys.at[k, d - 1], r.yr.at[k, d - 1], other_core()))
        for cp in cps:
            cp.wait_send()
        return out

    early.begin()
    early.turn()
    passed = to_core(0, direct_cps, lambda d: w1.at[:, :, d, s, direct])
    in_cps = along_x(2, lambda d: w2.at[:, :, d, s])
    fin_cps = along_x(3, lambda d: w3.at[d, :, :, s, :, low])
    early.pass_on()
    for cp in late_cps:
        cp.wait()
    late.begin()
    early.end()
    for cp in passed:
        cp.wait()
    left = lax.broadcasted_iota(jnp.int32, (TOK, 128), 1) < 64
    dctx = unroll(dot_nt(dy, wide(w1, 12, 4)), r.wide_f, x)
    for half in range(2):
        thirds = []
        for third in range(3):
            b = third * 4 + 2 * half
            thirds.append(dot(hidden_r, wide(w1, b, 2)) + bias_ref[b * 128 : b * 128 + 256][None, :])
        for e in range(2):
            lanes = slice(128 * e, 128 * e + 128)
            q = turn(thirds[0][:, lanes], co, s1, s2).astype(bf16).astype(f32) * 0.125
            k = turn(thirds[1][:, lanes], co, s1, s2)
            v = thirds[2][:, lanes]
            pair = 2 * half + e
            g = dctx[:, pair * 128 : pair * 128 + 128]
            h = 2 * pair
            kvs[h] = jnp.where(left, k, pltpu.roll(v, 64, 1)).astype(bf16)
            kvs[h + 1] = jnp.where(left, pltpu.roll(k, 64, 1), v).astype(bf16)
            qds[h] = jnp.where(left, q, pltpu.roll(g, 64, 1)).astype(bf16)
            qds[h + 1] = jnp.where(left, pltpu.roll(q, 64, 1), g).astype(bf16)

    def kv_copy(d):
        to = lax.rem(p + d, 16)
        return pltpu.make_async_remote_copy(
            src_ref=kvs.at[to // 2], dst_ref=kv.at[pl.ds(c * TOK, TOK)], send_sem=ks, recv_sem=kr,
            device_id={"ctx": to * 2 + s}, device_id_type=MESH,
        )

    def across(d):
        block = kv.at[pl.ds((lax.rem(p + 16 - d, 16) * 2 + s) * TOK, TOK)]
        return pltpu.make_async_remote_copy(
            src_ref=block, dst_ref=block, send_sem=cs, recv_sem=cr,
            device_id={"ctx": p * 2 + 1 - s}, device_id_type=MESH,
        )

    def each_query(k):
        h, i = k // 3, k % 3
        j, t, quarter = query_home(3 * c + i)
        to = 4 * h + j
        src = qds.at[h, pl.ds(64 * i, 64)]
        dst = qd.at[t, pl.ds(64 * quarter, 64)]

        @pl.when(to == c)
        def _():
            pltpu.make_async_copy(src, dst, qr).start()
            pltpu.make_async_copy(src, r.spare.at[i], qs).start()

        @pl.when(to != c)
        def _():
            pltpu.make_async_remote_copy(
                src_ref=src, dst_ref=dst, send_sem=qs, recv_sem=qr,
                device_id={"ctx": to}, device_id_type=MESH,
            ).start()

    own = pltpu.make_async_copy(kvs.at[p // 2], kv.at[pl.ds(c * TOK, TOK)], r.own_sem)
    own.start()
    late.turn()
    loop(1, 16, lambda d: kv_copy(d).start())
    loop(0, 24, each_query)
    own.wait()

    r.acc[...] = jnp.zeros_like(r.acc)
    late.pass_on()
    late.end()
    passed = to_core(1, in_cps, lambda d: w2.at[:, :, d, s])
    passed += to_core(2, fin_cps, lambda d: w3.at[d, :, :, s, :, low])
    for cp in passed:
        cp.wait()
    root = math.sqrt(2.0 / math.pi)
    mlp = jnp.zeros((TOK, D), f32)
    dh = jnp.zeros((TOK, D), f32)
    for i in range(4):
        if i == 2:
            wait_for(kv.at[pl.ds(0, 15 * TOK)], kr)
            loop(0, 16, lambda d: across(d).start())
        w_in = wide(w2, 4 * i, 4)
        w_fin = w3[(i + 4 - x) % 4].reshape(512, 512)
        pre = dot(hidden_r, w_in) + bias_ref[2048 + 512 * i : 2560 + 512 * i][None, :]
        sq = pre * pre
        th = jnp.tanh(root * (pre + 0.044715 * (pre * sq)))
        act = (0.5 * pre * (1.0 + th)).astype(bf16)
        slope = 0.5 * (1.0 + th) + (0.5 * root) * pre * (1.0 - th * th) * (
            1.0 + (3.0 * 0.044715) * sq
        )
        dpre = (dot_nt(dy, w_fin) * slope).astype(bf16)
        mlp = mlp + dot(act, w_fin)
        dh = dh + dot_nt(dpre, w_in)
        r.v0[6 + i : 7 + i, :] = jnp.sum(dpre.astype(f32), axis=0, keepdims=True)
        g_in = dot_tn(dpre, hidden).astype(bf16).reshape(4, 2, 64, 512)
        g_fin = dot_tn(act, dy).astype(bf16).reshape(4, 4, 2, 16, 512)
        for b in range(4):
            lanes = slice(128 * b, 128 * b + 128)
            r.gm[i, :, :, b, 0:64] = g_in[..., lanes]
            r.gm[:, :, :, i, 64 + 16 * b : 80 + 16 * b] = g_fin[..., lanes]
    r.res[...] = xf + mlp + (bias_ref[4096:4608] + bias_ref[1536:2048])[None, :]
    r.dh[...] = dh
    chip = send(r.gm.at[:, :, 1 - s], r.rcm, r.m_s.at[0], r.m_r.at[0], other_core())
    wait_for(kv.at[pl.ds(0, 15 * TOK)], ks)
    wait_for(qd, qs)
    wait_for(qd, qr)
    wait_for(kv.at[pl.ds(0, 16 * TOK)], cs)
    wait_for(kv.at[pl.ds(0, 16 * TOK)], cr)
    return chip


RETURNS = ((14, 16), (11, 14), (8, 11), (6, 8), (3, 6), (0, 3))


def attention_phase(r, chip):
    kvt, acc, s_sc, p_sc, m_sc, cqs = r.kvt, r.acc, r.s_sc, r.p_sc, r.m_sc, r.cqs
    half, other, both, rcm, hbuf = r.half, r.other, r.both, r.rcm, r.hbuf
    cq, kr, kv_ref, qd_ref, gm_ref = r.cq, r.kr, r.kv, r.qd, r.gm
    ws, wr, ss, sr, qs, qr = r.ws, r.wr, r.bs, r.br, r.rqs, r.rqr
    y, z, s, x = coords()
    c = lax.axis_index("ctx")
    p = c // 2
    h = c // 4
    j = c % 4
    n = kv_ref.shape[0]
    bnd = r.starts[x] - x * GROUP

    def prepare(i, _):
        o = pl.multiple_of(i * QB, QB)
        kvt[:, pl.ds(o, QB)] = kv_ref[pl.ds(o, QB), :].T
        return 0

    lax.fori_loop(0, n // QB, prepare, 0)
    lane = lax.broadcasted_iota(jnp.int32, (QB, 128), 1)

    def block(t):
        qb = query_block(t, j)
        qd = qd_ref[t]
        w1 = jnp.where(lane < 64, qd, jnp.zeros_like(qd))
        w2 = jnp.where(lane < 64, jnp.zeros_like(qd), qd)
        q_t = w1.T
        d_t = w2.T

        def scores(kt, masked, carry, tiles, first=False):
            m8, l8, r8 = carry
            for u in range(2 * tiles):
                o = pl.multiple_of(kt * QB + u * HB, HB)
                rows = kv_ref[pl.ds(o, HB), :]
                s = dot(rows, q_t)
                if masked and not (first and u > 1):
                    kp = o + lax.broadcasted_iota(jnp.int32, (HB, QB), 0)
                    qp = qb * QB + lax.broadcasted_iota(jnp.int32, (HB, QB), 1)
                    s = jnp.where((kp <= qp) & ((kp >= bnd) == (qp >= bnd)), s, -1e30)
                s = s.reshape(HB // 8, 8, QB)
                dp = dot(rows, d_t)
                p_sc[pl.ds(o, HB), :] = dp
                mn = jnp.maximum(m8, jnp.max(s, axis=0))
                e = jnp.exp(s - mn[None])
                s_sc[pl.ds(o, HB), :] = e.reshape(HB, QB)
                m_sc[2 * kt + u] = mn
                al = jnp.exp(m8 - mn)
                l8 = l8 * al + jnp.sum(e, axis=0)
                r8 = r8 * al + jnp.sum(e * dp.reshape(HB // 8, 8, QB), axis=0)
                m8 = mn
            return m8, l8, r8

        zero = jnp.zeros((8, QB), f32)
        base = t // 2 * 8
        tail = (qb - base) // TT + 1
        carry = lax.fori_loop(
            0, tail, lambda g, c: scores(base + TT * g, True, c, TT),
            (jnp.full((8, QB), -1e30, f32), zero, zero),
        )
        if base > 0:
            carry = scores(0, True, carry, UU, True)
        carry = lax.fori_loop(
            1, base // UU, lambda g, c: scores(g * UU, False, c, UU), carry
        )
        m8, l8, r8 = carry
        m = jnp.max(m8, axis=0, keepdims=True)
        w = jnp.exp(m8 - m)
        l = jnp.sum(l8 * w, axis=0, keepdims=True)
        lse = m + jnp.log(l)
        rd = jnp.sum(r8 * w, axis=0, keepdims=True) / l

        def grads(kt, carry, tiles):
            c_t, g_t = carry
            for u in range(tiles):
                o = pl.multiple_of((kt + u) * QB, QB)
                e = s_sc[pl.ds(o, QB), :].reshape(2, HB // 8, 8, QB)
                w0 = jnp.exp(m_sc[2 * (kt + u)] - lse)
                w1_ = jnp.exp(m_sc[2 * (kt + u) + 1] - lse)
                p = jnp.concatenate([e[0] * w0[None], e[1] * w1_[None]], axis=0).reshape(QB, QB)
                pb = p.astype(bf16)
                ds = (p * (p_sc[pl.ds(o, QB), :] - rd)).astype(bf16)
                c_t = c_t + dot(kvt[64:128, pl.ds(o, QB)], pb)
                g_t = g_t + dot(kvt[0:64, pl.ds(o, QB)], ds)
                acc[pl.ds(o, QB), :] += dot(ds, w1) + dot(pb, w2)
            return c_t, g_t

        z = jnp.zeros((64, QB), f32)
        c = lax.fori_loop(0, base // UU, lambda g, c: grads(g * UU, c, UU), (z, z))
        c_t, g_t = lax.fori_loop(0, tail, lambda g, c: grads(base + TT * g, c, TT), c)
        cqs[t] = jnp.concatenate([g_t * 0.125, c_t], axis=0).T.astype(bf16)

    def each_query(t, quarter):
        piece = 4 * query_block(t, j) + quarter
        to, i = piece // 3, piece % 3
        src = cqs.at[t, pl.ds(64 * quarter, 64)]
        dst = cq.at[h, pl.ds(64 * i, 64)]

        @pl.when(to == c)
        def _():
            pltpu.make_async_copy(src, dst, qr).start()
            pltpu.make_async_copy(src, r.spare.at[3 + i], qs).start()

        @pl.when(to != c)
        def _():
            pltpu.make_async_remote_copy(
                src_ref=src, dst_ref=dst, send_sem=qs, recv_sem=qr,
                device_id={"ctx": to}, device_id_type=MESH,
            ).start()

    def return_queries(t):
        loop(0, 4, lambda quarter: each_query(t, quarter))

    swaps = {}

    def exchange(g):
        lo, hi = RETURNS[g]

        def low(i):
            o = pl.multiple_of((2 * i + 1 - s) * TOK, TOK)
            half[i] = acc[pl.ds(o, TOK), :].astype(bf16)

        loop(lo, hi, low)
        part = pl.ds(lo, hi - lo)
        swaps[g] = send(half.at[part], other.at[part], ws.at[g], wr.at[g], other_core())

    def block_copy(i):
        return pltpu.make_async_remote_copy(
            src_ref=both.at[i], dst_ref=kr.at[h, p % 2], send_sem=ss, recv_sem=sr,
            device_id={"ctx": i * 2 + s}, device_id_type=MESH,
        )

    def push(g):
        lo, hi = RETURNS[g]
        swaps[g].wait()

        def one(i):
            o = pl.multiple_of((2 * i + s) * TOK, TOK)
            both[i] = (acc[pl.ds(o, TOK), :] + other[i].astype(f32)).astype(bf16)

            @pl.when(i == p)
            def _():
                pltpu.make_async_copy(both.at[i], kr.at[h, p % 2], sr).start()

            @pl.when(i != p)
            def _():
                block_copy(i).start()

        loop(lo, hi, one)

    def add(i):
        a, b = i // 4, i % 4
        hbuf[a, b] = (gm_ref[a, b, s].astype(f32) + rcm[a, b].astype(f32)).astype(bf16)

    sums = Reduce(hbuf, MLP_PARTS, r.mlp_bufs, r.ms, r.mr)
    for k in range(NQB):
        block(NQB - 1 - k)
        return_queries(NQB - 1 - k)
        exchange(k)
        if k > 0:
            push(k - 1)
        if k == 0:
            chip.wait()
            loop(0, 16, add)
            sums.begin(0)
        if k == 3:
            sums.end(0)
            sums.begin(1)
    push(NQB - 1)
    wait_for(cq, qr)
    wait_for(kr, sr)
    sums.end(1)
    sums.begin(2)
    return sums


def momenta_starts():
    c = lax.axis_index("ctx")
    return jnp.minimum(48 * c // 128, 10), 16 * c // 128, 64 * c // 128


def momenta_loads(r):
    c = lax.axis_index("ctx")
    starts = momenta_starts()
    loads = []
    for k, (m, width) in enumerate(((r.mq, 256), (r.mo, 128), (r.mi, 128))):
        first = pl.multiple_of(starts[k] * 128, 128)
        loads.append(
            pltpu.make_async_copy(
                m.at[:, pl.ds(first, width)],
                r.mwin.at[:, pl.ds((0, 256, 384)[k], width)],
                r.msem.at[k],
            )
        )
    loads.append(pltpu.make_async_copy(r.mf.at[pl.ds(16 * c, 16)], r.mfin, r.msem.at[3]))
    return loads


def momenta_begin(r):
    for cp in momenta_loads(r):
        cp.start()


def momenta(r):
    c = lax.axis_index("ctx")
    for cp in momenta_loads(r):
        cp.wait()
    r.mtr[...] = r.mwin[...].T
    offset = 48 * c - momenta_starts()[0] * 128
    return jnp.concatenate(
        [
            r.mtr[pl.ds(pl.multiple_of(offset, 16), 48), :],
            r.mtr[pl.ds(pl.multiple_of(256 + 16 * c % 128, 16), 16), :],
            r.mtr[pl.ds(pl.multiple_of(384 + 64 * c % 128, 64), 64), :],
        ]
        + [r.mfin[:, 128 * b : 128 * b + 128] for b in range(4)],
        axis=0,
    )


def leave(r, k):
    src, dst = ((r.out, r.out_to), (r.gt, r.gt_to), (r.gxa, r.gxa_to))[k]
    return pltpu.make_async_copy(src, dst, r.osem.at[k])


def back_phase(r, mlp_sums):
    dqkv, gx, us, ur, v0, v1, vy, vz, vx = r.dqkv, r.gx, r.us, r.ur, r.v0, r.v1, r.vy, r.vz, r.vx
    cq_ref, kr_ref, w1, ga, rcm, hbuf = r.cq, r.kr, r.w1, r.gm, r.rcm, r.hbuf
    vs, vr, xs, xr, ua = r.vs, r.vr, r.us_s, r.us_r, r.w3
    att = pl.ds(0, 80)
    y, z, s, x = coords()
    c = lax.axis_index("ctx")
    xf, inv, normed, hidden = norm_parts(r.x, r.gain[...], r.shift[...])
    dy = r.dy[...]
    co, s1, s2 = r.co[...], -r.s1[...], -r.s2[...]
    left = lax.broadcasted_iota(jnp.int32, (TOK, 128), 1) < 64
    ctx = []
    for pair in range(4):
        a = cq_ref[2 * pair].astype(f32)
        b = cq_ref[2 * pair + 1].astype(f32)
        e = kr_ref[2 * pair, 0].astype(f32) + kr_ref[2 * pair, 1].astype(f32)
        f = kr_ref[2 * pair + 1, 0].astype(f32) + kr_ref[2 * pair + 1, 1].astype(f32)
        dq = jnp.where(left, a, pltpu.roll(b, 64, 1))
        dk = jnp.where(left, e, pltpu.roll(f, 64, 1))
        dqkv[:, 128 * pair : 128 * pair + 128] = turn(dq, co, s1, s2).astype(bf16)
        dqkv[:, 512 + 128 * pair : 640 + 128 * pair] = turn(dk, co, s1, s2).astype(bf16)
        dqkv[:, 1024 + 128 * pair : 1152 + 128 * pair] = jnp.where(
            left, pltpu.roll(e, 64, 1), f
        ).astype(bf16)
        ctx.append(jnp.where(left, pltpu.roll(a, 64, 1), b).astype(bf16))
    ctx = jnp.concatenate(ctx, axis=1)
    r.hid[...] = ctx
    hi, lo = split(dot_tn(dy, ctx))
    hi, lo = hi.reshape(4, 4, 2, 16, 512), lo.reshape(4, 4, 2, 16, 512)
    for b in range(4):
        lanes = slice(128 * b, 128 * b + 128)
        ga[:, :, :, b, 48:64] = hi[..., lanes]
        ga[:, :, :, b, 64:80] = lo[..., lanes]
    for i in range(4):
        part = dqkv[:, 384 * i : 384 * i + 384]
        g = dot_tn(part, hidden).astype(bf16).reshape(4, 2, 48, 512)
        for b in range(4):
            ga[i, :, :, b, 0:48] = g[..., 128 * b : 128 * b + 128]
    chip = send(ga.at[:, :, 1 - s, :, att], rcm.at[:, :, :, att], r.m_s.at[1], r.m_r.at[1], other_core())
    r.out[...] = (r.res[...] + dot(rolled(r.hid, x), wide(w1, 12, 4))).astype(bf16)
    dh = r.dh[...]
    for third in range(3):
        part = dqkv[:, 512 * third : 512 * third + 512]
        dh = dh + dot_nt(part, wide(w1, 4 * third, 4))
        v0[2 + third : 3 + third, :] = jnp.sum(part.astype(f32), axis=0, keepdims=True)
    dh = unroll(dh, r.wide_f, x)
    scaled = dh * r.gain[...]
    dyf = dy.astype(f32)
    r.gt[...] = dyf + inv * (
        scaled
        - jnp.mean(scaled, axis=1, keepdims=True)
        - normed * jnp.mean(scaled * normed, axis=1, keepdims=True)
    )
    leave(r, 0).start()
    leave(r, 1).start()
    dsum = jnp.sum(dyf, axis=0, keepdims=True)
    v0[0:1, :] = jnp.sum(dh * normed, axis=0, keepdims=True)
    v0[1:2, :] = jnp.sum(dh, axis=0, keepdims=True)
    v0[5:6, :] = dsum
    v0[10:11, :] = dsum
    v0[11:16, :] = jnp.zeros((5, 512), f32)
    chip.wait()
    vcp = [send(v0, v1, vs.at[0], vr.at[0], other_core())]

    def add(i):
        a, b = i // 4, i % 4
        both = ga[a, b, s, :, 0:80].astype(f32) + rcm[a, b, :, 0:80].astype(f32)
        hi, lo = split(both[:, 48:64] + both[:, 64:80])
        hbuf[a, b, :, 0:48] = both[:, 0:48].astype(bf16)
        hbuf[a, b, :, 48:64] = hi
        hbuf[a, b, :, 64:80] = lo

    loop(0, 16, add)
    sums = Reduce(hbuf, ATT_PARTS, r.att_bufs, r.as_, r.ar)
    sums.begin(0)
    mt = momenta(r)

    def vec_stage(k, buf, axis):
        for cp in vcp:
            cp.wait()
        vcp.clear()
        if k == 0:
            v = v0[...] + v1[...]
        else:
            last = (vy, vz)[k - 1]
            v = (last[0] + last[1]) + (last[2] + last[3])
        place = {"y": y, "z": z, "x": x}[axis]
        buf[place] = v
        for d in (1, 2, 3):
            vcp.append(
                send(buf.at[place], buf.at[place], vs.at[3 * k + d], vr.at[3 * k + d], moved(axis, d))
            )

    sums.end(0)
    sums.begin(1)
    vec_stage(0, vy, "y")
    sums.end(1)
    sums.begin(2)
    vec_stage(1, vz, "z")
    lo = 64
    for v in mlp_sums.end(2):
        gx[lo : lo + v.shape[0], :] = v
        lo += v.shape[0]
    g = sums.end(2)
    gx[0:32, :] = g[0]
    gx[32:48, :] = g[1]
    gx[48:64, :] = g[2]
    grad = gx[...]
    u = (1.0 + MU) * grad + (MU * MU) * mt
    ub = u.astype(bf16)
    hi, lo = split(u[48:64])
    us[0, 0:48] = ub[0:48]
    us[0, 48:64] = jnp.zeros((16, 128), bf16)
    us[1, 0:16] = hi
    us[1, 16:32] = lo
    us[1, 32:64] = jnp.zeros((32, 128), bf16)
    us[2] = ub[64:128]
    us[3] = ub[128:192]
    cps = []
    for d in (1, 2, 3):
        cps.append(send(us.at[(x + d) % 4], ur.at[x], xs.at[d - 1], xr.at[d - 1], moved("x", d)))
    vec_stage(2, vx, "x")
    ur[x] = us[x]
    r.gxa[y, z, s] = grad.astype(bf16)
    for cp in cps:
        cp.wait()
    for k in range(4):
        piece = ur[k]

        @pl.when(x != 3)
        def _(k=k, piece=piece):
            ua[:, y, z, s, :, 128 * k : 128 * k + 128] = piece.reshape(4, 16, 128)

        @pl.when(x == 3)
        def _(k=k, piece=piece):
            for b in range(4):
                ua[k, y, z, s, :, 128 * b : 128 * b + 128] = piece[16 * b : 16 * b + 16]

    gather = Gather(
        [
            (lambda a, b, e: ua.at[pl.ds(0, 2), a, b, e], True),
            (lambda a, b, e: ua.at[pl.ds(2, 2), a, b, e], False),
        ],
        r.sa, r.ra,
    )
    gather.begin()
    for cp in vcp:
        cp.wait()
    r.vec[...] = (vx[0] + vx[1]) + (vx[2] + vx[3])
    gather.turn()
    gather.pass_on()
    gram(r, s, False)
    gather.end()
    gram(r, 1 - s, True)


def dot3(a, b):
    (ah, al), (bh, bl) = a, b
    return dot(ah, bh) + (dot(ah, bl) + dot(al, bh))


def gram(r, e, more):
    x = lax.axis_index("wsh")

    def put(v):
        r.a[...] = r.a[...] + v if more else v

    @pl.when(x == 1)
    def _():
        h, l = r.w3[0, :, :, e].reshape(256, 512), r.w3[1, :, :, e].reshape(256, 512)
        put(dot_tn(h, h) + (dot_tn(h, l) + dot_tn(l, h)))

    @pl.when(x != 1)
    def _():
        u = r.w3[:, :, :, e].reshape(1024, 512)
        put(dot_tn(u, u))


def newton_phase(r):
    y, z, s, x = coords()
    ua, ga, oa, a_ref = r.w3, r.gxa, r.oa, r.a
    ah, al, ph, pl_, th, tl = r.ah, r.al, r.ph, r.pl, r.th, r.tl
    os, rows, xs, xr = r.os, r.rows, r.os_s, r.os_r
    grads = Gather(
        [
            (lambda a, b, e: ga.at[a, b, e, pl.ds(0, 96)], True),
            (lambda a, b, e: ga.at[a, b, e, pl.ds(96, 96)], False),
        ],
        r.sb, r.rb,
    )
    grads.begin()

    def load(hi, lo):
        return hi[...], lo[...]

    def store(hi, lo, v):
        h, l = split(v)
        hi[...] = h
        lo[...] = l

    row = lax.broadcasted_iota(jnp.int32, (512, 512), 0)
    col = lax.broadcasted_iota(jnp.int32, (512, 512), 1)
    eye = row == col
    a = a_ref[...]
    square = jnp.sum(jnp.sum(jnp.where(eye, a, 0.0), axis=0, keepdims=True), axis=1, keepdims=True)
    scale = 1.0 / (jnp.sqrt(square) + 1e-07)
    a_ref[...] = a * (scale * scale)
    mine = ua[:, y, z, s].reshape(64, 512).astype(f32) * scale

    def poly():
        store(ah, al, a_ref[...])
        sq = dot3(load(ah, al), load(ah, al))
        return C2 * a_ref[...] + C3 * sq + jnp.where(eye, C1, 0.0)

    def step(_, mine):
        store(ph, pl_, poly())
        pair = load(ph, pl_)
        store(th, tl, dot3(pair, load(ah, al)))
        a_ref[...] = dot3(pair, load(th, tl))
        return dot3(split(mine), pair)

    mine = lax.fori_loop(0, 2, step, mine)
    grads.turn()
    mine = lax.fori_loop(2, NS_ITERS - 1, step, mine)
    grads.pass_on()
    store(ph, pl_, poly())
    mine = dot3(split(mine), load(ph, pl_))
    side = jnp.where(x == 0, math.sqrt(1536.0), jnp.where(x == 1, math.sqrt(512.0), math.sqrt(2048.0)))
    mine = mine * (0.2 * side)
    mine = jnp.concatenate(
        [jnp.where(x == 1, mine[0:16] + mine[16:32], mine[0:16]), mine[16:64]], axis=0
    ).astype(bf16)
    for k in range(4):
        by_lanes = mine[:, 128 * k : 128 * k + 128]
        by_rows = jnp.concatenate(
            [mine[16 * k : 16 * k + 16, 128 * b : 128 * b + 128] for b in range(4)], axis=0
        )
        os[k] = jnp.where(x == 3, by_rows, by_lanes)
    cps = []
    for d in (1, 2, 3):
        cps.append(send(os.at[(x + d) % 4], rows.at[x], xs.at[d - 1], xr.at[d - 1], moved("x", d)))
    rows[x] = os[x]
    grads.end()
    leave(r, 2).start()
    for cp in cps:
        cp.wait()
    oa[y, z, s, 0:48] = rows[0, 0:48]
    oa[y, z, s, 48:64] = rows[1, 0:16]
    oa[y, z, s, 64:128] = rows[2]
    oa[y, z, s, 128:192] = rows[3]
    update = Gather(
        [
            (lambda a, b, e: oa.at[a, b, e, pl.ds(0, 96)], True),
            (lambda a, b, e: oa.at[a, b, e, pl.ds(96, 96)], False),
        ],
        r.se, r.re,
    )
    update.begin()
    update.turn()
    update.pass_on()
    update.end()
    for k in range(3):
        leave(r, k).wait()


def scratch_list():
    V = pltpu.VMEM
    piece = (HEADS, TOK, 128)
    out = [
        ("fq", V((128, 1536), f32)), ("fo", V((128, 512), f32)),
        ("fi", V((128, 2048), f32)), ("ff", V((512, 512), f32)),
        ("x", V((TOK, D), bf16)), ("dy", V((TOK, D), bf16)),
        ("w1", V((4, 4, 4, 2, 64, 128), bf16)), ("w2", V((4, 4, 4, 2, 64, 128), bf16)),
        ("w3", V((4, 4, 4, 2, 16, 512), bf16)),
        ("kvs", V(piece, bf16)), ("qds", V(piece, bf16)),
        ("kv", V((GROUP, 128), bf16)), ("qd", V((NQB, QB, 128), bf16)),
        ("hid", V((TOK, D), bf16)), ("wide_f", V((TOK, D), f32)),
        ("co", V((TOK, 128), f32)), ("s1", V((TOK, 128), f32)), ("s2", V((TOK, 128), f32)),
        ("res", V((TOK, D), f32)), ("dh", V((TOK, D), f32)),
        ("gm", V((4, 4, 2, 4, 128, 128), bf16)),
        ("rcm", V((4, 4, 4, 128, 128), bf16)), ("hbuf", V((4, 4, 4, 128, 128), bf16)),
        ("kvt", V((128, GROUP), bf16)), ("acc", V((GROUP, 128), f32)),
        ("s_sc", V((GROUP, QB), f32)), ("p_sc", V((GROUP, QB), f32)),
        ("m_sc", V((GROUP // HB, 8, QB), f32)), ("cqs", V((NQB, QB, 128), bf16)),
        ("half", V((16, TOK, 128), bf16)), ("other", V((16, TOK, 128), bf16)),
        ("both", V((16, TOK, 128), bf16)),
        ("spare", V((6, 64, 128), bf16)),
        ("cq", V(piece, bf16)), ("kr", V((HEADS, 2, TOK, 128), bf16)),
        ("dqkv", V((TOK, 1536), bf16)),
        ("mwin", V((128, 512), f32)), ("mtr", V((512, 128), f32)), ("mfin", V((16, 512), f32)),
        ("gx", V((192, 128), f32)),
        ("us", V((4, 64, 128), bf16)), ("ur", V((4, 64, 128), bf16)),
        ("os", V((4, 64, 128), bf16)), ("rows", V((4, 64, 128), bf16)),
        ("v0", V((16, 512), f32)), ("v1", V((16, 512), f32)),
        ("vy", V((4, 16, 512), f32)), ("vz", V((4, 16, 512), f32)), ("vx", V((4, 16, 512), f32)),
        ("a", V((512, 512), f32)),
        ("out", V((TOK, D), bf16)), ("gt", V((TOK, D), f32)),
        ("gxa", V((4, 4, 2, 192, 128), bf16)),
    ]
    out += [(k, V((512, 512), bf16)) for k in ("ah", "al", "ph", "pl", "th", "tl")]
    for name, shape in (
        ("lsem", (6,)), ("osem", (3,)), ("msem", (4,)), ("xs", (5, 3)), ("xr", (5, 3)), ("ys", (3, 3)), ("yr", (3, 3)),
        ("sa", (2, 3)), ("ra", (2, 5)), ("sb", (2, 3)), ("rb", (2, 5)),
        ("se", (2, 3)), ("re", (2, 5)),
        ("own_sem", None), ("ks", None), ("kvr", None), ("qs", None), ("qr", None),
        ("cs", None), ("cr", None),
        ("m_s", (2,)), ("m_r", (2,)), ("ms", (3, 3)), ("mr", (3, 3)), ("as_", (3, 3)), ("ar", (3, 3)),
        ("ws", (6,)), ("wr", (6,)), ("bs", None), ("br", None), ("rqs", None), ("rqr", None),
        ("vs", (10,)), ("vr", (10,)), ("us_s", (3,)), ("us_r", (3,)), ("os_s", (3,)), ("os_r", (3,)),
    ):
        out.append((name, DMA if shape is None else DMA(shape)))
    out += [(f"mlp{i}", v) for i, v in enumerate(Reduce.scratch(MLP_PARTS))]
    out += [(f"att{i}", v) for i, v in enumerate(Reduce.scratch(ATT_PARTS))]
    return out


INPUTS = (
    "starts", "x_in", "dy_in", "gain", "shift", "bias", "wq", "wo", "wi", "wf", "mq", "mo", "mi", "mf",
)
OUTPUTS = ("out_to", "gt_to", "gxa_to", "oa", "vec")


def step_kernel(names, *refs):
    r = types.SimpleNamespace(**dict(zip(names, refs)))
    r.mlp_bufs = [getattr(r, f"mlp{i}") for i in range(5 * len(MLP_PARTS))]
    r.att_bufs = [getattr(r, f"att{i}") for i in range(5 * len(ATT_PARTS))]
    chip = front_phase(r)
    back_phase(r, attention_phase(r, chip))
    wait_for(r.both.at[pl.ds(0, 15)], r.bs)
    wait_for(r.cq, r.rqs)
    newton_phase(r)


def train_step(*args):
    scratch = scratch_list()
    names = INPUTS + OUTPUTS + tuple(k for k, _ in scratch)
    return pl.pallas_call(
        functools.partial(step_kernel, names),
        out_shape=tuple(
            jax.ShapeDtypeStruct(shape, t)
            for shape, t in (
                ((TOK, D), bf16), ((TOK, D), f32),
                ((4, 4, 2, 192, 128), bf16), ((4, 4, 2, 192, 128), bf16), ((16, 512), f32),
            )
        ),
        in_specs=[SM, ANY, ANY, VM, VM, VM] + [ANY] * 8,
        out_specs=(ANY, ANY, ANY, VM, VM),
        scratch_shapes=[v for _, v in scratch],
        compiler_params=pltpu.CompilerParams(
            vmem_limit_bytes=63 * 2**20, collective_id=1, has_side_effects=True
        ),
        name="train_step",
    )(*args)


def update_kernel(
    gx, oa, out, gt, wq, wo, wi, wf, mq, mo, mi, mf, vec, vm, gain, shift, bias,
    out_to, gt_to, nmq, nwq, nmo, nwo, nmi, nwi, nmf, nwf, nvm, nvec,
):
    out_to[...] = out[...]
    gt_to[...] = gt[...]

    @pl.when(pl.program_id(0) == 0)
    def _():
        for k in range(11):
            part = slice(512 * k, 512 * k + 512)
            v = VMU * vm[part] + vec[k]
            old = (gain[...], shift[...])[k] if k < 2 else bias[512 * k - 1024 : 512 * k - 512]
            nvm[part] = v
            nvec[part] = old - VLR * v

    for lo, n, w, m, nm, nw in (
        (0, 48, wq, mq, nmq, nwq),
        (48, 16, wo, mo, nmo, nwo),
        (64, 64, wi, mi, nmi, nwi),
    ):
        grad = gx[:, lo : lo + n, :].astype(f32).reshape(8 * n, 128).T
        turned = oa[:, lo : lo + n, :].astype(f32).reshape(8 * n, 128).T
        nm[...] = MU * m[...] + grad
        nw[...] = (1.0 - LR * WD) * w[...] - LR * turned
    for b in range(4):
        cols = slice(128 * b, 128 * b + 128)
        rows = slice(128 + 16 * b, 144 + 16 * b)
        grad = gx[:, rows, :].astype(f32).reshape(128, 128)
        turned = oa[:, rows, :].astype(f32).reshape(128, 128)
        nmf[:, cols] = MU * mf[:, cols] + grad
        nwf[:, cols] = (1.0 - LR * WD) * wf[:, cols] - LR * turned


def update(gx, oa, out, gt, weights, moments, vec, vec_mom, gain, shift, biases):
    def whole(v):
        return pl.BlockSpec(v.shape, lambda i, n=v.ndim: (0,) * n)

    piece = pl.BlockSpec((8, 192, 128), lambda i: (i, 0, 0))
    rows = pl.BlockSpec((48, D), lambda i: (i, 0))
    blocks = [
        pl.BlockSpec((128, 384), lambda i: (0, i)),
        pl.BlockSpec((128, 128), lambda i: (0, i)),
        pl.BlockSpec((128, 512), lambda i: (0, i)),
        pl.BlockSpec((128, 512), lambda i: (i, 0)),
    ]
    shape = lambda v: jax.ShapeDtypeStruct(v.shape, v.dtype)
    outs, specs = [shape(out), shape(gt)], [rows, rows]
    for w, b in zip(weights, blocks):
        outs += [shape(w)] * 2
        specs += [b, b]
    outs += [shape(vec_mom)] * 2
    specs += [whole(vec_mom)] * 2
    vectors = (vec, vec_mom, gain, shift, biases)
    return pl.pallas_call(
        update_kernel,
        grid=(4,),
        out_shape=tuple(outs),
        in_specs=[piece, piece, rows, rows] + blocks + blocks + [whole(v) for v in vectors],
        out_specs=tuple(specs),
        compiler_params=pltpu.CompilerParams(vmem_limit_bytes=60 * 2**20),
        name="update_weights",
    )(gx, oa, out, gt, *weights, *moments, *vectors)


def body(
    tokens, cotangent, ln_gain, ln_bias, biases, w_qkv, w_out, w_in, w_fin,
    mom_qkv, mom_out, mom_in, mom_fin, vec_mom, starts,
):
    weights = (w_qkv, w_out, w_in, w_fin)
    moments = (mom_qkv, mom_out, mom_in, mom_fin)
    block_out, grad_tokens, gx, oa, vec_sum = train_step(
        starts, tokens, cotangent, ln_gain[None, :], ln_bias[None, :], biases, *weights, *moments
    )
    return update(
        gx.reshape(32, 192, 128), oa.reshape(32, 192, 128), block_out, grad_tokens,
        weights, moments, vec_sum, vec_mom, ln_gain, ln_bias, biases,
    )


def solution(mesh):
    tok = P(("wsh", "ctx"), None)
    row = P("wsh", None)
    return jax.shard_map(
        body,
        mesh=mesh,
        in_specs=(tok, tok, P(), P(), P()) + (row,) * 8 + (P(), P()),
        out_specs=(tok, tok) + (row,) * 8 + (P(), P()),
        check_vma=False,
    )
```
